32 devices in a mesh: seq: 8 (over y, x, core), rep: 4 (over z).
Axes of the slice: x: 2, y: 2, z: 4, core: 2. Of those that a mesh axis runs over, the one named last changes fastest.
Arguments:
- tokens: bfloat16 [4, 8192, 768], P('rep', 'seq'), may hold values from -6 to 6
- lengths: int32 [4], P('rep'), may hold values from 7680 to 8192, as said below
- tile_valid: int32 [4, 8192], P('rep', 'seq'), may hold values from 0 to 1, as said below
- w_query: bfloat16 [768, 768], replicated, may hold values from -0.21875 to 0.21875
- w_key: bfloat16 [768, 768], replicated, may hold values from -0.21875 to 0.21875
- w_value: bfloat16 [768, 768], replicated, may hold values from -0.21875 to 0.21875
- w_out: bfloat16 [768, 768], replicated, may hold values from -4 to 4
- b_query: float32 [768], replicated, may hold values from -3 to 3
- b_value: float32 [768], replicated, may hold values from -3 to 3
- b_out: float32 [768], replicated, may hold values from -2 to 2
- gain_attn: float32 [768], replicated, may hold values from 0.1 to 1.9
- shift_attn: float32 [768], replicated, may hold values from -2 to 2
- gain_mlp: float32 [768], replicated, may hold values from 0.1 to 1.9
- shift_mlp: float32 [768], replicated, may hold values from -2 to 2
- w_up: bfloat16 [768, 3072], replicated, may hold values from -0.21875 to 0.21875
- b_up: float32 [3072], replicated, may hold values from -3 to 3
- w_down: bfloat16 [3072, 768], replicated, may hold values from -0.109375 to 0.109375
- b_down: float32 [768], replicated, may hold values from -2 to 2
- cotangent: bfloat16 [4, 8192, 768], P('rep', 'seq'), may hold values from -6 to 6
Outputs:
- mixed: bfloat16 [4, 8192, 768], P('rep', 'seq')
- grad_tokens: bfloat16 [4, 8192, 768], P('rep', 'seq')
- grad_w_query: float32 [768, 768], P('seq')
- grad_w_key: float32 [768, 768], P('seq')
- grad_w_value: float32 [768, 768], P('seq')
- grad_w_out: float32 [768, 768], P('seq')
- grad_b_query: float32 [768], P('seq')
- grad_b_value: float32 [768], P('seq')
- grad_b_out: float32 [768], P('seq')
- grad_gain_attn: float32 [768], P('seq')
- grad_shift_attn: float32 [768], P('seq')
- grad_gain_mlp: float32 [768], P('seq')
- grad_shift_mlp: float32 [768], P('seq')
- grad_w_up: float32 [768, 3072], P('seq')
- grad_b_up: float32 [3072], P('seq')
- grad_w_down: float32 [3072, 768], P('seq')
- grad_b_down: float32 [768], P('seq')
The draws below stay inside these ranges and needn't reach their ends.
Inputs may be any that keep to these rules, and one draw needn't show every extreme that they name: `lengths`: each set keeps at least its first 7680 tiles, and some set has all 8192. `tile_valid`: the first tile of each aligned block of 1024 tiles is valid.
All inputs are finite; a program needn't handle non-finite values.
Results may differ from the reference program's by a relative error of at most 0.04.
Values may be sent and summed in bfloat16 or wider, within the bound.
No kernel may reach another device: no remote copies, remote signals or barrier semaphores. Data moves between devices by JAX's collectives and lax.ppermute only.
A program may use at most 320 MiB of HBM per device.

```python
import jax
import jax.numpy as jnp
from jax import lax

D = 768
H = 16
HD = 48
FF = 3072
TOK_DEV = 1024
R = 16
LENGTH = 8192
SETS = 4


def draw_lengths(key, part):
    key = jax.random.fold_in(key, 11)
    first_key, second_key = jax.random.split(key)
    shortfall = jax.random.randint(first_key, (SETS,), 0, TOK_DEV // 2 + 1)
    chosen_set = jax.random.randint(second_key, (), 0, SETS)
    shortfall = jnp.where(jnp.arange(SETS) == chosen_set, 0, shortfall)
    return (LENGTH - shortfall).astype(jnp.int32)


def draw_tile_valid(key, part):
    key = jax.random.fold_in(key, 23)
    dice = jax.random.randint(key, (SETS, LENGTH), 0, 10)
    block_heads = (jnp.arange(LENGTH) % TOK_DEV == 0)[None, :]
    return jnp.where((dice < 7) | block_heads, 1, 0).astype(jnp.int32)


def block_levels(stream_key, extent, cuts, least, high):
    level = 1.0
    for axis_at, parts in cuts:
        heights = jax.random.uniform(jax.random.fold_in(jax.random.fold_in(stream_key, 6), axis_at), (parts,), jnp.float32, least / len(cuts), high / len(cuts))
        level = level * jnp.repeat(jnp.exp(heights), extent[axis_at] // parts).reshape((-1,) + (1,) * (len(extent) - 1 - axis_at))
    return level


def noise(stream_key, shape, deviation, reach, cuts=(), kind=jnp.bfloat16):
    loudness = block_levels(stream_key, shape, cuts, -0.22, 0.18) if cuts else 1.0
    result = jax.random.normal(stream_key, shape, jnp.float32) * deviation * loudness
    return jnp.minimum(jnp.maximum(result, -reach), reach).astype(kind)


def setup_inputs(seed: int = 0) -> dict:
    splits = jax.random.split(jax.random.key(seed), 20)
    return {
        "tokens": noise(splits[0], (SETS, LENGTH, D), 1.0, 6.0, ((0, 4), (1, 8))),
        "lengths": draw_lengths(jax.random.fold_in(splits[19], 71), 0),
        "tile_valid": draw_tile_valid(jax.random.fold_in(splits[19], 71), 0),
        "w_query": noise(splits[3], (D, D), D ** -0.5, 0.21875),
        "w_key": noise(splits[4], (D, D), D ** -0.5, 0.21875),
        "w_value": noise(splits[5], (D, D), D ** -0.5, 0.21875),
        "w_out": noise(splits[6], (D, D), 2 ** -0.5, 4.0),
        "b_query": noise(splits[7], (D,), 0.5, 3.0, (), jnp.float32),
        "b_value": noise(splits[8], (D,), 0.5, 3.0, (), jnp.float32),
        "b_out": noise(splits[9], (D,), 0.3, 2.0, (), jnp.float32),
        "gain_attn": jnp.clip(1.0 + 0.18 * jax.random.normal(splits[10], (D,), jnp.float32), 0.1, 1.9),
        "shift_attn": noise(splits[11], (D,), 0.3, 2.0, (), jnp.float32),
        "gain_mlp": jnp.clip(1.0 + 0.18 * jax.random.normal(splits[12], (D,), jnp.float32), 0.1, 1.9),
        "shift_mlp": noise(splits[13], (D,), 0.3, 2.0, (), jnp.float32),
        "w_up": noise(splits[14], (D, FF), D ** -0.5, 0.21875),
        "b_up": noise(splits[15], (FF,), 0.5, 3.0, (), jnp.float32),
        "w_down": noise(splits[16], (FF, D), FF ** -0.5, 0.109375),
        "b_down": noise(splits[17], (D,), 0.3, 2.0, (), jnp.float32),
        "cotangent": noise(splits[18], (SETS, LENGTH, D), 1.0, 6.0, ((0, 4), (1, 8))),
    }


@jax.custom_vjp
def low(v):
    return lax.optimization_barrier(v.astype(jnp.bfloat16)).astype(jnp.float32)

@jax.custom_vjp
def low_back(v):
    return v

def low_keep(v):
    return (low(v), None)

def low_pass(kept, grad):
    return (grad,)

def back_keep(v):
    return (v, None)

def back_low(kept, grad):
    return (low(grad),)
low.defvjp(low_keep, low_pass)
low_back.defvjp(back_keep, back_low)

def layer_norm(values, gain, shift):
    center = values - lax.optimization_barrier(jnp.mean(values, axis=-1, keepdims=True))
    spread = lax.optimization_barrier(jnp.mean(center * center, axis=-1, keepdims=True))
    return center * lax.rsqrt(spread + 1e-05) * gain + shift

def product(left, right):
    return jnp.dot(left, right, precision=lax.Precision.HIGHEST, preferred_element_type=jnp.float32)

def one_set(inputs, valid, weights):
    w_query, w_key, w_value, w_out, b_query, b_value, b_out, gain_attn, shift_attn, gain_mlp, shift_mlp, w_up, b_up, w_down, b_down = weights
    normed = low(layer_norm(inputs, gain_attn, shift_attn))
    queries = low_back(low(product(normed, w_query) + b_query)).reshape(LENGTH, H, HD)
    keys_all = low_back(low(product(normed, w_key))).reshape(LENGTH, H, HD)
    values_all = low_back(low(product(normed, w_value) + b_value)).reshape(LENGTH, H, HD)
    offsets = jnp.arange(H, dtype=jnp.int32) % R
    head_ids = jnp.arange(H, dtype=jnp.int32)
    far_keys = keys_all.reshape(LENGTH // R, R, H, HD)[:, offsets, head_ids, :]
    far_values = values_all.reshape(LENGTH // R, R, H, HD)[:, offsets, head_ids, :]
    far_valid = valid.reshape(LENGTH // R, R)[:, offsets]
    block_rows = min(512, TOK_DEV)
    score_scale = HD ** (-0.5)
    highest = lax.Precision.HIGHEST

    def attend(block_index):
        first = block_index.astype(jnp.int32) * block_rows
        segment = first // TOK_DEV * TOK_DEV
        query_block = lax.dynamic_slice_in_dim(queries, first, block_rows, 0)
        near_keys = lax.dynamic_slice_in_dim(keys_all, segment, TOK_DEV, 0)
        near_values = lax.dynamic_slice_in_dim(values_all, segment, TOK_DEV, 0)
        near_valid = lax.dynamic_slice_in_dim(valid, segment, TOK_DEV, 0)
        places = first + jnp.arange(block_rows, dtype=jnp.int32)
        chosen = places[:, None] % R == offsets[None, :]
        near_scores = low_back(jnp.einsum('qhd,khd->hqk', query_block, near_keys, precision=highest) * score_scale)
        far_scores = low_back(jnp.einsum('qhd,khd->hqk', query_block, far_keys, precision=highest) * score_scale)
        near_ok = (near_valid > 0.5)[None, None, :]
        far_ok = (far_valid.T[:, None, :] > 0.5) & chosen.T[:, :, None]
        peak = jnp.maximum(lax.optimization_barrier(jnp.max(jnp.where(near_ok, near_scores, -1e+30), axis=2)), lax.optimization_barrier(jnp.max(jnp.where(far_ok, far_scores, -1e+30), axis=2)))
        near_exp = jnp.where(near_ok, jnp.exp(jnp.where(near_ok, near_scores - peak[:, :, None], 0.0)), 0.0)
        far_exp = jnp.where(far_ok, jnp.exp(jnp.where(far_ok, far_scores - peak[:, :, None], 0.0)), 0.0)
        denom = lax.optimization_barrier(jnp.sum(near_exp, axis=2)) + lax.optimization_barrier(jnp.sum(far_exp, axis=2))
        numer = low_back(jnp.einsum('hqk,khd->qhd', low(near_exp), near_values, precision=highest) + jnp.einsum('hqk,khd->qhd', low(far_exp), far_values, precision=highest))
        return numer / denom.T[:, :, None]
    pieces = lax.map(jax.checkpoint(attend), jnp.arange(LENGTH // block_rows, dtype=jnp.int32))
    attended = pieces.reshape(LENGTH, D)
    branch = low_back(product(low_back(low(attended)), w_out) + b_out)
    hidden = inputs + branch
    normed_two = low(layer_norm(hidden, gain_mlp, shift_mlp))
    upper = low_back(product(normed_two, w_up) + b_up)
    act = low(jax.nn.gelu(upper, approximate=False))
    return hidden + product(act, w_down) + b_down

def reference(tokens, lengths, tile_valid, w_query, w_key, w_value, w_out, b_query, b_value, b_out, gain_attn, shift_attn, gain_mlp, shift_mlp, w_up, b_up, w_down, b_down, cotangent):
    places = jnp.arange(LENGTH, dtype=jnp.int32)
    valid = jnp.where((tile_valid > 0) & (places[None, :] < lengths[:, None]), 1.0, 0.0).astype(jnp.float32)
    weights = tuple((w.astype(jnp.float32) for w in (w_query, w_key, w_value, w_out, b_query, b_value, b_out, gain_attn, shift_attn, gain_mlp, shift_mlp, w_up, b_up, w_down, b_down)))

    def forward(inputs, *params):
        return lax.map(lambda pair: one_set(pair[0], pair[1], params), (inputs, valid))
    outputs, pullback = jax.vjp(forward, tokens.astype(jnp.float32), *weights)
    grads = pullback(cotangent.astype(jnp.float32))
    grad_tokens, grad_w_query, grad_w_key, grad_w_value, grad_w_out, grad_b_query, grad_b_value, grad_b_out, grad_gain_attn, grad_shift_attn, grad_gain_mlp, grad_shift_mlp, grad_w_up, grad_b_up, grad_w_down, grad_b_down = grads
    return (outputs.astype(jnp.bfloat16), grad_tokens.astype(jnp.bfloat16), grad_w_query, grad_w_key, grad_w_value, grad_w_out, grad_b_query, grad_b_value, grad_b_out, grad_gain_attn, grad_shift_attn, grad_gain_mlp, grad_shift_mlp, grad_w_up, grad_b_up, grad_w_down, grad_b_down)
```

```python
import functools

import jax
import jax.numpy as jnp
from jax import lax
from jax.experimental import pallas as pl
from jax.experimental.pallas import tpu as pltpu
from jax.sharding import PartitionSpec as P

H = 16
R = 16
EPS = 1e-05
LOG2E = 1.4426950408889634
NEG = -1e30
BF = jnp.bfloat16
F32 = jnp.float32
VMEM_LIMIT = 60 * 1024 * 1024


def iota(shape, dim):
    return lax.broadcasted_iota(jnp.int32, shape, dim)


def dot(left, right):
    return jnp.dot(left, right, preferred_element_type=F32)


def dot_nt(left, right):
    return lax.dot_general(left, right, (((1,), (1,)), ((), ())), preferred_element_type=F32)


def params():
    return pltpu.CompilerParams(vmem_limit_bytes=VMEM_LIMIT)


def cost(micros):
    return pl.CostEstimate(flops=int(micros * 1.15e9), bytes_accessed=1024, transcendentals=0)


def whole():
    return pl.BlockSpec(memory_space=pltpu.VMEM)


def idle(arrays):
    return [pl.BlockSpec(memory_space=pl.ANY)] * len(arrays)


def scalars():
    return pl.BlockSpec(memory_space=pltpu.SMEM)


def shape(dims, kind):
    return jax.ShapeDtypeStruct(dims, kind)


def normalized(values):
    center = values - jnp.mean(values, axis=-1, keepdims=True)
    rstd = lax.rsqrt(jnp.mean(center * center, axis=-1, keepdims=True) + EPS)
    return center * rstd, rstd


def norm_backward(grad, unit, rstd):
    return rstd * (
        grad
        - jnp.mean(grad, axis=-1, keepdims=True)
        - unit * jnp.mean(grad * unit, axis=-1, keepdims=True)
    )


def own_head(rows, first_row, columns, size):
    feature = iota((rows, columns), 0) + first_row
    start = (iota((rows, columns), 1) % R) * size
    return (feature >= start) & (feature < start + size)


def group_pick(groups, columns):
    return (iota((groups, columns), 1) // R == iota((groups, columns), 0)).astype(BF)


def project_body(
    info, x, gain, shift, wq, wk, wv, bq, bv, valid, q_out, k_out, v_out, n_out, far_out, *, size
):
    rows, width = x.shape
    unit, _ = normalized(x[...].astype(F32))
    normed = (unit * gain[...] + shift[...]).astype(BF)
    n_out[...] = normed.T
    q_out[...] = (dot(normed, wq[...]) + bq[...]).astype(BF).T
    keys = dot(normed, wk[...]).astype(BF)
    values = (dot(normed, wv[...]) + bv[...]).astype(BF)
    k_out[...] = keys.T
    v_out[...] = values.T
    feature = iota((rows, width), 1)
    start = (iota((rows, width), 0) % R) * size
    mine = (feature >= start) & (feature < start + size)
    pick = group_pick(rows // R, rows)
    zero = jnp.zeros((rows, width), BF)
    far_out[:, :width] = dot(pick, jnp.where(mine, keys, zero)).astype(BF)
    far_out[:, width : 2 * width] = dot(pick, jnp.where(mine, values, zero)).astype(BF)
    place = iota((1, rows), 1) + pl.program_id(0) * rows
    good = jnp.where((valid[...] > 0) & (place < info[0]), 1.0, 0.0)
    residue = (iota((rows, 128), 0) % R == iota((rows, 128), 1)).astype(BF)
    found = dot((pick.astype(F32) * good).astype(BF), residue)
    far_out[:, 2 * width :] = jnp.where(found > 0.5, 0.0, NEG).astype(BF)


def project(info, x, gain, shift, wq, wk, wv, bq, bv, valid, size):
    tokens, width = x.shape
    rows = 256
    column = pl.BlockSpec((width, rows), lambda i: (0, i))
    return pl.pallas_call(
        functools.partial(project_body, size=size),
        grid=(tokens // rows,),
        in_specs=[scalars(), pl.BlockSpec((rows, width), lambda i: (i, 0))]
        + [whole()] * 7
        + [pl.BlockSpec((1, rows), lambda i: (0, i))],
        out_specs=[column] * 4 + [pl.BlockSpec((rows // R, 2 * width + 128), lambda i: (i, 0))],
        out_shape=[shape((width, tokens), BF)] * 4 + [shape((tokens // R, 2 * width + 128), BF)],
        compiler_params=params(),
        cost_estimate=cost(10),
        name="project",
    )(info, x, gain, shift, wq, wk, wv, bq, bv, valid)


def near_body(info, q, k, v, valid, e_out, numer_out, peak_out, *, scale):
    tokens = q.shape[1]
    scaled = q[...].astype(F32) * scale
    high = scaled.astype(BF)
    low = (scaled - high.astype(F32)).astype(BF)
    first = iota((32, tokens), 0) == 0
    queries = jnp.concatenate([high, low, first.astype(BF)], axis=0)
    good = (valid[...] > 0) & (iota((1, tokens), 1) < info[0])
    mask = jnp.where(first, jnp.where(good, 0.0, NEG), 0.0).astype(BF)
    keys = jnp.concatenate([k[...], k[...], mask], axis=0).T
    values = jnp.concatenate([v[...], (iota((16, tokens), 0) == 0).astype(BF)], axis=0)
    scores = dot(keys, queries)
    peak = jnp.max(scores, axis=0, keepdims=True)
    weights = jnp.exp2(scores - peak).astype(BF)
    e_out[0] = weights
    numer_out[0] = dot(values, weights)
    peak_out[0] = peak


def near(info, q, k, v, valid, scale):
    width, tokens = q.shape
    size = width // H
    head = pl.BlockSpec((size, tokens), lambda h: (h, 0))

    def block(rows):
        return pl.BlockSpec((1, rows, tokens), lambda h: (h, 0, 0))

    return pl.pallas_call(
        functools.partial(near_body, scale=scale),
        grid=(H,),
        in_specs=[scalars()] + [head] * 3 + [pl.BlockSpec((1, tokens), lambda h: (0, 0))],
        out_specs=[block(tokens), block(size + 16), block(1)],
        out_shape=[
            shape((H, tokens, tokens), BF),
            shape((H, size + 16, tokens), F32),
            shape((H, 1, tokens), F32),
        ],
        compiler_params=params(),
        cost_estimate=cost(31),
        name="near",
    )(info, q, k, v, valid)


def merge_body(*refs, scale, pieces, size):
    (q, numer, peak, x, w_out, b_out, gain, shift) = refs[:8]
    parts = refs[8 : 8 + pieces]
    (att_out, near_out, far_out, hidden_out, n_out, nt_out, e_out) = refs[8 + pieces : 15 + pieces]
    keys, values, masks, att = refs[15 + pieces :]
    width, rows = q.shape
    chunk = parts[0].shape[0]

    @pl.when(pl.program_id(0) == 0)
    def _():
        for i, part in enumerate(parts):
            keys[i * chunk : (i + 1) * chunk, :] = part[:, :width]
            values[:, i * chunk : (i + 1) * chunk] = part[:, width : 2 * width].T
            masks[i * chunk : (i + 1) * chunk, :] = part[:, 2 * width :]

    mine = own_head(width, 0, rows, size)
    queries = jnp.where(mine, q[...], jnp.zeros((width, rows), BF))
    residue = (iota((128, rows), 1) % R == iota((128, rows), 0)).astype(BF)
    scores = dot(keys[...], queries) * scale + dot(masks[...], residue)
    far_peak = jnp.max(scores, axis=0, keepdims=True)
    weights = jnp.exp2(scores - far_peak)
    far_denom = jnp.sum(weights, axis=0, keepdims=True)
    weights = weights.astype(BF)
    e_out[...] = weights
    far_numer = dot(values[...], weights)
    place = iota((1, rows), 1) % R
    far_row = jnp.zeros((1, rows), F32)
    for h in range(H):
        lane = slice(h * size, (h + 1) * size)
        here = place == h
        near_peak = peak[h]
        top = jnp.maximum(near_peak, jnp.where(here, far_peak, NEG))
        near_fade = jnp.exp2(near_peak - top)
        far_fade = jnp.where(here, jnp.exp2(far_peak - top), 0.0)
        inverse = 1.0 / (near_fade * numer[h, size : size + 1, :] + far_fade * far_denom)
        near_fade = near_fade * inverse
        far_fade = far_fade * inverse
        near_out[h] = near_fade
        far_row = far_row + far_fade
        att[lane, :] = numer[h, :size, :] * near_fade + far_numer[lane, :] * far_fade
    far_out[...] = far_row
    attended = att[...]
    att_out[...] = attended
    hidden = x[...].astype(F32) + dot(attended.astype(BF).T, w_out[...]) + b_out[...]
    hidden_out[...] = hidden
    unit, _ = normalized(hidden)
    normed = (unit * gain[...] + shift[...]).astype(BF)
    n_out[...] = normed
    nt_out[...] = normed.T


def merge(q, numer, peak, x, w_out, b_out, gain, shift, parts, scale):
    width, tokens = q.shape
    size = width // H
    rows = 256
    far = sum(part.shape[0] for part in parts)
    column = pl.BlockSpec((width, rows), lambda i: (0, i))
    block = pl.BlockSpec((rows, width), lambda i: (i, 0))

    def heads(depth):
        return pl.BlockSpec((H, depth, rows), lambda i: (0, 0, i))

    return pl.pallas_call(
        functools.partial(merge_body, scale=scale, pieces=len(parts), size=size),
        grid=(tokens // rows,),
        in_specs=[column, heads(size + 16), heads(1), block]
        + [whole()] * 4
        + [whole()] * len(parts),
        out_specs=[
            column,
            heads(1),
            pl.BlockSpec((1, rows), lambda i: (0, i)),
            block,
            block,
            column,
            pl.BlockSpec((far, rows), lambda i: (0, i)),
        ],
        out_shape=[
            shape((width, tokens), F32),
            shape((H, 1, tokens), F32),
            shape((1, tokens), F32),
            shape((tokens, width), F32),
            shape((tokens, width), BF),
            shape((width, tokens), BF),
            shape((far, tokens), BF),
        ],
        scratch_shapes=[
            pltpu.VMEM((far, width), BF),
            pltpu.VMEM((width, far), BF),
            pltpu.VMEM((far, 128), BF),
            pltpu.VMEM((width, rows), F32),
        ],
        compiler_params=params(),
        cost_estimate=cost(13),
        name="merge",
    )(q, numer, peak, x, w_out, b_out, gain, shift, *parts)


def gelu_pair(u):
    size = jnp.abs(u)
    t = 1.0 / (1.0 + (0.3275911 * 0.7071067811865476) * size)
    bell = jnp.exp2(u * u * (-0.5 * LOG2E))
    poly = t * (
        0.5 * 0.254829592
        + t
        * (
            0.5 * -0.284496736
            + t * (0.5 * 1.421413741 + t * (0.5 * -1.453152027 + t * (0.5 * 1.061405429)))
        )
    )
    tail = poly * bell
    phi = jnp.where(u > 0, 1.0 - tail, tail)
    return u * phi, phi + u * bell * 0.3989422804014327


def feed_body(
    info, n, nt, g, w_up, w_down, b_up, hidden, b_down,
    mixed_out, dn_out, up_keep, up_send, down_keep, down_send, bias_out,
    gt, act, dup, mix, grad, *, blocks,
):
    step = pl.program_id(0)
    tokens, width = n.shape
    wide = w_up.shape[1]
    half = wide // 2
    me = info[1]

    @pl.when(step == 0)
    def _():
        gt[...] = g[...].T
        mix[...] = jnp.zeros_like(mix)
        dn_out[...] = jnp.zeros_like(dn_out)

    bias = b_up[...]
    bias_sum = jnp.zeros((1, wide), F32)
    rows = 256
    for i in range(tokens // rows):
        at = slice(i * rows, (i + 1) * rows)
        upper = dot(n[at, :], w_up[...]) + bias
        value, slope = gelu_pair(upper)
        value = value.astype(BF)
        act[at, :] = value
        mix[at, :] += dot(value, w_down[...])
        d_upper = (dot_nt(g[at, :], w_down[...]) * slope).astype(BF)
        dup[at, :] = d_upper
        bias_sum = bias_sum + jnp.sum(d_upper.astype(F32), axis=0, keepdims=True)
        dn_out[at, :] += dot_nt(d_upper, w_up[...])
    bias_out[...] = bias_sum
    grad[...] = dot(nt[...], dup[...])
    share = width // blocks
    for j in range(blocks // 2):
        for out, core in ((up_keep, 0), (up_send, 1)):
            start = pl.multiple_of(((2 * j + core) ^ me) * share, share)
            out[j] = grad[pl.ds(start, share), :].astype(BF)
    grad[...] = dot(gt[...], act[...])
    for out, core in ((down_keep, 0), (down_send, 1)):

        @pl.when((me & 1) == core)
        def _():
            out[0] = grad[:, :half].astype(BF)

        @pl.when((me & 1) != core)
        def _():
            out[0] = grad[:, half:].astype(BF)

    @pl.when(step == pl.num_programs(0) - 1)
    def _():
        mixed_out[...] = (hidden[...] + mix[...] + b_down[...]).astype(BF)


def feed(info, n, nt, g, w_up, w_down, b_up, hidden, b_down):
    tokens, width = n.shape
    hidden_units = w_up.shape[1]
    blocks = 8
    steps = 4
    wide = hidden_units // steps
    rows = pl.BlockSpec((blocks // 2, width // blocks, wide), lambda c, info: (0, 0, c))
    pair = pl.BlockSpec((1, width, wide // 2), lambda c, info: (c ^ (info[1] >> 1), 0, 0))
    full = pl.BlockSpec(memory_space=pltpu.VMEM)
    return pl.pallas_call(
        functools.partial(feed_body, blocks=blocks),
        grid_spec=pltpu.PrefetchScalarGridSpec(
            num_scalar_prefetch=1,
            grid=(steps,),
            in_specs=[
                full,
                full,
                full,
                pl.BlockSpec((width, wide), lambda c, info: (0, c)),
                pl.BlockSpec((wide, width), lambda c, info: (c, 0)),
                pl.BlockSpec((1, wide), lambda c, info: (0, c)),
                full,
                full,
            ],
            out_specs=[full, full, rows, rows, pair, pair]
            + [pl.BlockSpec((1, wide), lambda c, info: (0, c))],
            scratch_shapes=[
                pltpu.VMEM((width, tokens), BF),
                pltpu.VMEM((tokens, wide), BF),
                pltpu.VMEM((tokens, wide), BF),
                pltpu.VMEM((tokens, width), F32),
                pltpu.VMEM((width, wide), F32),
            ],
        ),
        out_shape=[
            shape((tokens, width), BF),
            shape((tokens, width), F32),
            shape((blocks // 2, width // blocks, hidden_units), BF),
            shape((blocks // 2, width // blocks, hidden_units), BF),
            shape((blocks // 2, width, hidden_units // blocks), BF),
            shape((blocks // 2, width, hidden_units // blocks), BF),
            shape((1, hidden_units), F32),
        ],
        compiler_params=params(),
        cost_estimate=cost(46),
        name="feed",
    )(info, n, nt, g, w_up, w_down, b_up, hidden, b_down)


def split_body(*refs, pieces, size, score_scale, blocks):
    (info, hidden, dn, g, gain, att, near_fade, far_fade, w_out, q, e_far) = refs[:11]
    parts = refs[11 : 11 + pieces]
    outs = refs[11 + pieces :]
    (dh_out, dnum_out, delta_out, dq_out, keep, send, vec_out) = outs[:7]
    if pieces:
        far_grads = outs[7 : 7 + pieces]
        (near_num, far_num, out_acc, keys, values, key_acc, value_acc) = outs[7 + pieces :]
        chunk = parts[0].shape[0]
    else:
        (far_num, far_delta_out, near_num, out_acc) = outs[7:]
    step = pl.program_id(0)
    width, rows = q.shape
    me = info[1]

    @pl.when(step == 0)
    def _():
        for i, part in enumerate(parts):
            keys[:, i * chunk : (i + 1) * chunk] = part[:, :width].T
            values[i * chunk : (i + 1) * chunk, :] = part[:, width : 2 * width]
        if pieces:
            key_acc[...] = jnp.zeros_like(key_acc)
            value_acc[...] = jnp.zeros_like(value_acc)
        out_acc[...] = jnp.zeros_like(out_acc)
        vec_out[...] = jnp.zeros_like(vec_out)

    unit, rstd = normalized(hidden[...])
    d_normed = dn[...]
    upstream = g[...].astype(F32)
    d_hidden = upstream + norm_backward(d_normed * gain[...], unit, rstd)
    dh_out[...] = d_hidden
    d_branch = d_hidden.astype(BF)
    vec_out[0:1, :] += jnp.sum(d_branch.astype(F32), axis=0, keepdims=True)
    vec_out[1:2, :] += jnp.sum(d_normed * unit, axis=0, keepdims=True)
    vec_out[2:3, :] += jnp.sum(d_normed, axis=0, keepdims=True)
    vec_out[3:4, :] += jnp.sum(upstream, axis=0, keepdims=True)
    attended = att[...]
    out_acc[...] += dot(attended.astype(BF), d_branch)
    d_att = dot_nt(w_out[...], d_branch).astype(BF).astype(F32)
    place = iota((1, rows), 1) % R
    far_delta = jnp.zeros((1, rows), F32)
    product = d_att * attended
    for h in range(H):
        lane = slice(h * size, (h + 1) * size)
        here = place == h
        total = jnp.sum(product[lane, :], axis=0, keepdims=True)
        fade = near_fade[h]
        far = jnp.where(here, far_fade[...], 0.0)
        near_num[lane, :] = (d_att[lane, :] * fade).astype(BF)
        far_num[lane, :] = (d_att[lane, :] * far).astype(BF)
        delta_out[h] = -total * fade
        far_delta = far_delta + total * far
    dnum_out[...] = near_num[...]
    if pieces:
        mine = own_head(width, 0, rows, size)
        queries = jnp.where(mine, q[...], jnp.zeros((width, rows), BF))
        numer = far_num[...]
        weights = e_far[...]
        prob = dot(values[...], numer) - far_delta
        d_scores = (weights.astype(F32) * prob).astype(BF)
        dq_out[...] = jnp.where(mine, dot(keys[...], d_scores), 0.0)
        key_acc[...] += dot_nt(d_scores, queries)
        value_acc[...] += dot_nt(weights, numer)
    else:
        far_delta_out[...] = far_delta

    @pl.when(step == pl.num_programs(0) - 1)
    def _():
        if pieces:
            for i, out in enumerate(far_grads):
                at = slice(i * chunk, (i + 1) * chunk)
                out[:, :width] = (key_acc[at, :] * score_scale).astype(BF)
                out[:, width:] = value_acc[at, :].astype(BF)
        share = width // blocks
        for j in range(blocks // 2):
            for out, core in ((keep, 0), (send, 1)):
                start = pl.multiple_of(((2 * j + core) ^ me) * share, share)
                out[j] = out_acc[pl.ds(start, share), :].astype(BF)


def split(info, hidden, dn, g, gain, att, near_fade, far_fade, w_out, q, e_far, parts, score_scale):
    width, tokens = q.shape
    size = width // H
    rows = 256
    blocks = 8
    far = e_far.shape[0]
    column = pl.BlockSpec((width, rows), lambda i: (0, i))
    block = pl.BlockSpec((rows, width), lambda i: (i, 0))
    heads = pl.BlockSpec((H, 1, rows), lambda i: (0, 0, i))
    row = pl.BlockSpec((1, rows), lambda i: (0, i))
    small = not parts
    extra_specs = [column, row] if small else [whole()] * len(parts)
    extra_shapes = (
        [shape((width, tokens), BF), shape((1, tokens), F32)]
        if small
        else [shape((part.shape[0], 2 * width), BF) for part in parts]
    )
    far_scratch = [
        pltpu.VMEM((width, far), BF),
        pltpu.VMEM((far, width), BF),
        pltpu.VMEM((far, width), F32),
        pltpu.VMEM((far, width), F32),
    ]
    number = pltpu.VMEM((width, rows), BF)
    total = pltpu.VMEM((width, width), F32)
    return pl.pallas_call(
        functools.partial(
            split_body, pieces=len(parts), size=size, score_scale=score_scale, blocks=blocks
        ),
        grid=(tokens // rows,),
        in_specs=[
            scalars(),
            block,
            block,
            block,
            whole(),
            column,
            heads,
            row,
            whole(),
            column,
            pl.BlockSpec(memory_space=pl.ANY)
            if small
            else pl.BlockSpec((far, rows), lambda i: (0, i)),
        ]
        + [whole()] * len(parts),
        out_specs=[block, column, heads, column] + [whole()] * 3 + extra_specs,
        out_shape=[
            shape((tokens, width), F32),
            shape((width, tokens), BF),
            shape((H, 1, tokens), F32),
            shape((width, tokens), F32),
            shape((blocks // 2, width // blocks, width), BF),
            shape((blocks // 2, width // blocks, width), BF),
            shape((8, width), F32),
        ]
        + extra_shapes,
        scratch_shapes=[number, total] if small else [number, number, total] + far_scratch,
        compiler_params=params(),
        cost_estimate=cost(19),
        name="split",
    )(info, hidden, dn, g, gain, att, near_fade, far_fade, w_out, q, e_far, *parts)


def back_body(*refs, score_scale):
    (e, dnum, delta, q, k, v, dq_far) = refs[:7]
    (dq_out, dk_out, dv_out, scores) = refs[-4:]
    size, tokens = q.shape
    numer = dnum[...]
    low = delta[0]
    terms = []
    for _ in range(3):
        term = low.astype(BF).astype(F32)
        terms.append(term)
        low = low - term
    at = iota((16, tokens), 0)
    extra = jnp.where(
        at == 0, terms[0], jnp.where(at == 1, terms[1], jnp.where(at == 2, terms[2], 0.0))
    ).astype(BF)
    blank = jnp.zeros((64, tokens), BF)
    numer_ext = jnp.concatenate([numer, extra, blank], axis=0)
    values = jnp.concatenate([v[...], (at < 3).astype(BF), blank], axis=0).T
    pad = jnp.zeros((80, tokens), BF)
    query_rows = jnp.concatenate([q[...], pad], axis=0).T
    numer_rows = jnp.concatenate([numer, pad], axis=0).T
    rows = 512
    for i in range(tokens // rows):
        part = slice(i * rows, (i + 1) * rows)
        prob = dot(values[part, :], numer_ext)
        weights = e[0, part, :]
        d_scores = (weights.astype(F32) * prob).astype(BF)
        scores[part, :] = d_scores
        dk_out[:, part] = dot(d_scores, query_rows).T[:size] * score_scale
        dv_out[:, part] = dot(weights, numer_rows).T[:size]
    dq_out[...] = ((dot(k[...], scores[...]) + dq_far[...]) * score_scale).astype(BF)


def back(e, dnum, delta, q, k, v, dq_far, first, count, score_scale, after):
    width, tokens = q.shape
    size = width // H
    head = pl.BlockSpec((size, tokens), lambda h: (h + first, 0))
    out = pl.BlockSpec((size, tokens), lambda h: (h, 0))
    return pl.pallas_call(
        functools.partial(back_body, score_scale=score_scale),
        grid=(count,),
        in_specs=[
            pl.BlockSpec((1, tokens, tokens), lambda h: (h + first, 0, 0)),
            head,
            pl.BlockSpec((1, 1, tokens), lambda h: (h + first, 0, 0)),
            head,
            head,
            head,
            head,
        ]
        + idle(after),
        out_specs=[out] * 3,
        out_shape=[
            shape((count * size, tokens), BF),
            shape((count * size, tokens), F32),
            shape((count * size, tokens), F32),
        ],
        scratch_shapes=[pltpu.VMEM((tokens, tokens), BF)],
        compiler_params=params(),
        cost_estimate=cost(2.5 * count),
        name="back",
    )(e, dnum, delta, q, k, v, dq_far, *after)


def weigh_body(*refs, pieces, groups, size, first_row, blocks):
    (info, nt) = refs[:2]
    dqs = refs[2 : 2 + groups]
    dks = refs[2 + groups : 2 + 2 * groups]
    dvs = refs[2 + 2 * groups : 2 + 3 * groups]
    parts = refs[2 + 3 * groups : 2 + 3 * groups + pieces]
    (dq_out, dk_out, dv_out, keep, send, bias_out, acc) = refs[-7:]
    rows, tokens = dq_out.shape
    width = nt.shape[0]
    me = info[1]
    mine = own_head(rows, first_row, tokens, size)
    pick = group_pick(tokens // R, tokens)
    part_rows = rows // groups
    for i, part in enumerate(dqs):
        dq_out[i * part_rows : (i + 1) * part_rows, :] = part[...]
    for out, near_parts, base in ((dk_out, dks, 0), (dv_out, dvs, width)):
        lane = slice(base + first_row, base + first_row + rows)
        total = parts[0][:, lane].astype(F32)
        for part in parts[1:]:
            total = total + part[:, lane].astype(F32)
        high = total.astype(BF)
        low = (total - high.astype(F32)).astype(BF)
        spread = jnp.where(mine, dot(high.T, pick) + dot(low.T, pick), 0.0)
        for i, part in enumerate(near_parts):
            at = slice(i * part_rows, (i + 1) * part_rows)
            out[at, :] = (part[...] + spread[at, :]).astype(BF)
    ones = jnp.ones((8, tokens), BF)
    share = width // blocks
    for i, grad in enumerate((dq_out, dk_out, dv_out)):
        value = grad[...]
        bias_out[i] = dot_nt(ones, value)
        acc[...] = dot_nt(nt[...], value)
        for j in range(blocks // 2):
            for out, core in ((keep, 0), (send, 1)):
                start = pl.multiple_of(((2 * j + core) ^ me) * share, share)
                out[j, :, i * rows : (i + 1) * rows] = acc[pl.ds(start, share), :].astype(BF)


def weigh(info, nt, dqs, dks, dvs, parts, first_row, after):
    width, tokens = nt.shape
    rows = sum(part.shape[0] for part in dqs)
    blocks = 8
    grads = shape((blocks // 2, width // blocks, 3 * rows), BF)
    ins = dqs + dks + dvs + parts
    return pl.pallas_call(
        functools.partial(
            weigh_body,
            pieces=len(parts),
            groups=len(dqs),
            size=width // H,
            first_row=first_row,
            blocks=blocks,
        ),
        in_specs=[scalars(), whole()] + [whole()] * len(ins) + idle(after),
        out_specs=[whole()] * 6,
        out_shape=[shape((rows, tokens), BF)] * 3 + [grads, grads, shape((3, 8, rows), F32)],
        scratch_shapes=[pltpu.VMEM((width, rows), F32)],
        compiler_params=params(),
        cost_estimate=cost(9),
        name="weigh",
    )(info, nt, *ins, *after)


def input_body(*refs, groups):
    (x, gain, dh, wq, wk, wv) = refs[:6]
    grads = refs[6 : 6 + 3 * groups]
    dx_out, vec_out = refs[-2:]

    @pl.when(pl.program_id(0) == 0)
    def _():
        vec_out[...] = jnp.zeros_like(vec_out)

    total = None
    for i, weight in enumerate((wq, wk, wv)):
        for j in range(groups):
            grad = grads[i * groups + j]
            rows = grad.shape[0]
            term = dot(weight[:, j * rows : (j + 1) * rows], grad[...])
            total = term if total is None else total + term
    d_normed = total.T
    unit, rstd = normalized(x[...].astype(F32))
    vec_out[0:1, :] += jnp.sum(d_normed * unit, axis=0, keepdims=True)
    vec_out[1:2, :] += jnp.sum(d_normed, axis=0, keepdims=True)
    dx_out[...] = (dh[...] + norm_backward(d_normed * gain[...], unit, rstd)).astype(BF)


def input_grad(x, gain, dh, wq, wk, wv, dq, dk, dv, after):
    tokens, width = x.shape
    rows = 256
    groups = len(dq)
    block = pl.BlockSpec((rows, width), lambda i: (i, 0))
    return pl.pallas_call(
        functools.partial(input_body, groups=groups),
        grid=(tokens // rows,),
        in_specs=[block, whole(), block]
        + [whole()] * 3
        + [pl.BlockSpec((part.shape[0], rows), lambda i: (0, i)) for part in dq + dk + dv]
        + idle(after),
        out_specs=[block, whole()],
        out_shape=[shape((tokens, width), BF), shape((8, width), F32)],
        compiler_params=params(),
        cost_estimate=cost(11),
        name="input_grad",
    )(x, gain, dh, wq, wk, wv, *dq, *dk, *dv, *after)


def swap(value, axis, mask):
    count = lax.axis_size(axis)
    return lax.ppermute(value, axis, [(i, i ^ mask) for i in range(count)])


def add(left, right):
    return (left.astype(F32) + right.astype(F32)).astype(BF)


def halves(value):
    rows = value.shape[-2] // 2
    return value[..., :rows, :], value[..., rows:, :]


class Sum:
    def __init__(self, keep, send):
        self.rounds = self.run(keep, send)
        self.result = None

    def step(self):
        return next(self.rounds, [])

    def run(self, keep, send):
        got = swap(send, "seq", 1)
        yield [got]
        first, second = halves(add(keep, got))
        one, two = swap(first[1::2], "seq", 2), swap(second[2:], "seq", 4)
        yield [one, two]
        first, second = add(first[0::2], one), add(second[:2], two)
        one, two = swap(first[1], "seq", 4), swap(second[1], "seq", 2)
        yield [one, two]
        value = jnp.concatenate([add(first[0], one), add(second[0], two)], axis=0)
        place = lax.axis_index("rep")
        bits = (place & 1, (place >> 1) & 1)
        for bit, mask in zip(bits, (1, 2)):
            first, second = halves(value)
            got = swap(jnp.where(bit == 0, second, first), "rep", mask)
            yield [got]
            value = add(jnp.where(bit == 0, first, second), got)
        for bit, mask in zip(bits[::-1], (2, 1)):
            got = swap(value, "rep", mask)
            yield [got]
            first, second = jnp.where(bit == 0, value, got), jnp.where(bit == 0, got, value)
            value = jnp.concatenate([first, second], axis=0)
        self.result = value


class PlainSum:
    def __init__(self, keep, send, turn=False):
        both = jnp.stack([keep, send], axis=1)
        if turn:
            both = both.swapaxes(2, 3)
        share = lax.psum_scatter(
            both.reshape(-1, both.shape[-1]), "seq", scatter_dimension=0, tiled=True
        )
        self.result = lax.psum(share, "rep")

    def step(self):
        return []


def vector_sum(value):
    if lax.axis_size("seq") != 8 or lax.axis_size("rep") != 4:
        return lax.psum(value, ("seq", "rep"))
    got = [value] + [swap(value, "seq", b) for b in range(1, 8)]
    value = sum(got[1:], got[0])
    one, two, three = (swap(value, "rep", b) for b in (1, 2, 3))
    return (value + one) + (two + three)


def far_back(values, keys, numer, delta, queries, weights, mine, score_scale):
    prob = dot(values, numer) - delta
    d_scores = (weights.astype(F32) * prob).astype(BF)
    dq = jnp.where(mine, dot(keys.T, d_scores), 0.0)
    queries = jnp.where(mine, queries, jnp.zeros_like(queries))
    dk = dot_nt(d_scores, queries) * score_scale
    return dq, jnp.concatenate([dk.astype(BF), dot_nt(weights, numer).astype(BF)], axis=1)


def per_device(
    tokens,
    lengths,
    tile_valid,
    w_query,
    w_key,
    w_value,
    w_out,
    b_query,
    b_value,
    b_out,
    gain_attn,
    shift_attn,
    gain_mlp,
    shift_mlp,
    w_up,
    b_up,
    w_down,
    b_down,
    cotangent,
):
    rows, width = tokens.shape[1:]
    size = width // H
    score_scale = size ** (-0.5)
    scale = score_scale * LOG2E
    devices = lax.axis_size("seq")
    direct = devices == 8 and lax.axis_size("rep") == 4
    me = lax.axis_index("seq")
    info = jnp.stack([lengths[0] - me * rows, me if direct else jnp.zeros_like(me)])
    info = info.astype(jnp.int32)
    x = tokens[0]
    g = cotangent[0]
    line = lambda v: v.reshape(1, -1)
    q, k, v, nt, far = project(
        info, x, line(gain_attn), line(shift_attn), w_query, w_key, w_value,
        line(b_query), line(b_value), tile_valid, size,
    )
    if direct:
        parts = [far] + [swap(far, "seq", b) for b in range(1, devices)]
    else:
        parts = [lax.all_gather(far, "seq", axis=0, tiled=True)]
    e, numer, peak = near(info, q, k, v, tile_valid, scale)
    att, near_fade, far_fade, hidden, n_two, nt_two, e_far = merge(
        q, numer, peak, x, w_out, line(b_out), line(gain_mlp), line(shift_mlp), parts, scale
    )
    mixed, dn_two, up_keep, up_send, down_keep, down_send, bias_up = feed(
        info, n_two, nt_two, g, w_up, w_down, line(b_up), hidden, line(b_down)
    )
    total = Sum if direct else PlainSum
    up = total(up_keep, up_send)
    down = total(down_keep, down_send) if direct else total(down_keep, down_send, True)
    flying = up.step() + down.step()
    split_outs = split(
        info, hidden, dn_two, g, line(gain_mlp), att, near_fade, far_fade, w_out, q, e_far,
        parts if direct else [], score_scale,
    )
    dh, dnum, delta, dq_far, out_keep, out_send, vec_mid = split_outs[:7]
    if direct:
        far_grads = split_outs[7:]
        owned = [far_grads[0]] + [swap(far_grads[b], "seq", b) for b in range(1, devices)]
    else:
        far_num, far_delta = split_outs[7:]
        dq_far, far_grad = far_back(
            parts[0][:, width : 2 * width], parts[0][:, :width], far_num, far_delta, q, e_far,
            own_head(width, 0, rows, size), score_scale,
        )
        owned = [lax.psum_scatter(far_grad, "seq", scatter_dimension=0, tiled=True)]
    out = total(out_keep, out_send)
    sums = [up, down, out]
    dqs, dks, dvs, shares, biases = [], [], [], [], []
    count = H // 4

    def attend(first, after):
        return back(e, dnum, delta, q, k, v, dq_far, first, count, score_scale, after)

    def advance(*chosen):
        return [array for item in chosen for array in item.step()]

    for half in range(2):
        grads = []
        for quarter in range(2):
            landed, flying = flying, []
            if half == 0 and quarter == 0:
                flying = advance(up, out)
            else:
                flying = advance(*sums)
            grads.append(attend((2 * half + quarter) * count, landed))
        landed, flying = flying, []
        flying = advance(*sums)
        dq, dk, dv, keep, send, bias = weigh(
            info, nt, *([part[i] for part in grads] for i in range(3)), owned,
            half * 2 * count * size, landed,
        )
        dqs.append(dq)
        dks.append(dk)
        dvs.append(dv)
        biases.append(bias[:, 0])
        sums.append(total(keep, send))
        shares.append(sums[-1])
    landed, flying = flying, advance(*sums)
    dx, vec_in = input_grad(
        x, line(gain_attn), dh, w_query, w_key, w_value, dqs, dks, dvs, landed
    )
    while flying:
        flying = advance(*sums)
    bias_all = jnp.concatenate(biases, axis=1)
    vectors = jnp.concatenate(
        [bias_all[0:1], bias_all[2:3], vec_mid[0:1], vec_in[:2], vec_mid[1:4], bias_up.reshape(-1, width)],
        axis=0,
    )
    vectors = vector_sum(vectors)
    share = width // devices
    mine = lax.dynamic_slice_in_dim(vectors[:8], me * share, share, 1)
    mine_up = lax.dynamic_slice_in_dim(vectors[8:].reshape(-1), me * 4 * share, 4 * share, 0)
    wide = 2 * count * size
    qkv = [
        jnp.concatenate([s.result[:, i * wide : (i + 1) * wide] for s in shares], axis=1).astype(
            F32
        )
        for i in range(3)
    ]
    grad_down = down.result.astype(F32)
    if direct:
        grad_down = grad_down.T
    return (
        mixed[None],
        dx[None],
        qkv[0],
        qkv[1],
        qkv[2],
        out.result.astype(F32),
        mine[0],
        mine[1],
        mine[2],
        mine[3],
        mine[4],
        mine[5],
        mine[6],
        up.result.astype(F32),
        mine_up,
        grad_down,
        mine[7],
    )


def solution(mesh):
    split_specs = P("rep", "seq", None)
    in_specs = (split_specs, P("rep"), P("rep", "seq")) + (P(),) * 15 + (split_specs,)
    out_specs = (
        (split_specs,) * 2
        + (P("seq", None),) * 4
        + (P("seq"),) * 7
        + (P("seq", None), P("seq"), P("seq", None), P("seq"))
    )
    return jax.shard_map(
        per_device, mesh=mesh, in_specs=in_specs, out_specs=out_specs, check_vma=False
    )
```

```python
import functools

import jax
import jax.numpy as jnp
from jax import lax
from jax.experimental import pallas as pl
from jax.experimental.pallas import tpu as pltpu
from jax.sharding import PartitionSpec as P

H = 16
R = 16
EPS = 1e-05
LOG2E = 1.4426950408889634
NEG = -1e30
BF = jnp.bfloat16
F32 = jnp.float32
VMEM_LIMIT = 48 * 1024 * 1024
PER_STEP = 1
SAFE = 60.0
B_QUERY, B_VALUE, B_OUT, GAIN_ATTN, SHIFT_ATTN, GAIN_MLP, SHIFT_MLP, B_DOWN = (
    slice(i, i + 1) for i in range(8)
)


def row_of(vector):
    return vector[...].reshape(1, -1)


def iota(shape, dim):
    return lax.broadcasted_iota(jnp.int32, shape, dim)


def dot(left, right):
    return jnp.dot(left, right, preferred_element_type=F32)


def dot_nt(left, right):
    return lax.dot_general(left, right, (((1,), (1,)), ((), ())), preferred_element_type=F32)


def params():
    return pltpu.CompilerParams(vmem_limit_bytes=VMEM_LIMIT)


def cost(micros):
    return pl.CostEstimate(flops=int(micros * 1.15e9), bytes_accessed=1024, transcendentals=0)


def whole():
    return pl.BlockSpec(memory_space=pltpu.VMEM)


def idle(arrays):
    return [pl.BlockSpec(memory_space=pl.ANY)] * len(arrays)


def scalars():
    return pl.BlockSpec(memory_space=pltpu.SMEM)


def shape(dims, kind):
    return jax.ShapeDtypeStruct(dims, kind)


def normalized(values):
    center = values - jnp.mean(values, axis=-1, keepdims=True)
    rstd = lax.rsqrt(jnp.mean(center * center, axis=-1, keepdims=True) + EPS)
    return center * rstd, rstd


def norm_backward(grad, unit, rstd):
    return rstd * (
        grad
        - jnp.mean(grad, axis=-1, keepdims=True)
        - unit * jnp.mean(grad * unit, axis=-1, keepdims=True)
    )


def own_head(rows, first_row, columns, size):
    feature = iota((rows, columns), 0) + first_row
    start = (iota((rows, columns), 1) % R) * size
    return (feature >= start) & (feature < start + size)


def group_pick(groups, columns):
    return (iota((groups, columns), 1) // R == iota((groups, columns), 0)).astype(BF)


def place_of(info, j, leaves):
    core = ((info[1] & 1) ^ leaves) & info[2]
    straight, turned = j << 1, ((j & 1) << 2) | (j & 2)
    return info[1] ^ leaves ^ jnp.where(core == 1, turned, straight)


def project_body(
    info, x, gain, shift, wq, wk, wv, bq, bv, valid, q_out, k_out, v_out, n_out, far_out, *, size
):
    rows, width = x.shape
    unit, _ = normalized(x[...].astype(F32))
    normed = (unit * row_of(gain) + row_of(shift)).astype(BF)
    n_out[...] = normed.T
    q_out[...] = (dot(normed, wq[...]) + row_of(bq)).astype(BF).T
    keys = dot(normed, wk[...]).astype(BF)
    values = (dot(normed, wv[...]) + row_of(bv)).astype(BF)
    k_out[...] = keys.T
    v_out[...] = values.T
    feature = iota((rows, width), 1)
    start = (iota((rows, width), 0) % R) * size
    mine = (feature >= start) & (feature < start + size)
    pick = group_pick(rows // R, rows)
    zero = jnp.zeros((rows, width), BF)
    far_out[:, :width] = dot(pick, jnp.where(mine, keys, zero)).astype(BF)
    far_out[:, width : 2 * width] = dot(pick, jnp.where(mine, values, zero)).astype(BF)
    place = iota((1, rows), 1) + pl.program_id(0) * rows
    good = jnp.where((valid[...] > 0) & (place < info[0]), 1.0, 0.0)
    residue = (iota((rows, 128), 0) % R == iota((rows, 128), 1)).astype(BF)
    found = dot((pick.astype(F32) * good).astype(BF), residue)
    far_out[:, 2 * width :] = jnp.where(found > 0.5, 0.0, NEG).astype(BF)


def project(info, x, gain, shift, wq, wk, wv, bq, bv, valid, size):
    tokens, width = x.shape
    rows = 256
    column = pl.BlockSpec((width, rows), lambda i: (0, i))
    return pl.pallas_call(
        functools.partial(project_body, size=size),
        grid=(tokens // rows,),
        in_specs=[scalars(), pl.BlockSpec((rows, width), lambda i: (i, 0))]
        + [whole()] * 7
        + [pl.BlockSpec((1, rows), lambda i: (0, i))],
        out_specs=[column] * 4 + [pl.BlockSpec((rows // R, 2 * width + 128), lambda i: (i, 0))],
        out_shape=[shape((width, tokens), BF)] * 4 + [shape((tokens // R, 2 * width + 128), BF)],
        compiler_params=params(),
        cost_estimate=cost(10),
        name="project",
    )(info, x, gain, shift, wq, wk, wv, bq, bv, valid)


def near_body(*refs, scale, size):
    (info, q, k, v, valid) = refs[:5]
    (e_out, numer_out, peak_out) = refs[-3:]
    tokens = q.shape[1]
    first = iota((32, tokens), 0) == 0
    good = (valid[...] > 0) & (iota((1, tokens), 1) < info[0])
    mask = jnp.where(first, jnp.where(good, 0.0, NEG), 0.0).astype(BF)
    one = first.astype(BF)
    for i in range(PER_STEP):
        lane = slice(i * size, (i + 1) * size)
        scaled = q[lane, :].astype(F32) * scale
        plain = k[lane, :].astype(F32)
        high = scaled.astype(BF)
        low = (scaled - high.astype(F32)).astype(BF)
        queries = jnp.concatenate([high, low, one], axis=0)
        keys = jnp.concatenate([k[lane, :], k[lane, :], mask], axis=0).T
        values = jnp.concatenate([v[lane, :], one[:16]], axis=0)
        bound = jnp.max(jnp.sum(scaled * scaled, axis=0)) * jnp.max(
            jnp.sum(plain * plain, axis=0)
        )
        safe = bound < SAFE * SAFE

        @pl.when(safe)
        def _():
            weights = jnp.exp2(dot(keys, queries)).astype(BF)
            e_out[i] = weights
            numer_out[i] = dot(values, weights)
            peak_out[i] = jnp.zeros((1, tokens), F32)

        @pl.when(jnp.logical_not(safe))
        def _():
            scores = dot(keys, queries)
            peak = jnp.max(scores, axis=0, keepdims=True)
            weights = jnp.exp2(scores - peak).astype(BF)
            e_out[i] = weights
            numer_out[i] = dot(values, weights)
            peak_out[i] = peak


def near(info, q, k, v, valid, scale, first, count, after):
    width, tokens = q.shape
    size = width // H
    head = pl.BlockSpec((PER_STEP * size, tokens), lambda h: (h + first // PER_STEP, 0))

    def block(rows):
        return pl.BlockSpec((PER_STEP, rows, tokens), lambda h: (h, 0, 0))

    return pl.pallas_call(
        functools.partial(near_body, scale=scale, size=size),
        grid=(count // PER_STEP,),
        in_specs=[scalars()]
        + [head] * 3
        + [pl.BlockSpec((1, tokens), lambda h: (0, 0))]
        + idle(after),
        out_specs=[block(tokens), block(size + 16), block(1)],
        out_shape=[
            shape((count, tokens, tokens), BF),
            shape((count, size + 16, tokens), F32),
            shape((count, 1, tokens), F32),
        ],
        compiler_params=params(),
        cost_estimate=cost(2 * count),
        name="near",
    )(info, q, k, v, valid, *after)


def merge_body(*refs, scale, pieces, groups, size):
    (q, x, w_out, b_out, gain, shift) = refs[:6]
    parts = refs[6 : 6 + pieces]
    numers = refs[6 + pieces : 6 + pieces + groups]
    peaks = refs[6 + pieces + groups : 6 + pieces + 2 * groups]
    (att_out, near_out, far_out, hidden_out, n_out, nt_out, e_out) = refs[-11:-4]
    keys, values, masks, att = refs[-4:]
    width, rows = q.shape
    heads = [(group, h) for group, ref in enumerate(peaks) for h in range(ref.shape[0])]

    @pl.when(pl.program_id(0) == 0)
    def _():
        first = 0
        for part in parts:
            at = slice(first, first + part.shape[0])
            first = at.stop
            keys[at, :] = part[:, :width]
            values[:, at] = part[:, width : 2 * width].T
            masks[at, :] = part[:, 2 * width :]

    mine = own_head(width, 0, rows, size)
    queries = jnp.where(mine, q[...], jnp.zeros((width, rows), BF))
    residue = (iota((128, rows), 1) % R == iota((128, rows), 0)).astype(BF)
    scores = dot(keys[...], queries) * scale + dot(masks[...], residue)
    far_peak = jnp.max(scores, axis=0, keepdims=True)
    weights = jnp.exp2(scores - far_peak)
    far_denom = jnp.sum(weights, axis=0, keepdims=True)
    weights = weights.astype(BF)
    e_out[...] = weights
    far_numer = dot(values[...], weights)
    place = iota((1, rows), 1) % R
    far_row = jnp.zeros((1, rows), F32)
    for h, (group, at) in enumerate(heads):
        lane = slice(h * size, (h + 1) * size)
        here = place == h
        numer = numers[group]
        near_peak = peaks[group][at]
        top = jnp.maximum(near_peak, jnp.where(here, far_peak, NEG))
        near_fade = jnp.exp2(near_peak - top)
        far_fade = jnp.where(here, jnp.exp2(far_peak - top), 0.0)
        inverse = 1.0 / (near_fade * numer[at, size : size + 1, :] + far_fade * far_denom)
        near_fade = near_fade * inverse
        far_fade = far_fade * inverse
        near_out[h] = near_fade
        far_row = far_row + far_fade
        att[lane, :] = numer[at, :size, :] * near_fade + far_numer[lane, :] * far_fade
    far_out[...] = far_row
    attended = att[...]
    att_out[...] = attended
    hidden = x[...].astype(F32) + dot(attended.astype(BF).T, w_out[...]) + row_of(b_out)
    hidden_out[...] = hidden
    unit, _ = normalized(hidden)
    normed = (unit * row_of(gain) + row_of(shift)).astype(BF)
    n_out[...] = normed
    nt_out[...] = normed.T


def merge(q, numers, peaks, x, w_out, b_out, gain, shift, parts, scale):
    width, tokens = q.shape
    size = width // H
    rows = 256
    far = sum(part.shape[0] for part in parts)
    column = pl.BlockSpec((width, rows), lambda i: (0, i))
    block = pl.BlockSpec((rows, width), lambda i: (i, 0))

    def heads(count, depth):
        return pl.BlockSpec((count, depth, rows), lambda i: (0, 0, i))

    return pl.pallas_call(
        functools.partial(
            merge_body, scale=scale, pieces=len(parts), groups=len(peaks), size=size
        ),
        grid=(tokens // rows,),
        in_specs=[column, block]
        + [whole()] * 4
        + [whole()] * len(parts)
        + [heads(*part.shape[:2]) for part in numers + peaks],
        out_specs=[
            column,
            heads(H, 1),
            pl.BlockSpec((1, rows), lambda i: (0, i)),
            block,
            block,
            column,
            pl.BlockSpec((far, rows), lambda i: (0, i)),
        ],
        out_shape=[
            shape((width, tokens), F32),
            shape((H, 1, tokens), F32),
            shape((1, tokens), F32),
            shape((tokens, width), F32),
            shape((tokens, width), BF),
            shape((width, tokens), BF),
            shape((far, tokens), BF),
        ],
        scratch_shapes=[
            pltpu.VMEM((far, width), BF),
            pltpu.VMEM((width, far), BF),
            pltpu.VMEM((far, 128), BF),
            pltpu.VMEM((width, rows), F32),
        ],
        compiler_params=params(),
        cost_estimate=cost(13),
        name="merge",
    )(q, x, w_out, b_out, gain, shift, *parts, *numers, *peaks)


def gelu_pair(u):
    size = jnp.abs(u)
    t = 1.0 / (1.0 + (0.3275911 * 0.7071067811865476) * size)
    bell = jnp.exp2(u * u * (-0.5 * LOG2E))
    poly = t * (
        0.5 * 0.254829592
        + t
        * (
            0.5 * -0.284496736
            + t * (0.5 * 1.421413741 + t * (0.5 * -1.453152027 + t * (0.5 * 1.061405429)))
        )
    )
    tail = poly * bell
    phi = jnp.where(u > 0, 1.0 - tail, tail)
    return u * phi, phi + u * bell * 0.3989422804014327


def feed_body(
    info, n, nt, g, w_up, w_down, b_up, hidden, b_down,
    mixed_out, dn_out, up_keep, up_send, down_keep, down_send, bias_out,
    gt, act, dup, mix, grad, b_up_row, *, blocks,
):
    step = pl.program_id(0)
    tokens, width = n.shape
    wide = w_up.shape[1]
    half = wide // 2

    @pl.when(step == 0)
    def _():
        gt[...] = g[...].T
        b_up_row[...] = row_of(b_up)
        mix[...] = jnp.zeros_like(mix)
        dn_out[...] = jnp.zeros_like(dn_out)

    part = hidden.shape[0]
    mix[pl.ds(pl.multiple_of(step * part, part), part), :] += hidden[...] + row_of(b_down)
    bias = b_up_row[:, pl.ds(pl.multiple_of(step * wide, wide), wide)]
    bias_sum = jnp.zeros((1, wide), F32)
    rows = 256
    for i in range(tokens // rows):
        at = slice(i * rows, (i + 1) * rows)
        upper = dot(n[at, :], w_up[...]) + bias
        value, slope = gelu_pair(upper)
        value = value.astype(BF)
        act[at, :] = value
        mix[at, :] += dot(value, w_down[...])
        d_upper = (dot_nt(g[at, :], w_down[...]) * slope).astype(BF)
        dup[at, :] = d_upper
        bias_sum = bias_sum + jnp.sum(d_upper.astype(F32), axis=0, keepdims=True)
        dn_out[at, :] += dot_nt(d_upper, w_up[...])
    bias_out[...] = bias_sum
    grad[...] = dot(nt[...], dup[...])
    share = width // blocks
    for j in range(blocks // 2):
        for out, leaves in ((up_keep, 0), (up_send, 1)):
            start = pl.multiple_of(place_of(info, j, leaves) * share, share)
            out[j] = grad[pl.ds(start, share), :].astype(BF)
    for out, leaves in ((down_keep, 0), (down_send, 1)):
        start = pl.multiple_of(((info[1] & 1) ^ leaves) * half, half)
        out[0] = dot(gt[...], act[:, pl.ds(start, half)]).astype(BF)

    @pl.when(step == pl.num_programs(0) - 1)
    def _():
        mixed_out[...] = mix[...].astype(BF)


def feed(info, n, nt, g, w_up, w_down, b_up, hidden, b_down):
    tokens, width = n.shape
    hidden_units = w_up.shape[1]
    blocks = 8
    steps = 4
    wide = hidden_units // steps
    rows = pl.BlockSpec((blocks // 2, width // blocks, wide), lambda c, info: (0, 0, c))

    def pair(leaves):
        def place(c, info):
            chips = c ^ (info[1] >> 1)
            core = ((info[1] & 1) ^ leaves) & info[2]
            return (jnp.where(core == 1, ((chips & 1) << 1) | (chips >> 1), chips), 0, 0)

        return pl.BlockSpec((1, width, wide // 2), place)

    full = pl.BlockSpec(memory_space=pltpu.VMEM)
    return pl.pallas_call(
        functools.partial(feed_body, blocks=blocks),
        grid_spec=pltpu.PrefetchScalarGridSpec(
            num_scalar_prefetch=1,
            grid=(steps,),
            in_specs=[
                full,
                full,
                full,
                pl.BlockSpec((width, wide), lambda c, info: (0, c)),
                pl.BlockSpec((wide, width), lambda c, info: (c, 0)),
                full,
                pl.BlockSpec((tokens // steps, width), lambda c, info: (c, 0)),
                full,
            ],
            out_specs=[full, full, rows, rows, pair(0), pair(1)]
            + [pl.BlockSpec((1, wide), lambda c, info: (0, c))],
            scratch_shapes=[
                pltpu.VMEM((width, tokens), BF),
                pltpu.VMEM((tokens, wide), BF),
                pltpu.VMEM((tokens, wide), BF),
                pltpu.VMEM((tokens, width), F32),
                pltpu.VMEM((width, wide), F32),
                pltpu.VMEM((1, hidden_units), F32),
            ],
        ),
        out_shape=[
            shape((tokens, width), BF),
            shape((tokens, width), F32),
            shape((blocks // 2, width // blocks, hidden_units), BF),
            shape((blocks // 2, width // blocks, hidden_units), BF),
            shape((blocks // 2, width, hidden_units // blocks), BF),
            shape((blocks // 2, width, hidden_units // blocks), BF),
            shape((1, hidden_units), F32),
        ],
        compiler_params=params(),
        cost_estimate=cost(46),
        name="feed",
    )(info, n, nt, g, w_up, w_down, b_up, hidden, b_down)


def split_body(*refs, size):
    (hidden, dn, g, gain, att, near_fade, far_fade, w_out) = refs[:8]
    (dh_out, db_out, dnum_out, delta_out, far_num, far_delta_out, vec_out) = refs[-7:]
    width, rows = att.shape

    @pl.when(pl.program_id(0) == 0)
    def _():
        vec_out[...] = jnp.zeros_like(vec_out)

    unit, rstd = normalized(hidden[...])
    d_normed = dn[...]
    upstream = g[...].astype(F32)
    d_hidden = upstream + norm_backward(d_normed * row_of(gain), unit, rstd)
    dh_out[...] = d_hidden
    d_branch = d_hidden.astype(BF)
    db_out[...] = d_branch
    vec_out[0:1, :] += jnp.sum(d_branch.astype(F32), axis=0, keepdims=True)
    vec_out[1:2, :] += jnp.sum(d_normed * unit, axis=0, keepdims=True)
    vec_out[2:3, :] += jnp.sum(d_normed, axis=0, keepdims=True)
    vec_out[3:4, :] += jnp.sum(upstream, axis=0, keepdims=True)
    d_att = dot_nt(w_out[...], d_branch).astype(BF).astype(F32)
    product = d_att * att[...]
    place = iota((1, rows), 1) % R
    far_delta = jnp.zeros((1, rows), F32)
    for h in range(H):
        lane = slice(h * size, (h + 1) * size)
        total = jnp.sum(product[lane, :], axis=0, keepdims=True)
        fade = near_fade[h]
        far = jnp.where(place == h, far_fade[...], 0.0)
        dnum_out[lane, :] = (d_att[lane, :] * fade).astype(BF)
        far_num[lane, :] = (d_att[lane, :] * far).astype(BF)
        delta_out[h] = -total * fade
        far_delta = far_delta + total * far
    far_delta_out[...] = far_delta


def split(hidden, dn, g, gain, att, near_fade, far_fade, w_out, after):
    width, tokens = att.shape
    rows = 256
    column = pl.BlockSpec((width, rows), lambda i: (0, i))
    block = pl.BlockSpec((rows, width), lambda i: (i, 0))
    heads = pl.BlockSpec((H, 1, rows), lambda i: (0, 0, i))
    row = pl.BlockSpec((1, rows), lambda i: (0, i))
    return pl.pallas_call(
        functools.partial(split_body, size=width // H),
        grid=(tokens // rows,),
        in_specs=[block, block, block, whole(), column, heads, row, whole()] + idle(after),
        out_specs=[block, block, column, heads, column, row, whole()],
        out_shape=[
            shape((tokens, width), F32),
            shape((tokens, width), BF),
            shape((width, tokens), BF),
            shape((H, 1, tokens), F32),
            shape((width, tokens), BF),
            shape((1, tokens), F32),
            shape((8, width), F32),
        ],
        compiler_params=params(),
        cost_estimate=cost(9),
        name="split",
    )(hidden, dn, g, gain, att, near_fade, far_fade, w_out, *after)


def far_body(*refs, pieces, size, score_scale, blocks):
    (q, numer, delta, e) = refs[:4]
    parts = refs[4 : 4 + pieces]
    (dq_out, keep, send, keys, values, grad) = refs[-6:]
    width, tokens = q.shape
    first = 0
    for part in parts:
        at = slice(first, first + part.shape[0])
        first = at.stop
        keys[:, at] = part[:, :width].T
        values[at, :] = part[:, width : 2 * width]
    share = first // blocks
    mine = own_head(width, 0, tokens, size)
    queries = jnp.where(mine, q[...], jnp.zeros((width, tokens), BF))
    weights = e[...]
    prob = dot(values[...], numer[...]) - delta[...]
    d_scores = (weights.astype(F32) * prob).astype(BF)
    dq_out[...] = jnp.where(mine, dot(keys[...], d_scores), 0.0).astype(BF)
    for lane, left, right, factor in (
        (slice(0, width), d_scores, queries, score_scale),
        (slice(width, 2 * width), weights, numer[...], 1.0),
    ):
        grad[...] = dot_nt(left, right) * factor
        for j in range(blocks):
            out = (keep, send)[j % 2]
            out[j // 2, :, lane] = grad[j * share : (j + 1) * share, :].astype(BF)


def far_kernel(q, numer, delta, e, parts, score_scale, after):
    width, tokens = q.shape
    far = e.shape[0]
    blocks = 8
    grads = shape((blocks // 2, far // blocks, 2 * width), BF)
    return pl.pallas_call(
        functools.partial(
            far_body, pieces=len(parts), size=width // H, score_scale=score_scale, blocks=blocks
        ),
        in_specs=[whole()] * (4 + len(parts)) + idle(after),
        out_specs=[whole()] * 3,
        out_shape=[shape((width, tokens), BF), grads, grads],
        scratch_shapes=[
            pltpu.VMEM((width, far), BF),
            pltpu.VMEM((far, width), BF),
            pltpu.VMEM((far, width), F32),
        ],
        compiler_params=params(),
        cost_estimate=cost(9),
        name="far",
    )(q, numer, delta, e, *parts, *after)


def back_body(*refs, size, score_scale):
    (e, dnum, delta, q, k, v, dq_far) = refs[:7]
    (out, scores) = refs[-2:]
    tokens = q.shape[1]
    at = iota((16, tokens), 0)
    blank = jnp.zeros((64, tokens), BF)
    ones = (at < 3).astype(BF)
    probs = []
    for i in range(PER_STEP):
        lane = slice(i * size, (i + 1) * size)
        low = delta[i]
        terms = []
        for _ in range(3):
            term = low.astype(BF).astype(F32)
            terms.append(term)
            low = low - term
        extra = jnp.where(
            at == 0, terms[0], jnp.where(at == 1, terms[1], jnp.where(at == 2, terms[2], 0.0))
        ).astype(BF)
        numer = jnp.concatenate([dnum[lane, :], extra, blank], axis=0)
        values = jnp.concatenate([v[lane, :], ones, blank], axis=0).T
        scores[i] = (e[i].astype(F32) * dot(values, numer)).astype(BF)
    for i in range(PER_STEP):
        lane = slice(i * size, (i + 1) * size)
        d_scores = scores[i]
        near_part = dot(k[lane, :], d_scores)
        out[0, lane, :] = ((near_part + dq_far[lane, :].astype(F32)) * score_scale).astype(BF)
        out[1, lane, :] = (dot_nt(q[lane, :], d_scores) * score_scale).astype(BF)
        out[2, lane, :] = dot_nt(dnum[lane, :], e[i]).astype(BF)


def back(e, skip, dnum, delta, q, k, v, dq_far, first, count, score_scale, after):
    width, tokens = q.shape
    size = width // H
    wide = PER_STEP * size
    start, skip = first // PER_STEP, skip // PER_STEP
    head = pl.BlockSpec((wide, tokens), lambda h: (h + start, 0))
    return pl.pallas_call(
        functools.partial(back_body, size=size, score_scale=score_scale),
        grid=(count // PER_STEP,),
        in_specs=[
            pl.BlockSpec((PER_STEP, tokens, tokens), lambda h: (h + skip, 0, 0)),
            head,
            pl.BlockSpec((PER_STEP, 1, tokens), lambda h: (h + start, 0, 0)),
            head,
            head,
            head,
            head,
        ]
        + idle(after),
        out_specs=pl.BlockSpec((3, wide, tokens), lambda h: (0, h, 0)),
        out_shape=shape((3, count * size, tokens), BF),
        scratch_shapes=[pltpu.VMEM((PER_STEP, tokens, tokens), BF)],
        compiler_params=params(),
        cost_estimate=cost(2.3 * count),
        name="back",
    )(e, dnum, delta, q, k, v, dq_far, *after)


def weigh_body(*refs, pieces, groups, extra, size, first_row, blocks):
    (info, nt) = refs[:2]
    grads = refs[2 : 2 + groups]
    parts = refs[2 + groups : 2 + groups + pieces]
    others = refs[2 + groups + pieces : 2 + groups + pieces + extra]
    (d_out, keep, send, bias_out, acc) = refs[-5:]
    rows, tokens = d_out.shape[1:]
    width = nt.shape[0]
    step = pl.program_id(0)

    @pl.when(step == 0)
    def _():
        at = 0
        for part in grads:
            d_out[0, at : at + part.shape[1], :] = part[0]
            at = at + part.shape[1]

    @pl.when((step == 1) | (step == 2))
    def _():
        total = parts[0][...].astype(F32)
        for part in parts[1:]:
            total = total + part[...].astype(F32)
        high = total.astype(BF)
        low = (total - high.astype(F32)).astype(BF)
        pick = group_pick(tokens // R, tokens)
        spread = jnp.where(
            own_head(rows, first_row, tokens, size), dot(high.T, pick) + dot(low.T, pick), 0.0
        )
        at = 0
        for part in grads:
            end = at + part.shape[1]
            d_out[0, at:end, :] = (part[0].astype(F32) + spread[at:end, :]).astype(BF)
            at = end

    @pl.when(step < 3)
    def _():
        value = d_out[0]
        bias_out[0] = dot_nt(jnp.ones((8, tokens), BF), value)
        acc[...] = dot_nt(nt[...], value)

    if extra:

        @pl.when(step >= 3)
        def _():
            acc[...] = dot(others[0][...].astype(BF), others[1][...])

    share = width // blocks
    for j in range(blocks // 2):
        for out, leaves in ((keep, 0), (send, 1)):
            start = pl.multiple_of(place_of(info, j, leaves) * share, share)
            out[j] = acc[pl.ds(start, share), :].astype(BF)


def weigh(info, nt, grads, parts, extra, first_row, after):
    width, tokens = nt.shape
    rows = sum(part.shape[1] for part in grads)
    blocks = 8
    steps = 3 + (width // rows if extra else 0)
    column = first_row // rows
    lanes = width // rows
    kind = lambda i: jnp.minimum(i, 2)
    sums = shape((blocks // 2, width // blocks, steps * rows), BF)
    sums_spec = pl.BlockSpec((blocks // 2, width // blocks, rows), lambda i: (0, 0, i))
    return pl.pallas_call(
        functools.partial(
            weigh_body,
            pieces=len(parts),
            groups=len(grads),
            extra=len(extra),
            size=width // H,
            first_row=first_row,
            blocks=blocks,
        ),
        grid=(steps,),
        in_specs=[scalars(), whole()]
        + [pl.BlockSpec((1, part.shape[1], tokens), lambda i: (kind(i), 0, 0)) for part in grads]
        + [
            pl.BlockSpec(
                (part.shape[0], rows), lambda i: (0, column + lanes * (kind(i) // 2))
            )
            for part in parts
        ]
        + (
            [whole(), pl.BlockSpec((tokens, rows), lambda i: (0, jnp.maximum(i - 3, 0)))]
            if extra
            else []
        )
        + idle(after),
        out_specs=[
            pl.BlockSpec((1, rows, tokens), lambda i: (kind(i), 0, 0)),
            sums_spec,
            sums_spec,
            pl.BlockSpec((1, 8, rows), lambda i: (kind(i), 0, 0)),
        ],
        out_shape=[shape((3, rows, tokens), BF), sums, sums, shape((3, 8, rows), F32)],
        scratch_shapes=[pltpu.VMEM((width, rows), F32)],
        compiler_params=params(),
        cost_estimate=cost(2.2 * steps),
        name="weigh",
    )(info, nt, *grads, *parts, *extra, *after)


def input_body(*refs, groups, begun):
    (x, gain, dh, wq, wk, wv) = refs[:6]
    grads = refs[6 : 6 + groups]
    rest = refs[6 + groups :]
    dx_out, vec_out = refs[-2:]
    width = x.shape[1]

    @pl.when(pl.program_id(0) == 0)
    def _():
        if begun:
            vec_out[...] = rest[0][...]
        else:
            biases, (vec_mid, bias_up) = rest[:groups], rest[groups : groups + 2]
            vec_out[...] = jnp.zeros_like(vec_out)
            at = 0
            for bias in biases:
                end = at + bias.shape[2]
                vec_out[B_QUERY, at:end] = bias[0, 0:1, :]
                vec_out[B_VALUE, at:end] = bias[2, 0:1, :]
                at = end
            vec_out[B_OUT, :] = vec_mid[0:1, :]
            vec_out[GAIN_MLP, :] = vec_mid[1:2, :]
            vec_out[SHIFT_MLP, :] = vec_mid[2:3, :]
            vec_out[B_DOWN, :] = vec_mid[3:4, :]
            for i in range(bias_up.shape[1] // width):
                vec_out[8 + i : 9 + i, :] = bias_up[:, i * width : (i + 1) * width]

    total = None
    for i, weight in enumerate((wq, wk, wv)):
        at = 0
        for grad in grads:
            end = at + grad.shape[1]
            term = dot(weight[:, at:end], grad[i])
            total = term if total is None else total + term
            at = end
    d_normed = total.T
    unit, rstd = normalized(x[...].astype(F32))
    vec_out[GAIN_ATTN, :] += jnp.sum(d_normed * unit, axis=0, keepdims=True)
    vec_out[SHIFT_ATTN, :] += jnp.sum(d_normed, axis=0, keepdims=True)
    dx_out[...] = (dh[...] + norm_backward(d_normed * row_of(gain), unit, rstd)).astype(BF)


def input_grad(x, gain, dh, wq, wk, wv, grads, sums, begun, after):
    tokens, width = x.shape
    rows = 256
    steps = tokens // rows // 2
    first = steps if begun else 0
    block = pl.BlockSpec((rows, width), lambda i: (i + first, 0))
    inputs = [x, gain, dh, wq, wk, wv, *grads]
    specs = (
        [block, whole(), block]
        + [whole()] * 3
        + [pl.BlockSpec((3, part.shape[1], rows), lambda i: (0, 0, i + first)) for part in grads]
    )
    if begun:
        inputs += [begun[1], begun[0]]
        specs += [whole()] + idle(begun[:1])
    else:
        inputs += sums
        specs += [whole()] * len(sums)
    return pl.pallas_call(
        functools.partial(input_body, groups=len(grads), begun=bool(begun)),
        grid=(steps,),
        in_specs=specs + idle(after),
        out_specs=[block, whole()],
        out_shape=[shape((tokens, width), BF), shape((16, width), F32)],
        input_output_aliases={len(inputs) - 1: 0} if begun else {},
        compiler_params=params(),
        cost_estimate=cost(5),
        name="input_grad",
    )(*inputs, *after)


def swap(value, axis, mask):
    count = lax.axis_size(axis)
    return lax.ppermute(value, axis, [(i, i ^ mask) for i in range(count)])


def swap_seq(value, turn):
    masks = (2, 4) if turn == 0 else (4, 2)
    return lax.ppermute(value, "seq", [(i, i ^ masks[i & 1]) for i in range(8)])


def swap_rep(value, turn):
    pairs = []
    for i in range(8):
        for z in range(4):
            mask = (1, 2)[(i + turn) & 1]
            pairs.append((i * 4 + z, i * 4 + (z ^ mask)))
    return lax.ppermute(value, ("seq", "rep"), pairs)


def total_of(terms):
    result = terms[0].astype(F32)
    for term in terms[1:]:
        result = result + term.astype(F32)
    return result


class Sum:
    def __init__(self, keep, send):
        self.terms, self.send = [keep], send
        self.stage = 0
        self.result = None
        self.flying = []

    def start(self, gate):
        stage, self.stage = self.stage, self.stage + 1
        if stage > 5:
            return []
        if stage:
            got, self.flying = gate(self.flying[0]), []
        if stage == 0:
            send = self.send
            self.flying = [swap(send, "seq", 1)]
        elif stage == 1:
            self.terms.append(got)
            send = total_of([term[1::2] for term in self.terms]).astype(BF)
            self.flying = [swap_seq(send, 0)]
        elif stage == 2:
            send = total_of([term[2] for term in self.terms] + [got[1]]).astype(BF)
            self.terms = [term[0] for term in self.terms + [got]]
            self.flying = [swap_seq(send, 1)]
        elif stage < 5:
            send = total_of(self.terms + [got]).astype(BF)
            self.terms = [send]
            self.flying = [swap_rep(send, stage - 3)]
        else:
            self.result = total_of(self.terms + [got])
            return []
        return [send]


class PlainSum:
    def __init__(self, keep, send, turn=False):
        both = jnp.stack([keep, send], axis=1)
        if turn:
            both = both.swapaxes(2, 3)
        share = lax.psum_scatter(
            both.reshape(-1, both.shape[-1]), "seq", scatter_dimension=0, tiled=True
        )
        self.result = lax.psum(share, "rep").astype(F32)
        self.flying = []

    def start(self, gate):
        return []


class VectorSum:
    def __init__(self, value):
        self.result = value
        self.stage = 0
        self.flying = []

    def start(self, gate):
        stage, self.stage = self.stage, self.stage + 1
        got, self.flying = [gate(array) for array in self.flying], []
        if stage == 0:
            self.flying = [swap(self.result, "seq", 1)]
        elif stage == 1:
            self.result = self.result + got[0]
            self.flying = [swap(self.result, "seq", mask) for mask in (2, 4, 6)]
        elif stage == 2:
            self.result = self.result + (got[0] + got[1] + got[2])
            self.flying = [swap(self.result, "rep", mask) for mask in (1, 2, 3)]
        elif stage == 3:
            self.result = (self.result + got[0]) + (got[1] + got[2])
        return []


def far_back(values, keys, numer, delta, queries, weights, mine, score_scale):
    prob = dot(values, numer) - delta
    d_scores = (weights.astype(F32) * prob).astype(BF)
    dq = jnp.where(mine, dot(keys.T, d_scores), 0.0).astype(BF)
    queries = jnp.where(mine, queries, jnp.zeros_like(queries))
    dk = dot_nt(d_scores, queries) * score_scale
    return dq, jnp.concatenate([dk.astype(BF), dot_nt(weights, numer).astype(BF)], axis=1)


def per_device(
    tokens,
    lengths,
    tile_valid,
    w_query,
    w_key,
    w_value,
    w_out,
    b_query,
    b_value,
    b_out,
    gain_attn,
    shift_attn,
    gain_mlp,
    shift_mlp,
    w_up,
    b_up,
    w_down,
    b_down,
    cotangent,
):
    rows, width = tokens.shape[1:]
    size = width // H
    score_scale = size ** (-0.5)
    scale = score_scale * LOG2E
    devices = lax.axis_size("seq")
    direct = devices == 8 and lax.axis_size("rep") == 4
    me = lax.axis_index("seq")
    seat = (me, jnp.ones_like(me)) if direct else (jnp.zeros_like(me),) * 2
    info = jnp.stack([lengths[0] - me * rows, *seat]).astype(jnp.int32)
    x = tokens[0]
    g = cotangent[0]

    def after(kernel, array):
        return lax.optimization_barrier((array, kernel))[0]

    q, k, v, nt, far = project(
        info, x, gain_attn, shift_attn, w_query, w_key, w_value, b_query, b_value, tile_valid, size
    )
    groups = (4, 12)
    if direct:
        twin = swap(far, "seq", 1)
        early = near(info, q, k, v, tile_valid, scale, 0, groups[0], [])
        pair = jnp.concatenate([far, after(early[2], twin)], axis=0)
        parts = [pair] + [swap(pair, "seq", mask) for mask in (2, 4, 6)]
        late = near(info, q, k, v, tile_valid, scale, groups[0], groups[1], [pair])
    else:
        parts = [lax.all_gather(far, "seq", axis=0, tiled=True)]
        early = near(info, q, k, v, tile_valid, scale, 0, groups[0], [])
        late = near(info, q, k, v, tile_valid, scale, groups[0], groups[1], [])
    numers, peaks = [early[1], late[1]], [early[2], late[2]]
    att, near_fade, far_fade, hidden, n_two, nt_two, e_far = merge(
        q, numers, peaks, x, w_out, b_out, gain_mlp, shift_mlp, parts, scale
    )
    mixed, dn_two, up_keep, up_send, down_keep, down_send, bias_up = feed(
        info, n_two, nt_two, g, w_up, w_down, b_up, hidden, b_down
    )

    def round_of(kernel, *sums):
        return [array for item in sums for array in item.start(lambda a: after(kernel, a))]

    total = Sum if direct else PlainSum
    up = total(up_keep, up_send)
    down = total(down_keep, down_send) if direct else total(down_keep, down_send, True)
    sent = round_of(None, up, down)
    dh, db, dnum, delta, far_num, far_delta, vec_mid = split(
        hidden, dn_two, g, gain_mlp, att, near_fade, far_fade, w_out, sent
    )
    sent = round_of(far_delta, up)
    if direct:
        dq_far, far_keep, far_send = far_kernel(
            q, far_num, far_delta, e_far, parts, score_scale, sent
        )
        far_got = swap(far_send, "seq", 1)
        sent = [far_send]
    else:
        dq_far, far_grad = far_back(
            parts[0][:, width : 2 * width], parts[0][:, :width], far_num, far_delta, q, e_far,
            own_head(width, 0, rows, size), score_scale,
        )
        owned = [lax.psum_scatter(far_grad, "seq", scatter_dimension=0, tiled=True)]
    sent = sent + round_of(dq_far, down)

    def attend(first, count, sent):
        late_part = first >= groups[0]
        weights, skip = (late[0], first - groups[0]) if late_part else (early[0], first)
        return back(
            weights, skip, dnum, delta, q, k, v, dq_far, first, count, score_scale, sent
        )

    def flights(*sums):
        return [array for item in sums for array in item.flying]

    heads = H // 2
    pieces = [attend(0, 4, sent)]
    sent = round_of(pieces[-1], up)
    if direct:
        far_sum = total_of([far_keep, after(pieces[-1], far_got)]).astype(BF)
        owned = [far_sum[0]] + [swap(far_sum[j], "seq", 2 * j) for j in range(1, 4)]
        sent = [far_sum] + sent
    pieces.append(attend(4, 4, sent))
    sent = round_of(pieces[-1], down, up)
    late_pieces = [attend(8, 4, sent)]
    sent = round_of(late_pieces[-1], down)
    grad_a, keep, send, bias_a = weigh(info, nt, pieces, owned, [att, db], 0, sent)
    first_grads = total(keep, send)
    sent = round_of(bias_a, first_grads, up)
    late_pieces.append(attend(12, 4, sent))
    sent = round_of(late_pieces[-1], first_grads, down)
    grad_b, keep, send, bias_b = weigh(info, nt, late_pieces, owned, [], heads * size, sent)
    last_grads = total(keep, send)
    sent = round_of(bias_b, last_grads, first_grads)
    begun = input_grad(
        x, gain_attn, dh, w_query, w_key, w_value, [grad_a, grad_b],
        [bias_a, bias_b, vec_mid, bias_up], None, sent + flights(up),
    )
    sent = round_of(begun[1], last_grads, first_grads)
    dx, vectors = input_grad(
        x, gain_attn, dh, w_query, w_key, w_value, [grad_a, grad_b], [], begun,
        sent + flights(down),
    )
    if direct:
        kernel, vectors = vectors, VectorSum(vectors)
        sums = (last_grads, vectors, first_grads)
        for _ in range(4):
            landed = lax.optimization_barrier((kernel, *flights(*sums)))
            where = {id(old): new for old, new in zip(flights(*sums), landed[1:])}
            if vectors.stage == 0:
                vectors.result = landed[0]
            for item in sums:
                item.start(lambda array: where[id(array)])
            kernel = landed[0]
        round_of(kernel, up, down)
        vectors = vectors.result
    else:
        vectors = lax.psum(vectors, ("seq", "rep"))
    share = width // devices
    mine = lax.dynamic_slice_in_dim(vectors[:8], me * share, share, 1)
    mine_up = lax.dynamic_slice_in_dim(vectors[8:12].reshape(-1), me * 4 * share, 4 * share, 0)
    wide = heads * size
    both = [first_grads.result, last_grads.result]
    qkv = [
        jnp.concatenate([s[:, i * wide : (i + 1) * wide] for s in both], axis=1)
        for i in range(3)
    ]
    grad_down = down.result
    if direct:
        grad_down = grad_down.T
    return (
        mixed[None],
        dx[None],
        qkv[0],
        qkv[1],
        qkv[2],
        first_grads.result[:, 3 * wide :],
        mine[0],
        mine[1],
        mine[2],
        mine[3],
        mine[4],
        mine[5],
        mine[6],
        up.result,
        mine_up,
        grad_down,
        mine[7],
    )


def solution(mesh):
    split_specs = P("rep", "seq", None)
    in_specs = (split_specs, P("rep"), P("rep", "seq")) + (P(),) * 15 + (split_specs,)
    out_specs = (
        (split_specs,) * 2
        + (P("seq", None),) * 4
        + (P("seq"),) * 7
        + (P("seq", None), P("seq"), P("seq", None), P("seq"))
    )
    return jax.shard_map(
        per_device, mesh=mesh, in_specs=in_specs, out_specs=out_specs, check_vma=False
    )
```

```python
import functools

import jax
import jax.numpy as jnp
from jax import lax
from jax.experimental import pallas as pl
from jax.experimental.pallas import tpu as pltpu
from jax.sharding import PartitionSpec as P

H = 16
R = 16
EPS = 1e-05
LOG2E = 1.4426950408889634
NEG = -1e30
BF = jnp.bfloat16
F32 = jnp.float32
PER_STEP = 1
SAFE = 60.0


def row_of(vector):
    return vector[...].reshape(1, -1)


def iota(shape, dim):
    return lax.broadcasted_iota(jnp.int32, shape, dim)


def dot(left, right):
    return jnp.dot(left, right, preferred_element_type=F32)


def dot_nt(left, right):
    return lax.dot_general(left, right, (((1,), (1,)), ((), ())), preferred_element_type=F32)


def params(mega=48):
    return pltpu.CompilerParams(vmem_limit_bytes=mega * 1024 * 1024)


def cost(micros):
    return pl.CostEstimate(flops=int(micros * 1.15e9), bytes_accessed=1024, transcendentals=0)


def whole():
    return pl.BlockSpec(memory_space=pltpu.VMEM)


def idle(arrays):
    return [pl.BlockSpec(memory_space=pl.ANY)] * len(arrays)


def scalars():
    return pl.BlockSpec(memory_space=pltpu.SMEM)


def shape(dims, kind):
    return jax.ShapeDtypeStruct(dims, kind)


def normalized(values):
    center = values - jnp.mean(values, axis=-1, keepdims=True)
    rstd = lax.rsqrt(jnp.mean(center * center, axis=-1, keepdims=True) + EPS)
    return center * rstd, rstd


def norm_backward(grad, unit, rstd):
    return rstd * (
        grad
        - jnp.mean(grad, axis=-1, keepdims=True)
        - unit * jnp.mean(grad * unit, axis=-1, keepdims=True)
    )


def own_head(rows, first_row, columns, size):
    feature = iota((rows, columns), 0) + first_row
    start = (iota((rows, columns), 1) % R) * size
    return (feature >= start) & (feature < start + size)


def group_pick(groups, columns):
    return (iota((groups, columns), 1) // R == iota((groups, columns), 0)).astype(BF)


def place_of(info, j, leaves):
    core = ((info[1] & 1) ^ leaves) & info[2]
    straight, turned = j << 1, ((j & 1) << 2) | (j & 2)
    return info[1] ^ leaves ^ jnp.where(core == 1, turned, straight)


def project_body(
    info, x, gain, shift, wq, wk, wv, bq, bv, valid, q_out, k_out, v_out, n_out, far_out, *, size
):
    rows, width = x.shape
    unit, _ = normalized(x[...].astype(F32))
    normed = (unit * row_of(gain) + row_of(shift)).astype(BF)
    n_out[...] = unit.astype(BF).T
    q_out[...] = (dot(normed, wq[...]) + row_of(bq)).astype(BF).T
    keys = dot(normed, wk[...]).astype(BF)
    values = (dot(normed, wv[...]) + row_of(bv)).astype(BF)
    k_out[...] = keys.T
    v_out[...] = values.T
    feature = iota((rows, width), 1)
    start = (iota((rows, width), 0) % R) * size
    mine = (feature >= start) & (feature < start + size)
    pick = group_pick(rows // R, rows)
    zero = jnp.zeros((rows, width), BF)
    far_out[:, :width] = dot(pick, jnp.where(mine, keys, zero)).astype(BF)
    far_out[:, width : 2 * width] = dot(pick, jnp.where(mine, values, zero)).astype(BF)
    place = iota((1, rows), 1) + pl.program_id(0) * rows
    good = jnp.where((valid[...] > 0) & (place < info[0]), 1.0, 0.0)
    residue = (iota((rows, 128), 0) % R == iota((rows, 128), 1)).astype(BF)
    found = dot((pick.astype(F32) * good).astype(BF), residue)
    far_out[:, 2 * width :] = jnp.where(found > 0.5, 0.0, NEG).astype(BF)


def project(info, x, gain, shift, wq, wk, wv, bq, bv, valid, size):
    tokens, width = x.shape
    rows = 512
    column = pl.BlockSpec((width, rows), lambda i: (0, i))
    return pl.pallas_call(
        functools.partial(project_body, size=size),
        grid=(tokens // rows,),
        in_specs=[scalars(), pl.BlockSpec((rows, width), lambda i: (i, 0))]
        + [whole()] * 7
        + [pl.BlockSpec((1, rows), lambda i: (0, i))],
        out_specs=[column] * 4 + [pl.BlockSpec((rows // R, 2 * width + 128), lambda i: (i, 0))],
        out_shape=[shape((width, tokens), BF)] * 4 + [shape((tokens // R, 2 * width + 128), BF)],
        compiler_params=params(60),
        cost_estimate=cost(10),
        name="project",
    )(info, x, gain, shift, wq, wk, wv, bq, bv, valid)


def near_body(*refs, scale, size):
    (info, q, k, v, valid) = refs[:5]
    (e_out, numer_out, peak_out) = refs[-3:]
    tokens = q.shape[1]
    first = iota((32, tokens), 0) == 0
    good = (valid[...] > 0) & (iota((1, tokens), 1) < info[0])
    mask = jnp.where(first, jnp.where(good, 0.0, NEG), 0.0).astype(BF)
    one = first.astype(BF)
    for i in range(PER_STEP):
        lane = slice(i * size, (i + 1) * size)
        scaled = q[lane, :].astype(F32) * scale
        plain = k[lane, :].astype(F32)
        high = scaled.astype(BF)
        low = (scaled - high.astype(F32)).astype(BF)
        queries = jnp.concatenate([high, low, one], axis=0)
        keys = jnp.concatenate([k[lane, :], k[lane, :], mask], axis=0).T
        values = jnp.concatenate([v[lane, :], one[:16]], axis=0)
        bound = jnp.max(jnp.sum(scaled * scaled, axis=0)) * jnp.max(
            jnp.sum(plain * plain, axis=0)
        )
        safe = bound < SAFE * SAFE

        @pl.when(safe)
        def _():
            weights = jnp.exp2(dot(keys, queries)).astype(BF)
            e_out[i] = weights
            numer_out[i] = dot(values, weights)
            peak_out[i] = jnp.zeros((1, tokens), F32)

        @pl.when(jnp.logical_not(safe))
        def _():
            scores = dot(keys, queries)
            peak = jnp.max(scores, axis=0, keepdims=True)
            weights = jnp.exp2(scores - peak).astype(BF)
            e_out[i] = weights
            numer_out[i] = dot(values, weights)
            peak_out[i] = peak


def near(info, q, k, v, valid, scale, first, count, after):
    width, tokens = q.shape
    size = width // H
    head = pl.BlockSpec((PER_STEP * size, tokens), lambda h: (h + first // PER_STEP, 0))

    def block(rows):
        return pl.BlockSpec((PER_STEP, rows, tokens), lambda h: (h, 0, 0))

    return pl.pallas_call(
        functools.partial(near_body, scale=scale, size=size),
        grid=(count // PER_STEP,),
        in_specs=[scalars()]
        + [head] * 3
        + [pl.BlockSpec((1, tokens), lambda h: (0, 0))]
        + idle(after),
        out_specs=[block(tokens), block(size + 16), block(1)],
        out_shape=[
            shape((count, tokens, tokens), BF),
            shape((count, size + 16, tokens), F32),
            shape((count, 1, tokens), F32),
        ],
        compiler_params=params(60),
        cost_estimate=cost(2 * count),
        name="near",
    )(info, q, k, v, valid, *after)


def merge_body(*refs, scale, pieces, groups, size):
    (q, x, w_out, b_out, gain, shift) = refs[:6]
    parts = refs[6 : 6 + pieces]
    numers = refs[6 + pieces : 6 + pieces + groups]
    peaks = refs[6 + pieces + groups : 6 + pieces + 2 * groups]
    (att_out, near_out, far_out, hidden_out, n_out, nt_out, e_out) = refs[-11:-4]
    keys, values, masks, att = refs[-4:]
    width, rows = q.shape
    heads = [(group, h) for group, ref in enumerate(peaks) for h in range(ref.shape[0])]

    @pl.when(pl.program_id(0) == 0)
    def _():
        first = 0
        for part in parts:
            at = slice(first, first + part.shape[0])
            first = at.stop
            keys[at, :] = part[:, :width]
            values[:, at] = part[:, width : 2 * width].T
            masks[at, :] = part[:, 2 * width :]

    mine = own_head(width, 0, rows, size)
    queries = jnp.where(mine, q[...], jnp.zeros((width, rows), BF))
    residue = (iota((128, rows), 1) % R == iota((128, rows), 0)).astype(BF)
    scores = dot(keys[...], queries) * scale + dot(masks[...], residue)
    far_peak = jnp.max(scores, axis=0, keepdims=True)
    weights = jnp.exp2(scores - far_peak)
    far_denom = jnp.sum(weights, axis=0, keepdims=True)
    weights = weights.astype(BF)
    e_out[...] = weights
    far_numer = dot(values[...], weights)
    place = iota((1, rows), 1) % R
    far_row = jnp.zeros((1, rows), F32)
    for h, (group, at) in enumerate(heads):
        lane = slice(h * size, (h + 1) * size)
        here = place == h
        numer = numers[group]
        near_peak = peaks[group][at]
        top = jnp.maximum(near_peak, jnp.where(here, far_peak, NEG))
        near_fade = jnp.exp2(near_peak - top)
        far_fade = jnp.where(here, jnp.exp2(far_peak - top), 0.0)
        inverse = 1.0 / (near_fade * numer[at, size : size + 1, :] + far_fade * far_denom)
        near_fade = near_fade * inverse
        far_fade = far_fade * inverse
        near_out[h] = near_fade
        far_row = far_row + far_fade
        att[lane, :] = numer[at, :size, :] * near_fade + far_numer[lane, :] * far_fade
    far_out[...] = far_row
    attended = att[...].astype(BF)
    att_out[...] = attended
    hidden = x[...].astype(F32) + dot(attended.T, w_out[...]) + row_of(b_out)
    hidden_out[...] = hidden
    unit, _ = normalized(hidden)
    normed = (unit * row_of(gain) + row_of(shift)).astype(BF)
    n_out[...] = normed
    nt_out[...] = normed.T


def merge(q, numers, peaks, x, w_out, b_out, gain, shift, parts, scale):
    width, tokens = q.shape
    size = width // H
    rows = 512
    far = sum(part.shape[0] for part in parts)
    column = pl.BlockSpec((width, rows), lambda i: (0, i))
    block = pl.BlockSpec((rows, width), lambda i: (i, 0))

    def heads(count, depth):
        return pl.BlockSpec((count, depth, rows), lambda i: (0, 0, i))

    return pl.pallas_call(
        functools.partial(
            merge_body, scale=scale, pieces=len(parts), groups=len(peaks), size=size
        ),
        grid=(tokens // rows,),
        in_specs=[column, block]
        + [whole()] * 4
        + [whole()] * len(parts)
        + [heads(*part.shape[:2]) for part in numers + peaks],
        out_specs=[
            column,
            heads(H, 1),
            pl.BlockSpec((1, rows), lambda i: (0, i)),
            block,
            block,
            column,
            pl.BlockSpec((far, rows), lambda i: (0, i)),
        ],
        out_shape=[
            shape((width, tokens), BF),
            shape((H, 1, tokens), F32),
            shape((1, tokens), F32),
            shape((tokens, width), F32),
            shape((tokens, width), BF),
            shape((width, tokens), BF),
            shape((far, tokens), BF),
        ],
        scratch_shapes=[
            pltpu.VMEM((far, width), BF),
            pltpu.VMEM((width, far), BF),
            pltpu.VMEM((far, 128), BF),
            pltpu.VMEM((width, rows), F32),
        ],
        compiler_params=params(60),
        cost_estimate=cost(13),
        name="merge",
    )(q, x, w_out, b_out, gain, shift, *parts, *numers, *peaks)


def gelu_pair(u):
    size = jnp.abs(u)
    t = pltpu.reciprocal(1.0 + (0.3275911 * 0.7071067811865476) * size, approx=True)
    bell = jnp.exp2(u * u * (-0.5 * LOG2E))
    poly = t * (
        0.5 * 0.254829592
        + t
        * (
            0.5 * -0.284496736
            + t * (0.5 * 1.421413741 + t * (0.5 * -1.453152027 + t * (0.5 * 1.061405429)))
        )
    )
    tail = poly * bell
    phi = jnp.where(u > 0, 1.0 - tail, tail)
    return u * phi, phi + u * bell * 0.3989422804014327


def feed_body(
    info, n, nt, g, w_up, w_down, b_up,
    act, dn_out, up_keep, up_send, down_keep, down_send, bias_out,
    gt, dup, grad, b_up_row, dn, *, blocks,
):
    step = pl.program_id(0)
    tokens, width = n.shape
    wide = w_up.shape[1]
    half = wide // 2

    @pl.when(step == 0)
    def _():
        gt[...] = g[...].T
        b_up_row[...] = row_of(b_up)
        dn[...] = jnp.zeros_like(dn)

    bias = b_up_row[:, pl.ds(pl.multiple_of(step * wide, wide), wide)]
    bias_sum = jnp.zeros((1, wide), F32)
    rows = 256
    for i in range(tokens // rows):
        at = slice(i * rows, (i + 1) * rows)
        upper = dot(n[at, :], w_up[...]) + bias
        value, slope = gelu_pair(upper)
        value = value.astype(BF)
        act[at, :] = value
        d_upper = (dot_nt(g[at, :], w_down[...]) * slope).astype(BF)
        dup[at, :] = d_upper
        bias_sum = bias_sum + jnp.sum(d_upper.astype(F32), axis=0, keepdims=True)
        dn[at, :] += dot_nt(d_upper, w_up[...])
    bias_out[...] = bias_sum
    grad[...] = dot(nt[...], dup[...])
    share = width // blocks
    for j in range(blocks // 2):
        for out, leaves in ((up_keep, 0), (up_send, 1)):
            start = pl.multiple_of(place_of(info, j, leaves) * share, share)
            out[j] = grad[pl.ds(start, share), :].astype(BF)
    for out, leaves in ((down_keep, 0), (down_send, 1)):
        start = pl.multiple_of(((info[1] & 1) ^ leaves) * half, half)
        out[0] = dot(gt[...], act[:, pl.ds(start, half)]).astype(BF)

    @pl.when(step == pl.num_programs(0) - 1)
    def _():
        dn_out[...] = dn[...].astype(BF)


def feed(info, n, nt, g, w_up, w_down, b_up):
    tokens, width = n.shape
    hidden_units = w_up.shape[1]
    blocks = 8
    steps = 4
    wide = hidden_units // steps
    rows = pl.BlockSpec((blocks // 2, width // blocks, wide), lambda c, info: (0, 0, c))

    def pair(leaves):
        def place(c, info):
            chips = c ^ (info[1] >> 1)
            core = ((info[1] & 1) ^ leaves) & info[2]
            return (jnp.where(core == 1, ((chips & 1) << 1) | (chips >> 1), chips), 0, 0)

        return pl.BlockSpec((1, width, wide // 2), place)

    full = pl.BlockSpec(memory_space=pltpu.VMEM)
    return pl.pallas_call(
        functools.partial(feed_body, blocks=blocks),
        grid_spec=pltpu.PrefetchScalarGridSpec(
            num_scalar_prefetch=1,
            grid=(steps,),
            in_specs=[
                full,
                full,
                full,
                pl.BlockSpec((width, wide), lambda c, info: (0, c)),
                pl.BlockSpec((wide, width), lambda c, info: (c, 0)),
                full,
            ],
            out_specs=[pl.BlockSpec((tokens, wide), lambda c, info: (0, c)), full, rows, rows, pair(0), pair(1)]
            + [pl.BlockSpec((1, wide), lambda c, info: (0, c))],
            scratch_shapes=[
                pltpu.VMEM((width, tokens), BF),
                pltpu.VMEM((tokens, wide), BF),
                pltpu.VMEM((width, wide), F32),
                pltpu.VMEM((1, hidden_units), F32),
                pltpu.VMEM((tokens, width), F32),
            ],
        ),
        out_shape=[
            shape((tokens, hidden_units), BF),
            shape((tokens, width), BF),
            shape((blocks // 2, width // blocks, hidden_units), BF),
            shape((blocks // 2, width // blocks, hidden_units), BF),
            shape((blocks // 2, width, hidden_units // blocks), BF),
            shape((blocks // 2, width, hidden_units // blocks), BF),
            shape((1, hidden_units), F32),
        ],
        compiler_params=params(60),
        cost_estimate=cost(46),
        name="feed",
    )(info, n, nt, g, w_up, w_down, b_up)


def lower_body(act, w_down, hidden, b_down, *refs):
    refs[-1][...] = (dot(act[...], w_down[...]) + hidden[...] + row_of(b_down)).astype(BF)


def lower(act, w_down, hidden, b_down, after):
    tokens, hidden_units = act.shape
    width = w_down.shape[1]
    rows = 256
    block = pl.BlockSpec((rows, width), lambda i: (i, 0))
    return pl.pallas_call(
        lower_body,
        grid=(tokens // rows,),
        in_specs=[pl.BlockSpec((rows, hidden_units), lambda i: (i, 0)), whole(), block, whole()]
        + idle(after),
        out_specs=block,
        out_shape=shape((tokens, width), BF),
        compiler_params=params(),
        cost_estimate=cost(7),
        name="lower",
    )(act, w_down, hidden, b_down, *after)


def split_body(*refs, size):
    (hidden, dn, g, gain, att, near_fade, far_fade, w_out) = refs[:8]
    (db_out, dnum_out, delta_out, far_num, far_delta_out, vec_out) = refs[-6:]
    width, rows = att.shape

    @pl.when(pl.program_id(0) == 0)
    def _():
        vec_out[...] = jnp.zeros_like(vec_out)

    unit, rstd = normalized(hidden[...])
    d_normed = dn[...].astype(F32)
    upstream = g[...].astype(F32)
    d_hidden = upstream + norm_backward(d_normed * row_of(gain), unit, rstd)
    d_branch = d_hidden.astype(BF)
    db_out[...] = d_branch
    vec_out[0:1, :] += jnp.sum(d_branch.astype(F32), axis=0, keepdims=True)
    vec_out[1:2, :] += jnp.sum(d_normed * unit, axis=0, keepdims=True)
    vec_out[2:3, :] += jnp.sum(d_normed, axis=0, keepdims=True)
    vec_out[3:4, :] += jnp.sum(upstream, axis=0, keepdims=True)
    d_att = dot_nt(w_out[...], d_branch).astype(BF).astype(F32)
    product = d_att * att[...].astype(F32)
    place = iota((1, rows), 1) % R
    far_delta = jnp.zeros((1, rows), F32)
    for h in range(H):
        lane = slice(h * size, (h + 1) * size)
        total = jnp.sum(product[lane, :], axis=0, keepdims=True)
        fade = near_fade[h]
        far = jnp.where(place == h, far_fade[...], 0.0)
        dnum_out[lane, :] = (d_att[lane, :] * fade).astype(BF)
        far_num[lane, :] = (d_att[lane, :] * far).astype(BF)
        delta_out[h] = -total * fade
        far_delta = far_delta + total * far
    far_delta_out[...] = far_delta


def split(hidden, dn, g, gain, att, near_fade, far_fade, w_out, after):
    width, tokens = att.shape
    rows = 512
    column = pl.BlockSpec((width, rows), lambda i: (0, i))
    block = pl.BlockSpec((rows, width), lambda i: (i, 0))
    heads = pl.BlockSpec((H, 1, rows), lambda i: (0, 0, i))
    row = pl.BlockSpec((1, rows), lambda i: (0, i))
    return pl.pallas_call(
        functools.partial(split_body, size=width // H),
        grid=(tokens // rows,),
        in_specs=[block, block, block, whole(), column, heads, row, whole()] + idle(after),
        out_specs=[block, column, heads, column, row, whole()],
        out_shape=[
            shape((tokens, width), BF),
            shape((width, tokens), BF),
            shape((H, 1, tokens), F32),
            shape((width, tokens), BF),
            shape((1, tokens), F32),
            shape((8, width), F32),
        ],
        compiler_params=params(),
        cost_estimate=cost(9),
        name="split",
    )(hidden, dn, g, gain, att, near_fade, far_fade, w_out, *after)


def far_body(*refs, pieces, size, score_scale, blocks):
    (q, numer, delta, e) = refs[:4]
    parts = refs[4 : 4 + pieces]
    (dq_out, keep, send, keys, values, grad) = refs[-6:]
    width, tokens = q.shape
    first = 0
    for part in parts:
        at = slice(first, first + part.shape[0])
        first = at.stop
        keys[:, at] = part[:, :width].T
        values[at, :] = part[:, width : 2 * width]
    share = first // blocks
    mine = own_head(width, 0, tokens, size)
    queries = jnp.where(mine, q[...], jnp.zeros((width, tokens), BF))
    weights = e[...]
    prob = dot(values[...], numer[...]) - delta[...]
    d_scores = (weights.astype(F32) * prob).astype(BF)
    dq_out[...] = jnp.where(mine, dot(keys[...], d_scores), 0.0).astype(BF)
    for lane, left, right, factor in (
        (slice(0, width), d_scores, queries, score_scale),
        (slice(width, 2 * width), weights, numer[...], 1.0),
    ):
        grad[...] = dot_nt(left, right) * factor
        for j in range(blocks):
            out = (keep, send)[j % 2]
            out[j // 2, :, lane] = grad[j * share : (j + 1) * share, :].astype(BF)


def far_kernel(q, numer, delta, e, parts, score_scale, after):
    width, tokens = q.shape
    far = e.shape[0]
    blocks = 8
    grads = shape((blocks // 2, far // blocks, 2 * width), BF)
    return pl.pallas_call(
        functools.partial(
            far_body, pieces=len(parts), size=width // H, score_scale=score_scale, blocks=blocks
        ),
        in_specs=[whole()] * (4 + len(parts)) + idle(after),
        out_specs=[whole()] * 3,
        out_shape=[shape((width, tokens), BF), grads, grads],
        scratch_shapes=[
            pltpu.VMEM((width, far), BF),
            pltpu.VMEM((far, width), BF),
            pltpu.VMEM((far, width), F32),
        ],
        compiler_params=params(),
        cost_estimate=cost(9),
        name="far",
    )(q, numer, delta, e, *parts, *after)


def back_body(*refs, size, score_scale):
    (e, dnum, delta, q, k, v, dq_far) = refs[:7]
    (out, scores) = refs[-2:]
    tokens = q.shape[1]
    at = iota((16, tokens), 0)
    blank = jnp.zeros((64, tokens), BF)
    ones = (at < 3).astype(BF)
    probs = []
    for i in range(PER_STEP):
        lane = slice(i * size, (i + 1) * size)
        low = delta[i]
        terms = []
        for _ in range(3):
            term = low.astype(BF).astype(F32)
            terms.append(term)
            low = low - term
        extra = jnp.where(
            at == 0, terms[0], jnp.where(at == 1, terms[1], jnp.where(at == 2, terms[2], 0.0))
        ).astype(BF)
        numer = jnp.concatenate([dnum[lane, :], extra, blank], axis=0)
        values = jnp.concatenate([v[lane, :], ones, blank], axis=0).T
        scores[i] = (e[i].astype(F32) * dot(values, numer)).astype(BF)
    for i in range(PER_STEP):
        lane = slice(i * size, (i + 1) * size)
        d_scores = scores[i]
        near_part = dot(k[lane, :], d_scores)
        out[0, lane, :] = ((near_part + dq_far[lane, :].astype(F32)) * score_scale).astype(BF)
        out[1, lane, :] = (dot_nt(q[lane, :], d_scores) * score_scale).astype(BF)
        out[2, lane, :] = dot_nt(dnum[lane, :], e[i]).astype(BF)


def back(e, skip, dnum, delta, q, k, v, dq_far, first, count, score_scale, after):
    width, tokens = q.shape
    size = width // H
    wide = PER_STEP * size
    start, skip = first // PER_STEP, skip // PER_STEP
    head = pl.BlockSpec((wide, tokens), lambda h: (h + start, 0))
    return pl.pallas_call(
        functools.partial(back_body, size=size, score_scale=score_scale),
        grid=(count // PER_STEP,),
        in_specs=[
            pl.BlockSpec((PER_STEP, tokens, tokens), lambda h: (h + skip, 0, 0)),
            head,
            pl.BlockSpec((PER_STEP, 1, tokens), lambda h: (h + start, 0, 0)),
            head,
            head,
            head,
            head,
        ]
        + idle(after),
        out_specs=pl.BlockSpec((3, wide, tokens), lambda h: (0, h, 0)),
        out_shape=shape((3, count * size, tokens), BF),
        scratch_shapes=[pltpu.VMEM((PER_STEP, tokens, tokens), BF)],
        compiler_params=params(),
        cost_estimate=cost(2.3 * count),
        name="back",
    )(e, dnum, delta, q, k, v, dq_far, *after)


def weigh_body(*refs, pieces, groups, extra, size, first_row, blocks):
    (info, nt) = refs[:2]
    grads = refs[2 : 2 + groups]
    parts = refs[2 + groups : 2 + groups + pieces]
    others = refs[2 + groups + pieces : 2 + groups + pieces + extra]
    (d_out, keep, send, acc, lines) = refs[-5:]
    rows, tokens = d_out.shape[1:]
    width = nt.shape[0]
    step = pl.program_id(0)

    @pl.when(step == 0)
    def _():
        lines[...] = jnp.zeros_like(lines)
        at = 0
        for part in grads:
            d_out[0, at : at + part.shape[1], :] = part[0]
            at = at + part.shape[1]

    @pl.when((step == 1) | (step == 2))
    def _():
        total = parts[0][...].astype(F32)
        for part in parts[1:]:
            total = total + part[...].astype(F32)
        spread = jnp.where(
            own_head(rows, first_row, tokens, size),
            dot(total.astype(BF).T, group_pick(tokens // R, tokens)),
            0.0,
        )
        at = 0
        for part in grads:
            end = at + part.shape[1]
            d_out[0, at:end, :] = (part[0].astype(F32) + spread[at:end, :]).astype(BF)
            at = end

    @pl.when(step < 3)
    def _():
        value = d_out[0]
        lines[0:8, :] = jnp.where(
            iota((8, rows), 0) == 0, dot_nt(jnp.ones((8, tokens), BF), value), 0.0
        )
        acc[...] = dot_nt(nt[...], value)

    if extra:
        (att, db, vec_mid, bias_up) = others

        @pl.when(step >= 3)
        def _():
            acc[...] = dot(att[...], db[...])

        for half in range(width // rows):

            @pl.when(step == 3 + half)
            def _():
                lines[0:4, :] = vec_mid[0:4, half * rows : (half + 1) * rows]
                for i in range(bias_up.shape[1] // width):
                    start = i * width + half * rows
                    lines[4 + i : 5 + i, :] = bias_up[:, start : start + rows]

    share = width // blocks
    for j in range(blocks // 2):
        for out, leaves in ((keep, 0), (send, 1)):
            start = pl.multiple_of(place_of(info, j, leaves) * share, share)
            out[j, :share, :] = acc[pl.ds(start, share), :].astype(BF)
            out[j, share:, :] = lines[...].astype(BF)


def weigh(info, nt, grads, parts, extra, first_row, after):
    width, tokens = nt.shape
    rows = sum(part.shape[1] for part in grads)
    blocks = 8
    steps = 3 + (width // rows if extra else 0)
    column = first_row // rows
    lanes = width // rows
    kind = lambda i: jnp.minimum(i, 2)
    depth = width // blocks + 16
    sums = shape((blocks // 2, depth, steps * rows), BF)
    sums_spec = pl.BlockSpec((blocks // 2, depth, rows), lambda i: (0, 0, i))
    return pl.pallas_call(
        functools.partial(
            weigh_body,
            pieces=len(parts),
            groups=len(grads),
            extra=len(extra),
            size=width // H,
            first_row=first_row,
            blocks=blocks,
        ),
        grid=(steps,),
        in_specs=[scalars(), whole()]
        + [pl.BlockSpec((1, part.shape[1], tokens), lambda i: (kind(i), 0, 0)) for part in grads]
        + [
            pl.BlockSpec(
                (part.shape[0], rows), lambda i: (0, column + lanes * (kind(i) // 2))
            )
            for part in parts
        ]
        + (
            [whole(), pl.BlockSpec((tokens, rows), lambda i: (0, jnp.maximum(i - 3, 0)))]
            + [whole()] * 2
            if extra
            else []
        )
        + idle(after),
        out_specs=[
            pl.BlockSpec((1, rows, tokens), lambda i: (kind(i), 0, 0)),
            sums_spec,
            sums_spec,
        ],
        out_shape=[shape((3, rows, tokens), BF), sums, sums],
        scratch_shapes=[pltpu.VMEM((width, rows), F32), pltpu.VMEM((16, rows), F32)],
        compiler_params=params(),
        cost_estimate=cost(2.2 * steps),
        name="weigh",
    )(info, nt, *grads, *parts, *extra, *after)


def input_body(*refs, groups):
    (x, gain, dh, wq, wk, wv) = refs[:6]
    grads = refs[6 : 6 + groups]
    dx_out = refs[-1]
    total = None
    for i, weight in enumerate((wq, wk, wv)):
        at = 0
        for grad in grads:
            end = at + grad.shape[1]
            term = dot(weight[:, at:end], grad[i])
            total = term if total is None else total + term
            at = end
    d_normed = total.T
    unit, rstd = normalized(x[...].astype(F32))
    dx_out[...] = (dh[...].astype(F32) + norm_backward(d_normed * row_of(gain), unit, rstd)).astype(BF)


def input_grad(x, gain, dh, wq, wk, wv, grads, begun, after):
    tokens, width = x.shape
    rows = 256
    first = 1 if begun else 0
    steps = tokens // rows - 1 if begun else 1
    block = pl.BlockSpec((rows, width), lambda i: (i + first, 0))
    inputs = [x, gain, dh, wq, wk, wv, *grads, *begun]
    specs = (
        [block, whole(), block]
        + [whole()] * 3
        + [pl.BlockSpec((3, part.shape[1], rows), lambda i: (0, 0, i + first)) for part in grads]
        + idle(begun)
    )
    return pl.pallas_call(
        functools.partial(input_body, groups=len(grads)),
        grid=(steps,),
        in_specs=specs + idle(after),
        out_specs=block,
        out_shape=shape((tokens, width), BF),
        input_output_aliases={len(inputs) - 1: 0} if begun else {},
        compiler_params=params(),
        cost_estimate=cost(3 * steps),
        name="input_grad",
    )(*inputs, *after)


def affine_grads(grads, sums, weights, gain, shift):
    w_grads, d_gain, d_shift = [], 0.0, 0.0
    for grad, line, weight in zip(grads, sums, weights):
        weight = weight.astype(F32)
        w_grads.append(gain * grad + shift * line)
        d_gain = d_gain + jnp.sum(weight * grad, axis=1, keepdims=True)
        d_shift = d_shift + jnp.sum(weight * line, axis=1, keepdims=True)
    return w_grads, d_gain, d_shift


def finish_body(info, f_own, f_got, l_own, l_got, gain, shift, *refs):
    weights, (q_out, k_out, v_out, w_out), vec_outs, lines = refs[:3], refs[3:7], refs[7:-1], refs[-1]
    rows, width = q_out.shape
    half = width // 2
    first = f_own[...].astype(F32) + f_got[...].astype(F32)
    last = l_own[...].astype(F32) + l_got[...].astype(F32)
    grads = [
        jnp.concatenate([part[:, i * half : (i + 1) * half] for part in (first, last)], axis=1)
        for i in range(3)
    ]
    sums = [grad[rows : rows + 1, :] for grad in grads]
    grads = [grad[:rows, :] for grad in grads]
    w_out[...] = first[:rows, 3 * half :]
    here = iota((rows, width), 1) == iota((rows, width), 0) + info[1] * rows
    columns = [
        jnp.sum(jnp.where(here, row_of(line), 0.0), axis=1, keepdims=True) for line in (gain, shift)
    ]
    w_grads, d_gain, d_shift = affine_grads(grads, sums, [w[...] for w in weights], *columns)
    for out, grad in zip((q_out, k_out, v_out), w_grads):
        out[...] = grad
    (b_query, b_value, b_out, d_gain_out, d_shift_out, gain_mlp, shift_mlp, b_down, b_up) = vec_outs
    eye = iota((rows, rows), 0) == iota((rows, rows), 1)
    for out, column in ((d_gain_out, d_gain), (d_shift_out, d_shift)):
        out[...] = jnp.sum(jnp.where(eye, column, 0.0), axis=0, keepdims=True).reshape(rows)
    lines[0:8, :] = first[rows : rows + 8, 3 * half :]
    lines[8:9, :] = sums[0]
    lines[9:10, :] = sums[2]
    turn = (width - info[1] * rows) % width
    turned = pltpu.roll(lines[...], turn, 1)
    for out, i in (
        (b_out, 0), (gain_mlp, 1), (shift_mlp, 2), (b_down, 3), (b_query, 8), (b_value, 9)
    ):
        out[...] = turned[i : i + 1, :rows].reshape(rows)
    wide = b_up.shape[0]
    line = lines[pl.ds(4 + info[1] * wide // width, 1), :]
    line = jnp.where(info[1] * wide % width == 0, line[:, :wide], line[:, width - wide :])
    b_up[...] = line.reshape(wide)


def finish(info, first, last, gain, shift, weights, hidden_units):
    width = weights[0].shape[0]
    rows = first[0].shape[0] - 16
    full = pl.BlockSpec(memory_space=pltpu.VMEM)
    mine = pl.BlockSpec((rows, width), lambda i, info: (info[1], 0))
    return pl.pallas_call(
        finish_body,
        grid_spec=pltpu.PrefetchScalarGridSpec(
            num_scalar_prefetch=1,
            grid=(1,),
            in_specs=[full] * 6 + [mine] * 3,
            out_specs=[full] * 13,
            scratch_shapes=[pltpu.VMEM((16, width), F32)],
        ),
        out_shape=[shape((rows, width), F32)] * 4
        + [shape((rows,), F32)] * 8
        + [shape((hidden_units * rows // width,), F32)],
        compiler_params=params(),
        cost_estimate=cost(3),
        name="finish",
    )(info, *first, *last, gain, shift, *weights)


def finish_feed_body(u_own, u_got, d_own, d_got, up, down):
    up[...] = u_own[...].astype(F32) + u_got[...].astype(F32)
    down[...] = (d_own[...].astype(F32) + d_got[...].astype(F32)).T


def finish_feed(up, down):
    return pl.pallas_call(
        finish_feed_body,
        in_specs=[whole()] * 4,
        out_specs=[whole()] * 2,
        out_shape=[shape(up[0].shape, F32), shape(down[0].shape[::-1], F32)],
        compiler_params=params(),
        cost_estimate=cost(3),
        name="finish_feed",
    )(*up, *down)


def swap(value, axis, mask):
    count = lax.axis_size(axis)
    return lax.ppermute(value, axis, [(i, i ^ mask) for i in range(count)])


def swap_seq(value, turn):
    masks = (2, 4) if turn == 0 else (4, 2)
    return lax.ppermute(value, "seq", [(i, i ^ masks[i & 1]) for i in range(8)])


def swap_rep(value, turn):
    pairs = []
    for i in range(8):
        for z in range(4):
            mask = (1, 2)[(i + turn) & 1]
            pairs.append((i * 4 + z, i * 4 + (z ^ mask)))
    return lax.ppermute(value, ("seq", "rep"), pairs)


def total_of(terms):
    result = terms[0].astype(F32)
    for term in terms[1:]:
        result = result + term.astype(F32)
    return result


class Sum:
    def __init__(self, keep, send, straight=False):
        self.terms, self.send = [keep], send
        self.straight = straight
        self.stage = 0
        self.flying = []

    def start(self, gate):
        stage, self.stage = self.stage, self.stage + 1
        if stage > 5:
            return []
        if stage:
            got, self.flying = [gate(array) for array in self.flying], []
        if stage == 0:
            send = self.send
            self.flying = [swap(send, "seq", 1)]
        elif stage == 1:
            self.terms.append(got[0])
            if self.straight:
                send = total_of([term[1:] for term in self.terms]).astype(BF)
                self.flying = [
                    swap_seq(send[0], 0), swap_seq(send[1], 1), swap(send[2], "seq", 6)
                ]
                self.terms = [term[0] for term in self.terms]
                self.stage = 3
            else:
                send = total_of([term[1::2] for term in self.terms]).astype(BF)
                self.flying = [swap_seq(send, 0)]
        elif stage == 2:
            send = total_of([term[2] for term in self.terms] + [got[0][1]]).astype(BF)
            self.terms = [term[0] for term in self.terms + got]
            self.flying = [swap_seq(send, 1)]
        elif stage < 5:
            send = total_of(self.terms + got).astype(BF)
            self.terms = [send]
            self.flying = [swap_rep(send, stage - 3)]
        else:
            self.terms = self.terms + got
            return []
        return [send]


def plain_sum(value):
    share = lax.psum_scatter(value, "seq", scatter_dimension=0, tiled=True)
    return lax.psum(share, "rep").astype(F32)


def in_order(keep, send):
    both = jnp.stack([keep, send], axis=1)
    return both.reshape(-1, *both.shape[2:])


def far_back(values, keys, numer, delta, queries, weights, mine, score_scale):
    prob = dot(values, numer) - delta
    d_scores = (weights.astype(F32) * prob).astype(BF)
    dq = jnp.where(mine, dot(keys.T, d_scores), 0.0).astype(BF)
    queries = jnp.where(mine, queries, jnp.zeros_like(queries))
    dk = dot_nt(d_scores, queries) * score_scale
    return dq, jnp.concatenate([dk.astype(BF), dot_nt(weights, numer).astype(BF)], axis=1)


def per_device(
    tokens,
    lengths,
    tile_valid,
    w_query,
    w_key,
    w_value,
    w_out,
    b_query,
    b_value,
    b_out,
    gain_attn,
    shift_attn,
    gain_mlp,
    shift_mlp,
    w_up,
    b_up,
    w_down,
    b_down,
    cotangent,
):
    rows, width = tokens.shape[1:]
    size = width // H
    score_scale = size ** (-0.5)
    scale = score_scale * LOG2E
    devices = lax.axis_size("seq")
    direct = devices == 8 and lax.axis_size("rep") == 4
    me = lax.axis_index("seq")
    seat = (me, jnp.ones_like(me)) if direct else (jnp.zeros_like(me),) * 2
    info = jnp.stack([lengths[0] - me * rows, *seat]).astype(jnp.int32)
    x = tokens[0]
    g = cotangent[0]

    def after(kernel, array):
        return lax.optimization_barrier((array, kernel))[0]

    q, k, v, nt, far = project(
        info, x, gain_attn, shift_attn, w_query, w_key, w_value, b_query, b_value, tile_valid, size
    )
    groups = (4, 12)
    if direct:
        twin = swap(far, "seq", 1)
        early = near(info, q, k, v, tile_valid, scale, 0, groups[0], [])
        pair = jnp.concatenate([far, after(early[2], twin)], axis=0)
        parts = [pair] + [swap(pair, "seq", mask) for mask in (2, 4, 6)]
        late = near(info, q, k, v, tile_valid, scale, groups[0], groups[1], [pair])
    else:
        parts = [lax.all_gather(far, "seq", axis=0, tiled=True)]
        early = near(info, q, k, v, tile_valid, scale, 0, groups[0], [])
        late = near(info, q, k, v, tile_valid, scale, groups[0], groups[1], [])
    numers, peaks = [early[1], late[1]], [early[2], late[2]]
    att, near_fade, far_fade, hidden, n_two, nt_two, e_far = merge(
        q, numers, peaks, x, w_out, b_out, gain_mlp, shift_mlp, parts, scale
    )
    act, dn_two, up_keep, up_send, down_keep, down_send, bias_up = feed(
        info, n_two, nt_two, g, w_up, w_down, b_up
    )
    weights = (w_query, w_key, w_value)
    heads = H // 2

    def attend(first, sent):
        late_part = first >= groups[0]
        skip = first - groups[0] if late_part else first
        return back(
            (late if late_part else early)[0], skip, dnum, delta, q, k, v, dq_far, first, heads // 2,
            score_scale, sent,
        )

    def weigh_half(grads, extra, first, sent):
        return weigh(info, nt, grads, owned, extra, first * size, sent)

    if not direct:
        share = width // 8
        grad_up = plain_sum(in_order(up_keep, up_send).reshape(width, -1))
        grad_down = plain_sum(in_order(down_keep, down_send).swapaxes(1, 2).reshape(-1, width))
        db, dnum, delta, far_num, far_delta, vec_mid = split(
            hidden, dn_two, g, gain_mlp, att, near_fade, far_fade, w_out, []
        )
        dq_far, far_grad = far_back(
            parts[0][:, width : 2 * width], parts[0][:, :width], far_num, far_delta, q, e_far,
            own_head(width, 0, rows, size), score_scale,
        )
        owned = [lax.psum_scatter(far_grad, "seq", scatter_dimension=0, tiled=True)]
        pieces = [attend(first, []) for first in range(0, H, heads // 2)]
        grads, sums, lines = [], [], []
        for i, extra in enumerate(([att, db, vec_mid, bias_up], [])):
            grad, keep, send = weigh_half(pieces[2 * i : 2 * i + 2], extra, i * heads, [])
            grads.append(grad)
            both = in_order(keep, send)
            sums.append(plain_sum(both[:, :share].reshape(width, -1)))
            lines.append(lax.psum(both[0, share:].astype(F32), ("seq", "rep")))
        begun = input_grad(x, gain_attn, db, *weights, grads, [], [])
        dx = input_grad(x, gain_attn, db, *weights, grads, [begun], [])
        mixed = lower(act, w_down, hidden, b_down, [])
        wide = heads * size
        own = width // devices
        mine = lambda v, count=own: lax.dynamic_slice_in_dim(v, me * count, count, 0)
        triple = lambda pair: [
            jnp.concatenate([part[:, i * wide : (i + 1) * wide] for part in pair], axis=1)
            for i in range(3)
        ]
        totals = [line[0] for line in triple(lines)]
        qkv, d_gain, d_shift = affine_grads(
            triple(sums),
            totals,
            [mine(w) for w in weights],
            mine(gain_attn)[:, None],
            mine(shift_attn)[:, None],
        )
        grad_out, lines = sums[0][:, 3 * wide :], lines[0][:, 3 * wide :]
        vectors = [
            mine(totals[0]), mine(totals[2]), mine(lines[0]), d_gain[:, 0], d_shift[:, 0],
            mine(lines[1]), mine(lines[2]), mine(lines[3]),
            mine(lines[4:8].reshape(-1), own * w_up.shape[1] // width),
        ]
    else:

        def round_of(kernel, *sums, landing=()):
            flying = flights(*sums, *landing)
            landed = lax.optimization_barrier((kernel, *flying))[1:] if flying else []
            where = {id(old): new for old, new in zip(flying, landed)}
            for item in landing:
                item.flying = [where[id(array)] for array in item.flying]
            return [array for item in sums for array in item.start(lambda a: where[id(a)])]

        def flights(*sums):
            return [array for item in sums for array in item.flying]

        up, down = Sum(up_keep, up_send), Sum(down_keep, down_send)
        sent = round_of(None, up, down)
        db, dnum, delta, far_num, far_delta, vec_mid = split(
            hidden, dn_two, g, gain_mlp, att, near_fade, far_fade, w_out, sent
        )
        dq_far, far_keep, far_send = far_kernel(
            q, far_num, far_delta, e_far, parts, score_scale, round_of(far_delta, up)
        )
        far_got = swap(far_send, "seq", 1)
        pieces = [attend(0, [far_send] + round_of(dq_far, down))]
        sent = round_of(pieces[-1], up)
        far_sum = total_of([far_keep, after(pieces[-1], far_got)]).astype(BF)
        owned = [far_sum[0]] + [swap(far_sum[j], "seq", 2 * j) for j in range(1, 4)]
        pieces.append(attend(4, [far_sum] + sent))
        sent = round_of(pieces[-1], down, up)
        grad_a, keep, send = weigh_half(pieces, [att, db, vec_mid, bias_up], 0, sent)
        first_grads = Sum(keep, send)
        sent = round_of(grad_a, first_grads, down, landing=[up])
        pieces = [attend(8, sent + flights(up))]
        pieces.append(attend(12, round_of(pieces[-1], first_grads, up)))
        sent = round_of(pieces[-1], first_grads, down)
        grad_b, keep, send = weigh_half(pieces, [], heads, sent)
        last_grads = Sum(keep, send, True)
        sent = round_of(grad_b, last_grads, first_grads, landing=[up])
        begun = input_grad(
            x, gain_attn, db, *weights, [grad_a, grad_b], [], sent + flights(up)
        )
        sent = round_of(begun, last_grads)
        dx = input_grad(x, gain_attn, db, *weights, [grad_a, grad_b], [begun], sent)
        sent = round_of(dx, last_grads, first_grads, landing=[down])
        mixed = lower(after(dx, act), w_down, hidden, b_down, sent + flights(down))
        round_of(mixed, last_grads, first_grads, up, down)
        round_of(mixed, last_grads)
        grad_up, grad_down = finish_feed(up.terms, down.terms)
        *qkv, grad_out, b_q, b_v, b_o, d_gain, d_shift, g_m, s_m, b_d, b_u = finish(
            info, first_grads.terms, last_grads.terms, gain_attn, shift_attn, weights,
            w_up.shape[1],
        )
        vectors = [b_q, b_v, b_o, d_gain, d_shift, g_m, s_m, b_d, b_u]
    *vectors, bias_up, bias_down = vectors[:7] + [vectors[8], vectors[7]]
    return (mixed[None], dx[None], *qkv, grad_out, *vectors, grad_up, bias_up, grad_down, bias_down)


def solution(mesh):
    split_specs = P("rep", "seq", None)
    in_specs = (split_specs, P("rep"), P("rep", "seq")) + (P(),) * 15 + (split_specs,)
    out_specs = (
        (split_specs,) * 2
        + (P("seq", None),) * 4
        + (P("seq"),) * 7
        + (P("seq", None), P("seq"), P("seq", None), P("seq"))
    )
    return jax.shard_map(
        per_device, mesh=mesh, in_specs=in_specs, out_specs=out_specs, check_vma=False
    )
```

```python
import functools

import jax
import jax.numpy as jnp
from jax import lax
from jax.experimental import pallas as pl
from jax.experimental.pallas import tpu as pltpu
from jax.sharding import PartitionSpec as P

H = 16
R = 16
EPS = 1e-05
LOG2E = 1.4426950408889634
NEG = -1e30
BF = jnp.bfloat16
F32 = jnp.float32
PER_STEP = 1
SAFE = 60.0


def row_of(vector):
    return vector[...].reshape(1, -1)


def iota(shape, dim):
    return lax.broadcasted_iota(jnp.int32, shape, dim)


def dot(left, right):
    return jnp.dot(left, right, preferred_element_type=F32)


def dot_nt(left, right):
    return lax.dot_general(left, right, (((1,), (1,)), ((), ())), preferred_element_type=F32)


def params(mega=48):
    return pltpu.CompilerParams(vmem_limit_bytes=mega * 1024 * 1024)


def cost(micros):
    return pl.CostEstimate(flops=int(micros * 1.15e9), bytes_accessed=1024, transcendentals=0)


def whole():
    return pl.BlockSpec(memory_space=pltpu.VMEM)


def idle(arrays):
    return [pl.BlockSpec(memory_space=pl.ANY)] * len(arrays)


def scalars():
    return pl.BlockSpec(memory_space=pltpu.SMEM)


def shape(dims, kind):
    return jax.ShapeDtypeStruct(dims, kind)


def normalized(values):
    center = values - jnp.mean(values, axis=-1, keepdims=True)
    rstd = lax.rsqrt(jnp.mean(center * center, axis=-1, keepdims=True) + EPS)
    return center * rstd, rstd


def norm_backward(grad, unit, rstd):
    return rstd * (
        grad
        - jnp.mean(grad, axis=-1, keepdims=True)
        - unit * jnp.mean(grad * unit, axis=-1, keepdims=True)
    )


def own_head(rows, first_row, columns, size):
    feature = iota((rows, columns), 0) + first_row
    start = (iota((rows, columns), 1) % R) * size
    return (feature >= start) & (feature < start + size)


def group_pick(groups, columns):
    return (iota((groups, columns), 1) // R == iota((groups, columns), 0)).astype(BF)


def place_of(info, j, leaves):
    core = ((info[1] & 1) ^ leaves) & info[2]
    straight, turned = j << 1, ((j & 1) << 2) | (j & 2)
    return info[1] ^ leaves ^ jnp.where(core == 1, turned, straight)


def project_body(
    info, x, gain, shift, wq, wk, wv, bq, bv, valid, q_out, k_out, v_out, n_out, far_out, *, size
):
    rows, width = x.shape
    unit, _ = normalized(x[...].astype(F32))
    normed = (unit * row_of(gain) + row_of(shift)).astype(BF)
    n_out[...] = unit.astype(BF).T
    q_out[...] = (dot(normed, wq[...]) + row_of(bq)).astype(BF).T
    keys = dot(normed, wk[...]).astype(BF)
    values = (dot(normed, wv[...]) + row_of(bv)).astype(BF)
    k_out[...] = keys.T
    v_out[...] = values.T
    feature = iota((rows, width), 1)
    start = (iota((rows, width), 0) % R) * size
    mine = (feature >= start) & (feature < start + size)
    pick = group_pick(rows // R, rows)
    zero = jnp.zeros((rows, width), BF)
    far_out[:, :width] = dot(pick, jnp.where(mine, keys, zero)).astype(BF)
    far_out[:, width : 2 * width] = dot(pick, jnp.where(mine, values, zero)).astype(BF)
    place = iota((1, rows), 1) + pl.program_id(0) * rows
    good = jnp.where((valid[...] > 0) & (place < info[0]), 1.0, 0.0)
    residue = (iota((rows, 128), 0) % R == iota((rows, 128), 1)).astype(BF)
    found = dot((pick.astype(F32) * good).astype(BF), residue)
    far_out[:, 2 * width :] = jnp.where(found > 0.5, 0.0, NEG).astype(BF)


def project(info, x, gain, shift, wq, wk, wv, bq, bv, valid, size):
    tokens, width = x.shape
    rows = 512
    column = pl.BlockSpec((width, rows), lambda i: (0, i))
    return pl.pallas_call(
        functools.partial(project_body, size=size),
        grid=(tokens // rows,),
        in_specs=[scalars(), pl.BlockSpec((rows, width), lambda i: (i, 0))]
        + [whole()] * 7
        + [pl.BlockSpec((1, rows), lambda i: (0, i))],
        out_specs=[column] * 4 + [pl.BlockSpec((rows // R, 2 * width + 128), lambda i: (i, 0))],
        out_shape=[shape((width, tokens), BF)] * 4 + [shape((tokens // R, 2 * width + 128), BF)],
        compiler_params=params(60),
        cost_estimate=cost(10),
        name="project",
    )(info, x, gain, shift, wq, wk, wv, bq, bv, valid)


def near_body(*refs, scale, size):
    (info, q, k, v, valid) = refs[:5]
    (e_out, numer_out, peak_out) = refs[-3:]
    tokens = q.shape[1]
    first = iota((32, tokens), 0) == 0
    good = (valid[...] > 0) & (iota((1, tokens), 1) < info[0])
    mask = jnp.where(first, jnp.where(good, 0.0, NEG), 0.0).astype(BF)
    one = first.astype(BF)
    for i in range(PER_STEP):
        lane = slice(i * size, (i + 1) * size)
        scaled = q[lane, :].astype(F32) * scale
        plain = k[lane, :].astype(F32)
        high = scaled.astype(BF)
        low = (scaled - high.astype(F32)).astype(BF)
        queries = jnp.concatenate([high, low, one], axis=0)
        keys = jnp.concatenate([k[lane, :], k[lane, :], mask], axis=0).T
        values = jnp.concatenate([v[lane, :], one[:16]], axis=0)
        bound = jnp.max(jnp.sum(scaled * scaled, axis=0)) * jnp.max(
            jnp.sum(plain * plain, axis=0)
        )
        safe = bound < SAFE * SAFE

        @pl.when(safe)
        def _():
            weights = jnp.exp2(dot(keys, queries)).astype(BF)
            e_out[i] = weights
            numer_out[i] = dot(values, weights)
            peak_out[i] = jnp.zeros((1, tokens), F32)

        @pl.when(jnp.logical_not(safe))
        def _():
            scores = dot(keys, queries)
            peak = jnp.max(scores, axis=0, keepdims=True)
            weights = jnp.exp2(scores - peak).astype(BF)
            e_out[i] = weights
            numer_out[i] = dot(values, weights)
            peak_out[i] = peak


def near(info, q, k, v, valid, scale, first, count, after):
    width, tokens = q.shape
    size = width // H
    head = pl.BlockSpec((PER_STEP * size, tokens), lambda h: (h + first // PER_STEP, 0))

    def block(rows):
        return pl.BlockSpec((PER_STEP, rows, tokens), lambda h: (h, 0, 0))

    return pl.pallas_call(
        functools.partial(near_body, scale=scale, size=size),
        grid=(count // PER_STEP,),
        in_specs=[scalars()]
        + [head] * 3
        + [pl.BlockSpec((1, tokens), lambda h: (0, 0))]
        + idle(after),
        out_specs=[block(tokens), block(size + 16), block(1)],
        out_shape=[
            shape((count, tokens, tokens), BF),
            shape((count, size + 16, tokens), F32),
            shape((count, 1, tokens), F32),
        ],
        compiler_params=params(60),
        cost_estimate=cost(2 * count),
        name="near",
    )(info, q, k, v, valid, *after)


def merge_body(*refs, scale, pieces, groups, size):
    (q, x, w_out, b_out, gain, shift) = refs[:6]
    parts = refs[6 : 6 + pieces]
    numers = refs[6 + pieces : 6 + pieces + groups]
    peaks = refs[6 + pieces + groups : 6 + pieces + 2 * groups]
    (att_out, near_out, far_out, hidden_out, n_out, nt_out, e_out) = refs[-11:-4]
    keys, values, masks, att = refs[-4:]
    width, rows = q.shape
    heads = [(group, h) for group, ref in enumerate(peaks) for h in range(ref.shape[0])]

    @pl.when(pl.program_id(0) == 0)
    def _():
        first = 0
        for part in parts:
            at = slice(first, first + part.shape[0])
            first = at.stop
            keys[at, :] = part[:, :width]
            values[:, at] = part[:, width : 2 * width].T
            masks[at, :] = part[:, 2 * width :]

    mine = own_head(width, 0, rows, size)
    queries = jnp.where(mine, q[...], jnp.zeros((width, rows), BF))
    residue = (iota((128, rows), 1) % R == iota((128, rows), 0)).astype(BF)
    scores = dot(keys[...], queries) * scale + dot(masks[...], residue)
    far_peak = jnp.max(scores, axis=0, keepdims=True)
    weights = jnp.exp2(scores - far_peak)
    far_denom = jnp.sum(weights, axis=0, keepdims=True)
    weights = weights.astype(BF)
    e_out[...] = weights
    far_numer = dot(values[...], weights)
    place = iota((1, rows), 1) % R
    far_row = jnp.zeros((1, rows), F32)
    for h, (group, at) in enumerate(heads):
        lane = slice(h * size, (h + 1) * size)
        here = place == h
        numer = numers[group]
        near_peak = peaks[group][at]
        top = jnp.maximum(near_peak, jnp.where(here, far_peak, NEG))
        near_fade = jnp.exp2(near_peak - top)
        far_fade = jnp.where(here, jnp.exp2(far_peak - top), 0.0)
        inverse = 1.0 / (near_fade * numer[at, size : size + 1, :] + far_fade * far_denom)
        near_fade = near_fade * inverse
        far_fade = far_fade * inverse
        near_out[h] = near_fade
        far_row = far_row + far_fade
        att[lane, :] = numer[at, :size, :] * near_fade + far_numer[lane, :] * far_fade
    far_out[...] = far_row
    attended = att[...].astype(BF)
    att_out[...] = attended
    hidden = x[...].astype(F32) + dot(attended.T, w_out[...]) + row_of(b_out)
    hidden_out[...] = hidden
    unit, _ = normalized(hidden)
    normed = (unit * row_of(gain) + row_of(shift)).astype(BF)
    n_out[...] = normed
    nt_out[...] = normed.T


def merge(q, numers, peaks, x, w_out, b_out, gain, shift, parts, scale):
    width, tokens = q.shape
    size = width // H
    rows = 512
    far = sum(part.shape[0] for part in parts)
    column = pl.BlockSpec((width, rows), lambda i: (0, i))
    block = pl.BlockSpec((rows, width), lambda i: (i, 0))

    def heads(count, depth):
        return pl.BlockSpec((count, depth, rows), lambda i: (0, 0, i))

    return pl.pallas_call(
        functools.partial(
            merge_body, scale=scale, pieces=len(parts), groups=len(peaks), size=size
        ),
        grid=(tokens // rows,),
        in_specs=[column, block]
        + [whole()] * 4
        + [whole()] * len(parts)
        + [heads(*part.shape[:2]) for part in numers + peaks],
        out_specs=[
            column,
            heads(H, 1),
            pl.BlockSpec((1, rows), lambda i: (0, i)),
            block,
            block,
            column,
            pl.BlockSpec((far, rows), lambda i: (0, i)),
        ],
        out_shape=[
            shape((width, tokens), BF),
            shape((H, 1, tokens), F32),
            shape((1, tokens), F32),
            shape((tokens, width), F32),
            shape((tokens, width), BF),
            shape((width, tokens), BF),
            shape((far, tokens), BF),
        ],
        scratch_shapes=[
            pltpu.VMEM((far, width), BF),
            pltpu.VMEM((width, far), BF),
            pltpu.VMEM((far, 128), BF),
            pltpu.VMEM((width, rows), F32),
        ],
        compiler_params=params(60),
        cost_estimate=cost(13),
        name="merge",
    )(q, x, w_out, b_out, gain, shift, *parts, *numers, *peaks)


def gelu_pair(u):
    size = jnp.abs(u)
    t = pltpu.reciprocal(1.0 + (0.3275911 * 0.7071067811865476) * size, approx=True)
    bell = jnp.exp2(u * u * (-0.5 * LOG2E))
    poly = t * (
        0.5 * 0.254829592
        + t
        * (
            0.5 * -0.284496736
            + t * (0.5 * 1.421413741 + t * (0.5 * -1.453152027 + t * (0.5 * 1.061405429)))
        )
    )
    tail = poly * bell
    phi = jnp.where(u > 0, 1.0 - tail, tail)
    return u * phi, phi + u * bell * 0.3989422804014327


def feed_body(
    info, n, nt, g, w_up, w_down, b_up, act, gt, keep, send, dn_out, bias_out,
    dup, b_up_row, dn, grad, *, blocks,
):
    step = pl.program_id(0)
    tokens = n.shape[0]
    wide = w_up.shape[1]

    @pl.when(step == 0)
    def _():
        b_up_row[...] = row_of(b_up)
        dn[...] = jnp.zeros_like(dn)

    bias = b_up_row[:, pl.ds(pl.multiple_of(step * wide, wide), wide)]
    bias_sum = jnp.zeros((1, wide), F32)
    rows = 256
    for i in range(tokens // rows):
        at = slice(i * rows, (i + 1) * rows)
        upper = dot(n[at, :], w_up[...]) + bias
        value, slope = gelu_pair(upper)
        act[at, :] = value.astype(BF)
        d_upper = (dot_nt(g[at, :], w_down[...]) * slope).astype(BF)
        dup[at, :] = d_upper
        bias_sum = bias_sum + jnp.sum(d_upper.astype(F32), axis=0, keepdims=True)
        dn[at, :] += dot_nt(d_upper, w_up[...])
    bias_out[...] = bias_sum
    part = gt.shape[1]
    gt[...] = g[pl.ds(pl.multiple_of(step * part, part), part), :].T
    grad[...] = dot(nt[...], dup[...])
    share = nt.shape[0] // blocks
    for j in range(blocks // 2):
        for out, leaves in ((keep, 0), (send, 1)):
            start = pl.multiple_of(place_of(info, j, leaves) * share, share)
            out[j] = grad[pl.ds(start, share), :].astype(BF)

    @pl.when(step == pl.num_programs(0) - 1)
    def _():
        dn_out[...] = dn[...].astype(BF)


def feed(info, n, nt, g, w_up, w_down, b_up):
    tokens, width = n.shape
    hidden_units = w_up.shape[1]
    blocks = 8
    steps = 4
    wide = hidden_units // steps
    rows = pl.BlockSpec((blocks // 2, width // blocks, wide), lambda c: (0, 0, c))
    sums = shape((blocks // 2, width // blocks, hidden_units), BF)
    column = pl.BlockSpec((tokens, wide), lambda c: (0, c))
    return pl.pallas_call(
        functools.partial(feed_body, blocks=blocks),
        grid=(steps,),
        in_specs=[
            scalars(),
            whole(),
            whole(),
            whole(),
            pl.BlockSpec((width, wide), lambda c: (0, c)),
            pl.BlockSpec((wide, width), lambda c: (c, 0)),
            whole(),
        ],
        out_specs=[
            column,
            pl.BlockSpec((width, tokens // steps), lambda c: (0, c)),
            rows,
            rows,
            whole(),
            pl.BlockSpec((1, wide), lambda c: (0, c)),
        ],
        out_shape=[
            shape((tokens, hidden_units), BF),
            shape((width, tokens), BF),
            sums,
            sums,
            shape((tokens, width), BF),
            shape((1, hidden_units), F32),
        ],
        scratch_shapes=[
            pltpu.VMEM((tokens, wide), BF),
            pltpu.VMEM((1, hidden_units), F32),
            pltpu.VMEM((tokens, width), F32),
            pltpu.VMEM((width, wide), F32),
        ],
        compiler_params=params(60),
        cost_estimate=cost(34),
        name="feed",
    )(info, n, nt, g, w_up, w_down, b_up)


def down_body(info, gt, act, *refs):
    keep, send = refs[-2:]
    half = act.shape[1] // 2
    for out, leaves in ((keep, 0), (send, 1)):
        start = pl.multiple_of(((info[1] & 1) ^ leaves) * half, half)
        out[0] = dot(gt[...], act[:, pl.ds(start, half)]).astype(BF)


def down_grad(info, gt, act, after):
    width, tokens = gt.shape
    hidden_units = act.shape[1]
    blocks = 8
    steps = 4
    wide = hidden_units // steps

    def pair(leaves):
        def place(c, info):
            chips = c ^ (info[1] >> 1)
            core = ((info[1] & 1) ^ leaves) & info[2]
            return (jnp.where(core == 1, ((chips & 1) << 1) | (chips >> 1), chips), 0, 0)

        return pl.BlockSpec((1, width, wide // 2), place)

    return pl.pallas_call(
        down_body,
        grid_spec=pltpu.PrefetchScalarGridSpec(
            num_scalar_prefetch=1,
            grid=(steps,),
            in_specs=[
                pl.BlockSpec(memory_space=pltpu.VMEM),
                pl.BlockSpec((tokens, wide), lambda c, info: (0, c)),
            ]
            + idle(after),
            out_specs=[pair(0), pair(1)],
        ),
        out_shape=[shape((blocks // 2, width, hidden_units // blocks), BF)] * 2,
        compiler_params=params(60),
        cost_estimate=cost(8),
        name="down_grad",
    )(info, gt, act, *after)


def lower_body(act, w_down, hidden, b_down, *refs):
    refs[-1][...] = (dot(act[...], w_down[...]) + hidden[...] + row_of(b_down)).astype(BF)


def lower(act, w_down, hidden, b_down, after):
    tokens, hidden_units = act.shape
    width = w_down.shape[1]
    rows = 256
    block = pl.BlockSpec((rows, width), lambda i: (i, 0))
    return pl.pallas_call(
        lower_body,
        grid=(tokens // rows,),
        in_specs=[pl.BlockSpec((rows, hidden_units), lambda i: (i, 0)), whole(), block, whole()]
        + idle(after),
        out_specs=block,
        out_shape=shape((tokens, width), BF),
        compiler_params=params(),
        cost_estimate=cost(7),
        name="lower",
    )(act, w_down, hidden, b_down, *after)


def split_body(*refs, size):
    (hidden, dn, g, gain, att, near_fade, far_fade, w_out) = refs[:8]
    (db_out, dnum_out, delta_out, far_num, far_delta_out, vec_out) = refs[-6:]
    width, rows = att.shape

    @pl.when(pl.program_id(0) == 0)
    def _():
        vec_out[...] = jnp.zeros_like(vec_out)

    unit, rstd = normalized(hidden[...])
    d_normed = dn[...].astype(F32)
    upstream = g[...].astype(F32)
    d_hidden = upstream + norm_backward(d_normed * row_of(gain), unit, rstd)
    d_branch = d_hidden.astype(BF)
    db_out[...] = d_branch
    vec_out[0:1, :] += jnp.sum(d_branch.astype(F32), axis=0, keepdims=True)
    vec_out[1:2, :] += jnp.sum(d_normed * unit, axis=0, keepdims=True)
    vec_out[2:3, :] += jnp.sum(d_normed, axis=0, keepdims=True)
    vec_out[3:4, :] += jnp.sum(upstream, axis=0, keepdims=True)
    d_att = dot_nt(w_out[...], d_branch).astype(BF).astype(F32)
    product = d_att * att[...].astype(F32)
    place = iota((1, rows), 1) % R
    far_delta = jnp.zeros((1, rows), F32)
    for h in range(H):
        lane = slice(h * size, (h + 1) * size)
        total = jnp.sum(product[lane, :], axis=0, keepdims=True)
        fade = near_fade[h]
        far = jnp.where(place == h, far_fade[...], 0.0)
        dnum_out[lane, :] = (d_att[lane, :] * fade).astype(BF)
        far_num[lane, :] = (d_att[lane, :] * far).astype(BF)
        delta_out[h] = -total * fade
        far_delta = far_delta + total * far
    far_delta_out[...] = far_delta


def split(hidden, dn, g, gain, att, near_fade, far_fade, w_out, after):
    width, tokens = att.shape
    rows = 512
    column = pl.BlockSpec((width, rows), lambda i: (0, i))
    block = pl.BlockSpec((rows, width), lambda i: (i, 0))
    heads = pl.BlockSpec((H, 1, rows), lambda i: (0, 0, i))
    row = pl.BlockSpec((1, rows), lambda i: (0, i))
    return pl.pallas_call(
        functools.partial(split_body, size=width // H),
        grid=(tokens // rows,),
        in_specs=[block, block, block, whole(), column, heads, row, whole()] + idle(after),
        out_specs=[block, column, heads, column, row, whole()],
        out_shape=[
            shape((tokens, width), BF),
            shape((width, tokens), BF),
            shape((H, 1, tokens), F32),
            shape((width, tokens), BF),
            shape((1, tokens), F32),
            shape((8, width), F32),
        ],
        compiler_params=params(),
        cost_estimate=cost(9),
        name="split",
    )(hidden, dn, g, gain, att, near_fade, far_fade, w_out, *after)


def far_body(*refs, pieces, size, score_scale, blocks):
    (q, numer, delta, e) = refs[:4]
    parts = refs[4 : 4 + pieces]
    (dq_out, keep, send, keys, values, grad) = refs[-6:]
    width, tokens = q.shape
    first = 0
    for part in parts:
        at = slice(first, first + part.shape[0])
        first = at.stop
        keys[:, at] = part[:, :width].T
        values[at, :] = part[:, width : 2 * width]
    share = first // blocks
    mine = own_head(width, 0, tokens, size)
    queries = jnp.where(mine, q[...], jnp.zeros((width, tokens), BF))
    weights = e[...]
    prob = dot(values[...], numer[...]) - delta[...]
    d_scores = (weights.astype(F32) * prob).astype(BF)
    dq_out[...] = jnp.where(mine, dot(keys[...], d_scores), 0.0).astype(BF)
    for lane, left, right, factor in (
        (slice(0, width), d_scores, queries, score_scale),
        (slice(width, 2 * width), weights, numer[...], 1.0),
    ):
        grad[...] = dot_nt(left, right) * factor
        for j in range(blocks):
            out = (keep, send)[j % 2]
            out[j // 2, :, lane] = grad[j * share : (j + 1) * share, :].astype(BF)


def far_kernel(q, numer, delta, e, parts, score_scale, after):
    width, tokens = q.shape
    far = e.shape[0]
    blocks = 8
    grads = shape((blocks // 2, far // blocks, 2 * width), BF)
    return pl.pallas_call(
        functools.partial(
            far_body, pieces=len(parts), size=width // H, score_scale=score_scale, blocks=blocks
        ),
        in_specs=[whole()] * (4 + len(parts)) + idle(after),
        out_specs=[whole()] * 3,
        out_shape=[shape((width, tokens), BF), grads, grads],
        scratch_shapes=[
            pltpu.VMEM((width, far), BF),
            pltpu.VMEM((far, width), BF),
            pltpu.VMEM((far, width), F32),
        ],
        compiler_params=params(),
        cost_estimate=cost(9),
        name="far",
    )(q, numer, delta, e, *parts, *after)


def back_body(*refs, size, score_scale):
    (e, dnum, delta, q, k, v, dq_far) = refs[:7]
    (out, scores) = refs[-2:]
    tokens = q.shape[1]
    at = iota((16, tokens), 0)
    blank = jnp.zeros((64, tokens), BF)
    ones = (at < 3).astype(BF)
    probs = []
    for i in range(PER_STEP):
        lane = slice(i * size, (i + 1) * size)
        low = delta[i]
        terms = []
        for _ in range(3):
            term = low.astype(BF).astype(F32)
            terms.append(term)
            low = low - term
        extra = jnp.where(
            at == 0, terms[0], jnp.where(at == 1, terms[1], jnp.where(at == 2, terms[2], 0.0))
        ).astype(BF)
        numer = jnp.concatenate([dnum[lane, :], extra, blank], axis=0)
        values = jnp.concatenate([v[lane, :], ones, blank], axis=0).T
        scores[i] = (e[i].astype(F32) * dot(values, numer)).astype(BF)
    for i in range(PER_STEP):
        lane = slice(i * size, (i + 1) * size)
        d_scores = scores[i]
        near_part = dot(k[lane, :], d_scores)
        out[0, lane, :] = ((near_part + dq_far[lane, :].astype(F32)) * score_scale).astype(BF)
        out[1, lane, :] = (dot_nt(q[lane, :], d_scores) * score_scale).astype(BF)
        out[2, lane, :] = dot_nt(dnum[lane, :], e[i]).astype(BF)


def back(e, skip, dnum, delta, q, k, v, dq_far, first, count, score_scale, after):
    width, tokens = q.shape
    size = width // H
    wide = PER_STEP * size
    start, skip = first // PER_STEP, skip // PER_STEP
    head = pl.BlockSpec((wide, tokens), lambda h: (h + start, 0))
    return pl.pallas_call(
        functools.partial(back_body, size=size, score_scale=score_scale),
        grid=(count // PER_STEP,),
        in_specs=[
            pl.BlockSpec((PER_STEP, tokens, tokens), lambda h: (h + skip, 0, 0)),
            head,
            pl.BlockSpec((PER_STEP, 1, tokens), lambda h: (h + start, 0, 0)),
            head,
            head,
            head,
            head,
        ]
        + idle(after),
        out_specs=pl.BlockSpec((3, wide, tokens), lambda h: (0, h, 0)),
        out_shape=shape((3, count * size, tokens), BF),
        scratch_shapes=[pltpu.VMEM((PER_STEP, tokens, tokens), BF)],
        compiler_params=params(),
        cost_estimate=cost(2.3 * count),
        name="back",
    )(e, dnum, delta, q, k, v, dq_far, *after)


def weigh_body(*refs, pieces, groups, extra, size, first_row, blocks):
    (info, nt) = refs[:2]
    grads = refs[2 : 2 + groups]
    parts = refs[2 + groups : 2 + groups + pieces]
    others = refs[2 + groups + pieces : 2 + groups + pieces + extra]
    (d_out, keep, send, acc, lines) = refs[-5:]
    rows, tokens = d_out.shape[1:]
    width = nt.shape[0]
    step = pl.program_id(0)

    @pl.when(step == 0)
    def _():
        lines[...] = jnp.zeros_like(lines)
        at = 0
        for part in grads:
            d_out[0, at : at + part.shape[1], :] = part[0]
            at = at + part.shape[1]

    @pl.when((step == 1) | (step == 2))
    def _():
        total = parts[0][...].astype(F32)
        for part in parts[1:]:
            total = total + part[...].astype(F32)
        spread = jnp.where(
            own_head(rows, first_row, tokens, size),
            dot(total.astype(BF).T, group_pick(tokens // R, tokens)),
            0.0,
        )
        at = 0
        for part in grads:
            end = at + part.shape[1]
            d_out[0, at:end, :] = (part[0].astype(F32) + spread[at:end, :]).astype(BF)
            at = end

    @pl.when(step < 3)
    def _():
        value = d_out[0]
        lines[0:8, :] = jnp.where(
            iota((8, rows), 0) == 0, dot_nt(jnp.ones((8, tokens), BF), value), 0.0
        )
        acc[...] = dot_nt(nt[...], value)

    if extra:
        (att, db, vec_mid, bias_up) = others

        @pl.when(step >= 3)
        def _():
            acc[...] = dot(att[...], db[...])

        for half in range(width // rows):

            @pl.when(step == 3 + half)
            def _():
                lines[0:4, :] = vec_mid[0:4, half * rows : (half + 1) * rows]
                for i in range(bias_up.shape[1] // width):
                    start = i * width + half * rows
                    lines[4 + i : 5 + i, :] = bias_up[:, start : start + rows]

    share = width // blocks
    for j in range(blocks // 2):
        for out, leaves in ((keep, 0), (send, 1)):
            start = pl.multiple_of(place_of(info, j, leaves) * share, share)
            out[j, :share, :] = acc[pl.ds(start, share), :].astype(BF)
            out[j, share:, :] = lines[...].astype(BF)


def weigh(info, nt, grads, parts, extra, first_row, after):
    width, tokens = nt.shape
    rows = sum(part.shape[1] for part in grads)
    blocks = 8
    steps = 3 + (width // rows if extra else 0)
    column = first_row // rows
    lanes = width // rows
    kind = lambda i: jnp.minimum(i, 2)
    depth = width // blocks + 16
    sums = shape((blocks // 2, depth, steps * rows), BF)
    sums_spec = pl.BlockSpec((blocks // 2, depth, rows), lambda i: (0, 0, i))
    return pl.pallas_call(
        functools.partial(
            weigh_body,
            pieces=len(parts),
            groups=len(grads),
            extra=len(extra),
            size=width // H,
            first_row=first_row,
            blocks=blocks,
        ),
        grid=(steps,),
        in_specs=[scalars(), whole()]
        + [pl.BlockSpec((1, part.shape[1], tokens), lambda i: (kind(i), 0, 0)) for part in grads]
        + [
            pl.BlockSpec(
                (part.shape[0], rows), lambda i: (0, column + lanes * (kind(i) // 2))
            )
            for part in parts
        ]
        + (
            [whole(), pl.BlockSpec((tokens, rows), lambda i: (0, jnp.maximum(i - 3, 0)))]
            + [whole()] * 2
            if extra
            else []
        )
        + idle(after),
        out_specs=[
            pl.BlockSpec((1, rows, tokens), lambda i: (kind(i), 0, 0)),
            sums_spec,
            sums_spec,
        ],
        out_shape=[shape((3, rows, tokens), BF), sums, sums],
        scratch_shapes=[pltpu.VMEM((width, rows), F32), pltpu.VMEM((16, rows), F32)],
        compiler_params=params(),
        cost_estimate=cost(2.2 * steps),
        name="weigh",
    )(info, nt, *grads, *parts, *extra, *after)


def input_body(*refs, groups):
    (x, gain, dh, wq, wk, wv) = refs[:6]
    grads = refs[6 : 6 + groups]
    dx_out = refs[-1]
    total = None
    for i, weight in enumerate((wq, wk, wv)):
        at = 0
        for grad in grads:
            end = at + grad.shape[1]
            term = dot(weight[:, at:end], grad[i])
            total = term if total is None else total + term
            at = end
    d_normed = total.T
    unit, rstd = normalized(x[...].astype(F32))
    dx_out[...] = (dh[...].astype(F32) + norm_backward(d_normed * row_of(gain), unit, rstd)).astype(BF)


def input_grad(x, gain, dh, wq, wk, wv, grads, begun, after):
    tokens, width = x.shape
    rows = 256
    first = 1 if begun else 0
    steps = tokens // rows - 1 if begun else 1
    block = pl.BlockSpec((rows, width), lambda i: (i + first, 0))
    inputs = [x, gain, dh, wq, wk, wv, *grads, *begun]
    specs = (
        [block, whole(), block]
        + [whole()] * 3
        + [pl.BlockSpec((3, part.shape[1], rows), lambda i: (0, 0, i + first)) for part in grads]
        + idle(begun)
    )
    return pl.pallas_call(
        functools.partial(input_body, groups=len(grads)),
        grid=(steps,),
        in_specs=specs + idle(after),
        out_specs=block,
        out_shape=shape((tokens, width), BF),
        input_output_aliases={len(inputs) - 1: 0} if begun else {},
        compiler_params=params(),
        cost_estimate=cost(3 * steps),
        name="input_grad",
    )(*inputs, *after)


def affine_grads(grads, sums, weights, gain, shift):
    w_grads, d_gain, d_shift = [], 0.0, 0.0
    for grad, line, weight in zip(grads, sums, weights):
        weight = weight.astype(F32)
        w_grads.append(gain * grad + shift * line)
        d_gain = d_gain + jnp.sum(weight * grad, axis=1, keepdims=True)
        d_shift = d_shift + jnp.sum(weight * line, axis=1, keepdims=True)
    return w_grads, d_gain, d_shift


def finish_body(info, f_own, f_got, l_own, l_got, gain, shift, *refs):
    weights, (q_out, k_out, v_out, w_out), vec_outs, lines = refs[:3], refs[3:7], refs[7:-1], refs[-1]
    rows, width = q_out.shape
    half = width // 2
    first = f_own[...].astype(F32) + f_got[...].astype(F32)
    last = l_own[...].astype(F32) + l_got[...].astype(F32)
    grads = [
        jnp.concatenate([part[:, i * half : (i + 1) * half] for part in (first, last)], axis=1)
        for i in range(3)
    ]
    sums = [grad[rows : rows + 1, :] for grad in grads]
    grads = [grad[:rows, :] for grad in grads]
    w_out[...] = first[:rows, 3 * half :]
    here = iota((rows, width), 1) == iota((rows, width), 0) + info[1] * rows
    columns = [
        jnp.sum(jnp.where(here, row_of(line), 0.0), axis=1, keepdims=True) for line in (gain, shift)
    ]
    w_grads, d_gain, d_shift = affine_grads(grads, sums, [w[...] for w in weights], *columns)
    for out, grad in zip((q_out, k_out, v_out), w_grads):
        out[...] = grad
    (b_query, b_value, b_out, d_gain_out, d_shift_out, gain_mlp, shift_mlp, b_down, b_up) = vec_outs
    eye = iota((rows, rows), 0) == iota((rows, rows), 1)
    for out, column in ((d_gain_out, d_gain), (d_shift_out, d_shift)):
        out[...] = jnp.sum(jnp.where(eye, column, 0.0), axis=0, keepdims=True).reshape(rows)
    lines[0:8, :] = first[rows : rows + 8, 3 * half :]
    lines[8:9, :] = sums[0]
    lines[9:10, :] = sums[2]
    turn = (width - info[1] * rows) % width
    turned = pltpu.roll(lines[...], turn, 1)
    for out, i in (
        (b_out, 0), (gain_mlp, 1), (shift_mlp, 2), (b_down, 3), (b_query, 8), (b_value, 9)
    ):
        out[...] = turned[i : i + 1, :rows].reshape(rows)
    wide = b_up.shape[0]
    line = lines[pl.ds(4 + info[1] * wide // width, 1), :]
    line = jnp.where(info[1] * wide % width == 0, line[:, :wide], line[:, width - wide :])
    b_up[...] = line.reshape(wide)


def finish(info, first, last, gain, shift, weights, hidden_units):
    width = weights[0].shape[0]
    rows = first[0].shape[0] - 16
    full = pl.BlockSpec(memory_space=pltpu.VMEM)
    mine = pl.BlockSpec((rows, width), lambda i, info: (info[1], 0))
    return pl.pallas_call(
        finish_body,
        grid_spec=pltpu.PrefetchScalarGridSpec(
            num_scalar_prefetch=1,
            grid=(1,),
            in_specs=[full] * 6 + [mine] * 3,
            out_specs=[full] * 13,
            scratch_shapes=[pltpu.VMEM((16, width), F32)],
        ),
        out_shape=[shape((rows, width), F32)] * 4
        + [shape((rows,), F32)] * 8
        + [shape((hidden_units * rows // width,), F32)],
        compiler_params=params(),
        cost_estimate=cost(3),
        name="finish",
    )(info, *first, *last, gain, shift, *weights)


def finish_feed_body(u_own, u_got, d_own, d_got, up, down):
    up[...] = u_own[...].astype(F32) + u_got[...].astype(F32)
    down[...] = (d_own[...].astype(F32) + d_got[...].astype(F32)).T


def finish_feed(up, down):
    return pl.pallas_call(
        finish_feed_body,
        in_specs=[whole()] * 4,
        out_specs=[whole()] * 2,
        out_shape=[shape(up[0].shape, F32), shape(down[0].shape[::-1], F32)],
        compiler_params=params(),
        cost_estimate=cost(3),
        name="finish_feed",
    )(*up, *down)


def swap(value, axis, mask):
    count = lax.axis_size(axis)
    return lax.ppermute(value, axis, [(i, i ^ mask) for i in range(count)])


def swap_seq(value, turn):
    masks = (2, 4) if turn == 0 else (4, 2)
    return lax.ppermute(value, "seq", [(i, i ^ masks[i & 1]) for i in range(8)])


def swap_rep(value, turn):
    pairs = []
    for i in range(8):
        for z in range(4):
            mask = (1, 2)[(i + turn) & 1]
            pairs.append((i * 4 + z, i * 4 + (z ^ mask)))
    return lax.ppermute(value, ("seq", "rep"), pairs)


def total_of(terms):
    result = terms[0].astype(F32)
    for term in terms[1:]:
        result = result + term.astype(F32)
    return result


class Sum:
    def __init__(self, keep, send, straight=False):
        self.terms, self.send = [keep], send
        self.straight = straight
        self.stage = 0
        self.flying = []

    def start(self, gate):
        stage, self.stage = self.stage, self.stage + 1
        if stage > 5:
            return []
        if stage:
            got, self.flying = [gate(array) for array in self.flying], []
        if stage == 0:
            send = self.send
            self.flying = [swap(send, "seq", 1)]
        elif stage == 1:
            self.terms.append(got[0])
            if self.straight:
                send = total_of([term[1:] for term in self.terms]).astype(BF)
                self.flying = [
                    swap_seq(send[0], 0), swap_seq(send[1], 1), swap(send[2], "seq", 6)
                ]
                self.terms = [term[0] for term in self.terms]
                self.stage = 3
            else:
                send = total_of([term[1::2] for term in self.terms]).astype(BF)
                self.flying = [swap_seq(send, 0)]
        elif stage == 2:
            send = total_of([term[2] for term in self.terms] + [got[0][1]]).astype(BF)
            self.terms = [term[0] for term in self.terms + got]
            self.flying = [swap_seq(send, 1)]
        elif stage < 5:
            send = total_of(self.terms + got).astype(BF)
            self.terms = [send]
            self.flying = [swap_rep(send, stage - 3)]
        else:
            self.terms = self.terms + got
            return []
        return [send]


def plain_sum(value):
    share = lax.psum_scatter(value, "seq", scatter_dimension=0, tiled=True)
    return lax.psum(share, "rep").astype(F32)


def in_order(keep, send):
    both = jnp.stack([keep, send], axis=1)
    return both.reshape(-1, *both.shape[2:])


def far_back(values, keys, numer, delta, queries, weights, mine, score_scale):
    prob = dot(values, numer) - delta
    d_scores = (weights.astype(F32) * prob).astype(BF)
    dq = jnp.where(mine, dot(keys.T, d_scores), 0.0).astype(BF)
    queries = jnp.where(mine, queries, jnp.zeros_like(queries))
    dk = dot_nt(d_scores, queries) * score_scale
    return dq, jnp.concatenate([dk.astype(BF), dot_nt(weights, numer).astype(BF)], axis=1)


def per_device(
    tokens,
    lengths,
    tile_valid,
    w_query,
    w_key,
    w_value,
    w_out,
    b_query,
    b_value,
    b_out,
    gain_attn,
    shift_attn,
    gain_mlp,
    shift_mlp,
    w_up,
    b_up,
    w_down,
    b_down,
    cotangent,
):
    rows, width = tokens.shape[1:]
    size = width // H
    score_scale = size ** (-0.5)
    scale = score_scale * LOG2E
    devices = lax.axis_size("seq")
    direct = devices == 8 and lax.axis_size("rep") == 4
    me = lax.axis_index("seq")
    seat = (me, jnp.ones_like(me)) if direct else (jnp.zeros_like(me),) * 2
    info = jnp.stack([lengths[0] - me * rows, *seat]).astype(jnp.int32)
    x = tokens[0]
    g = cotangent[0]

    def after(kernel, array):
        return lax.optimization_barrier((array, kernel))[0]

    q, k, v, nt, far = project(
        info, x, gain_attn, shift_attn, w_query, w_key, w_value, b_query, b_value, tile_valid, size
    )
    groups = (4, 12)
    if direct:
        twin = swap(far, "seq", 1)
        early = near(info, q, k, v, tile_valid, scale, 0, groups[0], [])
        pair = jnp.concatenate([far, after(early[2], twin)], axis=0)
        parts = [pair] + [swap(pair, "seq", mask) for mask in (2, 4, 6)]
        late = near(info, q, k, v, tile_valid, scale, groups[0], groups[1], [pair])
    else:
        parts = [lax.all_gather(far, "seq", axis=0, tiled=True)]
        early = near(info, q, k, v, tile_valid, scale, 0, groups[0], [])
        late = near(info, q, k, v, tile_valid, scale, groups[0], groups[1], [])
    numers, peaks = [early[1], late[1]], [early[2], late[2]]
    att, near_fade, far_fade, hidden, n_two, nt_two, e_far = merge(
        q, numers, peaks, x, w_out, b_out, gain_mlp, shift_mlp, parts, scale
    )
    act, gt, up_keep, up_send, dn_two, bias_up = feed(
        info, n_two, nt_two, g, w_up, w_down, b_up
    )
    weights = (w_query, w_key, w_value)
    heads = H // 2

    def attend(first, sent):
        late_part = first >= groups[0]
        skip = first - groups[0] if late_part else first
        return back(
            (late if late_part else early)[0], skip, dnum, delta, q, k, v, dq_far, first, heads // 2,
            score_scale, sent,
        )

    def weigh_half(grads, extra, first, sent):
        return weigh(info, nt, grads, owned, extra, first * size, sent)

    if not direct:
        share = width // 8
        down_keep, down_send = down_grad(info, gt, act, [])
        grad_up = plain_sum(in_order(up_keep, up_send).reshape(width, -1))
        grad_down = plain_sum(in_order(down_keep, down_send).swapaxes(1, 2).reshape(-1, width))
        db, dnum, delta, far_num, far_delta, vec_mid = split(
            hidden, dn_two, g, gain_mlp, att, near_fade, far_fade, w_out, []
        )
        dq_far, far_grad = far_back(
            parts[0][:, width : 2 * width], parts[0][:, :width], far_num, far_delta, q, e_far,
            own_head(width, 0, rows, size), score_scale,
        )
        owned = [lax.psum_scatter(far_grad, "seq", scatter_dimension=0, tiled=True)]
        pieces = [attend(first, []) for first in range(0, H, heads // 2)]
        grads, sums, lines = [], [], []
        for i, extra in enumerate(([att, db, vec_mid, bias_up], [])):
            grad, keep, send = weigh_half(pieces[2 * i : 2 * i + 2], extra, i * heads, [])
            grads.append(grad)
            both = in_order(keep, send)
            sums.append(plain_sum(both[:, :share].reshape(width, -1)))
            lines.append(lax.psum(both[0, share:].astype(F32), ("seq", "rep")))
        begun = input_grad(x, gain_attn, db, *weights, grads, [], [])
        dx = input_grad(x, gain_attn, db, *weights, grads, [begun], [])
        mixed = lower(act, w_down, hidden, b_down, [])
        wide = heads * size
        own = width // devices
        mine = lambda v, count=own: lax.dynamic_slice_in_dim(v, me * count, count, 0)
        triple = lambda pair: [
            jnp.concatenate([part[:, i * wide : (i + 1) * wide] for part in pair], axis=1)
            for i in range(3)
        ]
        totals = [line[0] for line in triple(lines)]
        qkv, d_gain, d_shift = affine_grads(
            triple(sums),
            totals,
            [mine(w) for w in weights],
            mine(gain_attn)[:, None],
            mine(shift_attn)[:, None],
        )
        grad_out, lines = sums[0][:, 3 * wide :], lines[0][:, 3 * wide :]
        vectors = [
            mine(totals[0]), mine(totals[2]), mine(lines[0]), d_gain[:, 0], d_shift[:, 0],
            mine(lines[1]), mine(lines[2]), mine(lines[3]),
            mine(lines[4:8].reshape(-1), own * w_up.shape[1] // width),
        ]
    else:

        def round_of(kernel, *sums, landing=()):
            flying = flights(*sums, *landing)
            landed = lax.optimization_barrier((kernel, *flying))[1:] if flying else []
            where = {id(old): new for old, new in zip(flying, landed)}
            for item in landing:
                item.flying = [where[id(array)] for array in item.flying]
            return [array for item in sums for array in item.start(lambda a: where[id(a)])]

        def flights(*sums):
            return [array for item in sums for array in item.flying]

        up = Sum(up_keep, up_send)
        down_keep, down_send = down_grad(info, gt, act, round_of(None, up))
        down = Sum(down_keep, down_send)
        sent = round_of(down_keep, down, up)
        db, dnum, delta, far_num, far_delta, vec_mid = split(
            hidden, dn_two, g, gain_mlp, att, near_fade, far_fade, w_out, sent
        )
        dq_far, far_keep, far_send = far_kernel(
            q, far_num, far_delta, e_far, parts, score_scale, round_of(far_delta, down)
        )
        far_got = swap(far_send, "seq", 1)
        pieces = [attend(0, [far_send] + round_of(dq_far, up))]
        sent = round_of(pieces[-1], up, down)
        far_sum = total_of([far_keep, after(pieces[-1], far_got)]).astype(BF)
        owned = [far_sum[0]] + [swap(far_sum[j], "seq", 2 * j) for j in range(1, 4)]
        pieces.append(attend(4, [far_sum] + sent))
        sent = round_of(pieces[-1], down)
        grad_a, keep, send = weigh_half(pieces, [att, db, vec_mid, bias_up], 0, sent)
        first_grads = Sum(keep, send)
        sent = round_of(grad_a, first_grads, up, landing=[down])
        pieces = [attend(8, sent + flights(down))]
        pieces.append(attend(12, round_of(pieces[-1], first_grads, down)))
        sent = round_of(pieces[-1], first_grads, landing=[up])
        grad_b, keep, send = weigh_half(pieces, [], heads, sent + flights(up))
        last_grads = Sum(keep, send, True)
        sent = round_of(grad_b, last_grads, first_grads, landing=[down])
        begun = input_grad(
            x, gain_attn, db, *weights, [grad_a, grad_b], [], sent + flights(down)
        )
        sent = round_of(begun, last_grads)
        dx = input_grad(x, gain_attn, db, *weights, [grad_a, grad_b], [begun], sent)
        sent = round_of(dx, last_grads, first_grads)
        mixed = lower(after(dx, act), w_down, hidden, b_down, sent)
        round_of(mixed, last_grads, first_grads, up, down)
        round_of(mixed, last_grads)
        grad_up, grad_down = finish_feed(up.terms, down.terms)
        *qkv, grad_out, b_q, b_v, b_o, d_gain, d_shift, g_m, s_m, b_d, b_u = finish(
            info, first_grads.terms, last_grads.terms, gain_attn, shift_attn, weights,
            w_up.shape[1],
        )
        vectors = [b_q, b_v, b_o, d_gain, d_shift, g_m, s_m, b_d, b_u]
    *vectors, bias_up, bias_down = vectors[:7] + [vectors[8], vectors[7]]
    return (mixed[None], dx[None], *qkv, grad_out, *vectors, grad_up, bias_up, grad_down, bias_down)


def solution(mesh):
    split_specs = P("rep", "seq", None)
    in_specs = (split_specs, P("rep"), P("rep", "seq")) + (P(),) * 15 + (split_specs,)
    out_specs = (
        (split_specs,) * 2
        + (P("seq", None),) * 4
        + (P("seq"),) * 7
        + (P("seq", None), P("seq"), P("seq", None), P("seq"))
    )
    return jax.shard_map(
        per_device, mesh=mesh, in_specs=in_specs, out_specs=out_specs, check_vma=False
    )
```

```python
import functools

import jax
import jax.numpy as jnp
from jax import lax
from jax.experimental import pallas as pl
from jax.experimental.pallas import tpu as pltpu
from jax.sharding import PartitionSpec as P

H = 16
R = 16
EPS = 1e-05
LOG2E = 1.4426950408889634
NEG = -1e30
BF = jnp.bfloat16
F32 = jnp.float32
PER_STEP = 1
SAFE = 60.0


def row_of(vector):
    return vector[...].reshape(1, -1)


def iota(shape, dim):
    return lax.broadcasted_iota(jnp.int32, shape, dim)


def dot(left, right):
    return jnp.dot(left, right, preferred_element_type=F32)


def dot_nt(left, right):
    return lax.dot_general(left, right, (((1,), (1,)), ((), ())), preferred_element_type=F32)


def params(mega=48):
    return pltpu.CompilerParams(vmem_limit_bytes=mega * 1024 * 1024)


def cost(micros):
    return pl.CostEstimate(flops=int(micros * 1.15e9), bytes_accessed=1024, transcendentals=0)


def whole():
    return pl.BlockSpec(memory_space=pltpu.VMEM)


def idle(arrays):
    return [pl.BlockSpec(memory_space=pl.ANY)] * len(arrays)


def scalars():
    return pl.BlockSpec(memory_space=pltpu.SMEM)


def shape(dims, kind):
    return jax.ShapeDtypeStruct(dims, kind)


def normalized(values):
    center = values - jnp.mean(values, axis=-1, keepdims=True)
    rstd = lax.rsqrt(jnp.mean(center * center, axis=-1, keepdims=True) + EPS)
    return center * rstd, rstd


def norm_backward(grad, unit, rstd):
    return rstd * (
        grad
        - jnp.mean(grad, axis=-1, keepdims=True)
        - unit * jnp.mean(grad * unit, axis=-1, keepdims=True)
    )


def own_head(rows, first_row, columns, size):
    feature = iota((rows, columns), 0) + first_row
    start = (iota((rows, columns), 1) % R) * size
    return (feature >= start) & (feature < start + size)


def group_pick(groups, columns):
    return (iota((groups, columns), 1) // R == iota((groups, columns), 0)).astype(BF)


def place_of(info, j, leaves):
    core = ((info[1] & 1) ^ leaves) & info[2]
    straight, turned = j << 1, ((j & 1) << 2) | (j & 2)
    return info[1] ^ leaves ^ jnp.where(core == 1, turned, straight)


def project_body(
    info, x, gain, shift, wq, wk, wv, bq, bv, valid, q_out, k_out, v_out, n_out, far_out, *, size
):
    rows, width = x.shape
    unit, _ = normalized(x[...].astype(F32))
    normed = (unit * row_of(gain) + row_of(shift)).astype(BF)
    n_out[...] = unit.astype(BF).T
    q_out[...] = (dot(normed, wq[...]) + row_of(bq)).astype(BF).T
    keys = dot(normed, wk[...]).astype(BF)
    values = (dot(normed, wv[...]) + row_of(bv)).astype(BF)
    k_out[...] = keys.T
    v_out[...] = values.T
    feature = iota((rows, width), 1)
    start = (iota((rows, width), 0) % R) * size
    mine = (feature >= start) & (feature < start + size)
    pick = group_pick(rows // R, rows)
    zero = jnp.zeros((rows, width), BF)
    far_out[:, :width] = dot(pick, jnp.where(mine, keys, zero)).astype(BF)
    far_out[:, width : 2 * width] = dot(pick, jnp.where(mine, values, zero)).astype(BF)
    place = iota((1, rows), 1) + pl.program_id(0) * rows
    good = jnp.where((valid[...] > 0) & (place < info[0]), 1.0, 0.0)
    residue = (iota((rows, 128), 0) % R == iota((rows, 128), 1)).astype(BF)
    found = dot((pick.astype(F32) * good).astype(BF), residue)
    far_out[:, 2 * width :] = jnp.where(found > 0.5, 0.0, NEG).astype(BF)


def project(info, x, gain, shift, wq, wk, wv, bq, bv, valid, size):
    tokens, width = x.shape
    rows = 512
    column = pl.BlockSpec((width, rows), lambda i: (0, i))
    return pl.pallas_call(
        functools.partial(project_body, size=size),
        grid=(tokens // rows,),
        in_specs=[scalars(), pl.BlockSpec((rows, width), lambda i: (i, 0))]
        + [whole()] * 7
        + [pl.BlockSpec((1, rows), lambda i: (0, i))],
        out_specs=[column] * 4 + [pl.BlockSpec((rows // R, 2 * width + 128), lambda i: (i, 0))],
        out_shape=[shape((width, tokens), BF)] * 4 + [shape((tokens // R, 2 * width + 128), BF)],
        compiler_params=params(60),
        cost_estimate=cost(10),
        name="project",
    )(info, x, gain, shift, wq, wk, wv, bq, bv, valid)


def near_body(*refs, scale, size):
    (info, q, k, v, valid) = refs[:5]
    (e_out, numer_out, peak_out) = refs[-3:]
    tokens = q.shape[1]
    first = iota((32, tokens), 0) == 0
    good = (valid[...] > 0) & (iota((1, tokens), 1) < info[0])
    mask = jnp.where(first, jnp.where(good, 0.0, NEG), 0.0).astype(BF)
    one = first.astype(BF)
    for i in range(PER_STEP):
        lane = slice(i * size, (i + 1) * size)
        scaled = q[lane, :].astype(F32) * scale
        plain = k[lane, :].astype(F32)
        high = scaled.astype(BF)
        low = (scaled - high.astype(F32)).astype(BF)
        queries = jnp.concatenate([high, low, one], axis=0)
        keys = jnp.concatenate([k[lane, :], k[lane, :], mask], axis=0).T
        values = jnp.concatenate([v[lane, :], one[:16]], axis=0)
        bound = jnp.max(jnp.sum(scaled * scaled, axis=0)) * jnp.max(
            jnp.sum(plain * plain, axis=0)
        )
        safe = bound < SAFE * SAFE

        @pl.when(safe)
        def _():
            weights = jnp.exp2(dot(keys, queries)).astype(BF)
            e_out[i] = weights
            numer_out[i] = dot(values, weights)
            peak_out[i] = jnp.zeros((1, tokens), F32)

        @pl.when(jnp.logical_not(safe))
        def _():
            scores = dot(keys, queries)
            peak = jnp.max(scores, axis=0, keepdims=True)
            weights = jnp.exp2(scores - peak).astype(BF)
            e_out[i] = weights
            numer_out[i] = dot(values, weights)
            peak_out[i] = peak


def near(info, q, k, v, valid, scale, first, count, after):
    width, tokens = q.shape
    size = width // H
    head = pl.BlockSpec((PER_STEP * size, tokens), lambda h: (h + first // PER_STEP, 0))

    def block(rows):
        return pl.BlockSpec((PER_STEP, rows, tokens), lambda h: (h, 0, 0))

    return pl.pallas_call(
        functools.partial(near_body, scale=scale, size=size),
        grid=(count // PER_STEP,),
        in_specs=[scalars()]
        + [head] * 3
        + [pl.BlockSpec((1, tokens), lambda h: (0, 0))]
        + idle(after),
        out_specs=[block(tokens), block(size + 16), block(1)],
        out_shape=[
            shape((count, tokens, tokens), BF),
            shape((count, size + 16, tokens), F32),
            shape((count, 1, tokens), F32),
        ],
        compiler_params=params(60),
        cost_estimate=cost(2 * count),
        name="near",
    )(info, q, k, v, valid, *after)


def merge_body(*refs, scale, pieces, groups, size):
    (q, x, w_out, b_out, gain, shift) = refs[:6]
    parts = refs[6 : 6 + pieces]
    numers = refs[6 + pieces : 6 + pieces + groups]
    peaks = refs[6 + pieces + groups : 6 + pieces + 2 * groups]
    (att_out, near_out, far_out, hidden_out, n_out, nt_out, e_out) = refs[-11:-4]
    keys, values, masks, att = refs[-4:]
    width, rows = q.shape
    heads = [(group, h) for group, ref in enumerate(peaks) for h in range(ref.shape[0])]

    @pl.when(pl.program_id(0) == 0)
    def _():
        first = 0
        for part in parts:
            at = slice(first, first + part.shape[0])
            first = at.stop
            keys[at, :] = part[:, :width]
            values[:, at] = part[:, width : 2 * width].T
            masks[at, :] = part[:, 2 * width :]

    mine = own_head(width, 0, rows, size)
    queries = jnp.where(mine, q[...], jnp.zeros((width, rows), BF))
    residue = (iota((128, rows), 1) % R == iota((128, rows), 0)).astype(BF)
    scores = dot(keys[...], queries) * scale + dot(masks[...], residue)
    far_peak = jnp.max(scores, axis=0, keepdims=True)
    weights = jnp.exp2(scores - far_peak)
    far_denom = jnp.sum(weights, axis=0, keepdims=True)
    weights = weights.astype(BF)
    e_out[...] = weights
    far_numer = dot(values[...], weights)
    place = iota((1, rows), 1) % R
    far_row = jnp.zeros((1, rows), F32)
    for h, (group, at) in enumerate(heads):
        lane = slice(h * size, (h + 1) * size)
        here = place == h
        numer = numers[group]
        near_peak = peaks[group][at]
        top = jnp.maximum(near_peak, jnp.where(here, far_peak, NEG))
        near_fade = jnp.exp2(near_peak - top)
        far_fade = jnp.where(here, jnp.exp2(far_peak - top), 0.0)
        inverse = 1.0 / (near_fade * numer[at, size : size + 1, :] + far_fade * far_denom)
        near_fade = near_fade * inverse
        far_fade = far_fade * inverse
        near_out[h] = near_fade
        far_row = far_row + far_fade
        att[lane, :] = numer[at, :size, :] * near_fade + far_numer[lane, :] * far_fade
    far_out[...] = far_row
    attended = att[...].astype(BF)
    att_out[...] = attended
    hidden = x[...].astype(F32) + dot(attended.T, w_out[...]) + row_of(b_out)
    hidden_out[...] = hidden
    unit, _ = normalized(hidden)
    normed = (unit * row_of(gain) + row_of(shift)).astype(BF)
    n_out[...] = normed
    nt_out[...] = normed.T


def merge(q, numers, peaks, x, w_out, b_out, gain, shift, parts, scale):
    width, tokens = q.shape
    size = width // H
    rows = 512
    far = sum(part.shape[0] for part in parts)
    column = pl.BlockSpec((width, rows), lambda i: (0, i))
    block = pl.BlockSpec((rows, width), lambda i: (i, 0))

    def heads(count, depth):
        return pl.BlockSpec((count, depth, rows), lambda i: (0, 0, i))

    return pl.pallas_call(
        functools.partial(
            merge_body, scale=scale, pieces=len(parts), groups=len(peaks), size=size
        ),
        grid=(tokens // rows,),
        in_specs=[column, block]
        + [whole()] * 4
        + [whole()] * len(parts)
        + [heads(*part.shape[:2]) for part in numers + peaks],
        out_specs=[
            column,
            heads(H, 1),
            pl.BlockSpec((1, rows), lambda i: (0, i)),
            block,
            block,
            column,
            pl.BlockSpec((far, rows), lambda i: (0, i)),
        ],
        out_shape=[
            shape((width, tokens), BF),
            shape((H, 1, tokens), F32),
            shape((1, tokens), F32),
            shape((tokens, width), F32),
            shape((tokens, width), BF),
            shape((width, tokens), BF),
            shape((far, tokens), BF),
        ],
        scratch_shapes=[
            pltpu.VMEM((far, width), BF),
            pltpu.VMEM((width, far), BF),
            pltpu.VMEM((far, 128), BF),
            pltpu.VMEM((width, rows), F32),
        ],
        compiler_params=params(60),
        cost_estimate=cost(13),
        name="merge",
    )(q, x, w_out, b_out, gain, shift, *parts, *numers, *peaks)


def gelu_pair(u):
    size = jnp.abs(u)
    t = pltpu.reciprocal(1.0 + (0.3275911 * 0.7071067811865476) * size, approx=True)
    bell = jnp.exp2(u * u * (-0.5 * LOG2E))
    poly = t * (
        0.5 * 0.254829592
        + t
        * (
            0.5 * -0.284496736
            + t * (0.5 * 1.421413741 + t * (0.5 * -1.453152027 + t * (0.5 * 1.061405429)))
        )
    )
    tail = poly * bell
    phi = jnp.where(u > 0, 1.0 - tail, tail)
    return u * phi, phi + u * bell * 0.3989422804014327


def feed_body(
    info, n, nt, g, w_up, w_down, b_up, act, gt, keep, send, dn_out, bias_out,
    dup, b_up_row, dn, grad, *, blocks,
):
    step = pl.program_id(0)
    tokens = n.shape[0]
    wide = w_up.shape[1]

    @pl.when(step == 0)
    def _():
        b_up_row[...] = row_of(b_up)
        dn[...] = jnp.zeros_like(dn)

    bias = b_up_row[:, pl.ds(pl.multiple_of(step * wide, wide), wide)]
    bias_sum = jnp.zeros((1, wide), F32)
    rows = 256
    for i in range(tokens // rows):
        at = slice(i * rows, (i + 1) * rows)
        upper = dot(n[at, :], w_up[...]) + bias
        value, slope = gelu_pair(upper)
        act[at, :] = value.astype(BF)
        d_upper = (dot_nt(g[at, :], w_down[...]) * slope).astype(BF)
        dup[at, :] = d_upper
        bias_sum = bias_sum + jnp.sum(d_upper.astype(F32), axis=0, keepdims=True)
        dn[at, :] += dot_nt(d_upper, w_up[...])
    bias_out[...] = bias_sum
    part = gt.shape[1]
    gt[...] = g[pl.ds(pl.multiple_of(step * part, part), part), :].T
    grad[...] = dot(nt[...], dup[...])
    share = nt.shape[0] // blocks
    for j in range(blocks // 2):
        for out, leaves in ((keep, 0), (send, 1)):
            start = pl.multiple_of(place_of(info, j, leaves) * share, share)
            out[j] = grad[pl.ds(start, share), :].astype(BF)

    @pl.when(step == pl.num_programs(0) - 1)
    def _():
        dn_out[...] = dn[...].astype(BF)


def feed(info, n, nt, g, w_up, w_down, b_up):
    tokens, width = n.shape
    hidden_units = w_up.shape[1]
    blocks = 8
    steps = 4
    wide = hidden_units // steps
    rows = pl.BlockSpec((blocks // 2, width // blocks, wide), lambda c: (0, 0, c))
    sums = shape((blocks // 2, width // blocks, hidden_units), BF)
    column = pl.BlockSpec((tokens, wide), lambda c: (0, c))
    return pl.pallas_call(
        functools.partial(feed_body, blocks=blocks),
        grid=(steps,),
        in_specs=[
            scalars(),
            whole(),
            whole(),
            whole(),
            pl.BlockSpec((width, wide), lambda c: (0, c)),
            pl.BlockSpec((wide, width), lambda c: (c, 0)),
            whole(),
        ],
        out_specs=[
            column,
            pl.BlockSpec((width, tokens // steps), lambda c: (0, c)),
            rows,
            rows,
            whole(),
            pl.BlockSpec((1, wide), lambda c: (0, c)),
        ],
        out_shape=[
            shape((tokens, hidden_units), BF),
            shape((width, tokens), BF),
            sums,
            sums,
            shape((tokens, width), BF),
            shape((1, hidden_units), F32),
        ],
        scratch_shapes=[
            pltpu.VMEM((tokens, wide), BF),
            pltpu.VMEM((1, hidden_units), F32),
            pltpu.VMEM((tokens, width), F32),
            pltpu.VMEM((width, wide), F32),
        ],
        compiler_params=params(60),
        cost_estimate=cost(34),
        name="feed",
    )(info, n, nt, g, w_up, w_down, b_up)


def down_body(info, gt, act, *refs):
    keep, send, grad = refs[-3:]
    grad[...] = dot(gt[...], act[...])
    half = act.shape[1] // 2
    for out, leaves in ((keep, 0), (send, 1)):
        start = pl.multiple_of(((info[1] & 1) ^ leaves) * half, half)
        out[0] = grad[:, pl.ds(start, half)].astype(BF)


def down_grad(info, gt, act, after):
    width, tokens = gt.shape
    hidden_units = act.shape[1]
    blocks = 8
    steps = 4
    wide = hidden_units // steps

    def pair(leaves):
        def place(c, info):
            chips = c ^ (info[1] >> 1)
            core = ((info[1] & 1) ^ leaves) & info[2]
            return (jnp.where(core == 1, ((chips & 1) << 1) | (chips >> 1), chips), 0, 0)

        return pl.BlockSpec((1, width, wide // 2), place)

    return pl.pallas_call(
        down_body,
        grid_spec=pltpu.PrefetchScalarGridSpec(
            num_scalar_prefetch=1,
            grid=(steps,),
            in_specs=[
                pl.BlockSpec(memory_space=pltpu.VMEM),
                pl.BlockSpec((tokens, wide), lambda c, info: (0, c)),
            ]
            + idle(after),
            out_specs=[pair(0), pair(1)],
            scratch_shapes=[pltpu.VMEM((width, wide), F32)],
        ),
        out_shape=[shape((blocks // 2, width, hidden_units // blocks), BF)] * 2,
        compiler_params=params(60),
        cost_estimate=cost(8),
        name="down_grad",
    )(info, gt, act, *after)


def lower_body(act, w_down, hidden, b_down, *refs):
    refs[-1][...] = (dot(act[...], w_down[...]) + hidden[...] + row_of(b_down)).astype(BF)


def lower(act, w_down, hidden, b_down, after):
    tokens, hidden_units = act.shape
    width = w_down.shape[1]
    rows = 256
    block = pl.BlockSpec((rows, width), lambda i: (i, 0))
    return pl.pallas_call(
        lower_body,
        grid=(tokens // rows,),
        in_specs=[pl.BlockSpec((rows, hidden_units), lambda i: (i, 0)), whole(), block, whole()]
        + idle(after),
        out_specs=block,
        out_shape=shape((tokens, width), BF),
        compiler_params=params(),
        cost_estimate=cost(7),
        name="lower",
    )(act, w_down, hidden, b_down, *after)


def split_body(*refs, size):
    (hidden, dn, g, gain, att, near_fade, far_fade, w_out) = refs[:8]
    (db_out, dnum_out, delta_out, far_num, far_delta_out, vec_out) = refs[-6:]
    width, rows = att.shape

    @pl.when(pl.program_id(0) == 0)
    def _():
        vec_out[...] = jnp.zeros_like(vec_out)

    unit, rstd = normalized(hidden[...])
    d_normed = dn[...].astype(F32)
    upstream = g[...].astype(F32)
    d_hidden = upstream + norm_backward(d_normed * row_of(gain), unit, rstd)
    d_branch = d_hidden.astype(BF)
    db_out[...] = d_branch
    vec_out[0:1, :] += jnp.sum(d_branch.astype(F32), axis=0, keepdims=True)
    vec_out[1:2, :] += jnp.sum(d_normed * unit, axis=0, keepdims=True)
    vec_out[2:3, :] += jnp.sum(d_normed, axis=0, keepdims=True)
    vec_out[3:4, :] += jnp.sum(upstream, axis=0, keepdims=True)
    d_att = dot_nt(w_out[...], d_branch).astype(BF).astype(F32)
    product = d_att * att[...].astype(F32)
    place = iota((1, rows), 1) % R
    far_delta = jnp.zeros((1, rows), F32)
    for h in range(H):
        lane = slice(h * size, (h + 1) * size)
        total = jnp.sum(product[lane, :], axis=0, keepdims=True)
        fade = near_fade[h]
        far = jnp.where(place == h, far_fade[...], 0.0)
        dnum_out[lane, :] = (d_att[lane, :] * fade).astype(BF)
        far_num[lane, :] = (d_att[lane, :] * far).astype(BF)
        delta_out[h] = -total * fade
        far_delta = far_delta + total * far
    far_delta_out[...] = far_delta


def split(hidden, dn, g, gain, att, near_fade, far_fade, w_out, after):
    width, tokens = att.shape
    rows = 512
    column = pl.BlockSpec((width, rows), lambda i: (0, i))
    block = pl.BlockSpec((rows, width), lambda i: (i, 0))
    heads = pl.BlockSpec((H, 1, rows), lambda i: (0, 0, i))
    row = pl.BlockSpec((1, rows), lambda i: (0, i))
    return pl.pallas_call(
        functools.partial(split_body, size=width // H),
        grid=(tokens // rows,),
        in_specs=[block, block, block, whole(), column, heads, row, whole()] + idle(after),
        out_specs=[block, column, heads, column, row, whole()],
        out_shape=[
            shape((tokens, width), BF),
            shape((width, tokens), BF),
            shape((H, 1, tokens), F32),
            shape((width, tokens), BF),
            shape((1, tokens), F32),
            shape((8, width), F32),
        ],
        compiler_params=params(),
        cost_estimate=cost(9),
        name="split",
    )(hidden, dn, g, gain, att, near_fade, far_fade, w_out, *after)


def far_body(*refs, pieces, size, score_scale, blocks):
    (q, numer, delta, e) = refs[:4]
    parts = refs[4 : 4 + pieces]
    (dq_out, keep, send, keys, values, grad) = refs[-6:]
    width, tokens = q.shape
    first = 0
    for part in parts:
        at = slice(first, first + part.shape[0])
        first = at.stop
        keys[:, at] = part[:, :width].T
        values[at, :] = part[:, width : 2 * width]
    share = first // blocks
    mine = own_head(width, 0, tokens, size)
    queries = jnp.where(mine, q[...], jnp.zeros((width, tokens), BF))
    weights = e[...]
    prob = dot(values[...], numer[...]) - delta[...]
    d_scores = (weights.astype(F32) * prob).astype(BF)
    dq_out[...] = jnp.where(mine, dot(keys[...], d_scores), 0.0).astype(BF)
    for lane, left, right, factor in (
        (slice(0, width), d_scores, queries, score_scale),
        (slice(width, 2 * width), weights, numer[...], 1.0),
    ):
        grad[...] = dot_nt(left, right) * factor
        for j in range(blocks):
            out = (keep, send)[j % 2]
            out[j // 2, :, lane] = grad[j * share : (j + 1) * share, :].astype(BF)


def far_kernel(q, numer, delta, e, parts, score_scale, after):
    width, tokens = q.shape
    far = e.shape[0]
    blocks = 8
    grads = shape((blocks // 2, far // blocks, 2 * width), BF)
    return pl.pallas_call(
        functools.partial(
            far_body, pieces=len(parts), size=width // H, score_scale=score_scale, blocks=blocks
        ),
        in_specs=[whole()] * (4 + len(parts)) + idle(after),
        out_specs=[whole()] * 3,
        out_shape=[shape((width, tokens), BF), grads, grads],
        scratch_shapes=[
            pltpu.VMEM((width, far), BF),
            pltpu.VMEM((far, width), BF),
            pltpu.VMEM((far, width), F32),
        ],
        compiler_params=params(),
        cost_estimate=cost(9),
        name="far",
    )(q, numer, delta, e, *parts, *after)


def back_body(*refs, size, score_scale):
    (e, dnum, delta, q, k, v, dq_far) = refs[:7]
    (out, scores) = refs[-2:]
    tokens = q.shape[1]
    at = iota((16, tokens), 0)
    blank = jnp.zeros((64, tokens), BF)
    ones = (at < 3).astype(BF)
    probs = []
    for i in range(PER_STEP):
        lane = slice(i * size, (i + 1) * size)
        low = delta[i]
        terms = []
        for _ in range(3):
            term = low.astype(BF).astype(F32)
            terms.append(term)
            low = low - term
        extra = jnp.where(
            at == 0, terms[0], jnp.where(at == 1, terms[1], jnp.where(at == 2, terms[2], 0.0))
        ).astype(BF)
        numer = jnp.concatenate([dnum[lane, :], extra, blank], axis=0)
        values = jnp.concatenate([v[lane, :], ones, blank], axis=0).T
        scores[i] = (e[i].astype(F32) * dot(values, numer)).astype(BF)
    for i in range(PER_STEP):
        lane = slice(i * size, (i + 1) * size)
        d_scores = scores[i]
        near_part = dot(k[lane, :], d_scores)
        out[0, lane, :] = ((near_part + dq_far[lane, :].astype(F32)) * score_scale).astype(BF)
        out[1, lane, :] = (dot_nt(q[lane, :], d_scores) * score_scale).astype(BF)
        out[2, lane, :] = dot_nt(dnum[lane, :], e[i]).astype(BF)


def back(e, skip, dnum, delta, q, k, v, dq_far, first, count, score_scale, after):
    width, tokens = q.shape
    size = width // H
    wide = PER_STEP * size
    start, skip = first // PER_STEP, skip // PER_STEP
    head = pl.BlockSpec((wide, tokens), lambda h: (h + start, 0))
    return pl.pallas_call(
        functools.partial(back_body, size=size, score_scale=score_scale),
        grid=(count // PER_STEP,),
        in_specs=[
            pl.BlockSpec((PER_STEP, tokens, tokens), lambda h: (h + skip, 0, 0)),
            head,
            pl.BlockSpec((PER_STEP, 1, tokens), lambda h: (h + start, 0, 0)),
            head,
            head,
            head,
            head,
        ]
        + idle(after),
        out_specs=pl.BlockSpec((3, wide, tokens), lambda h: (0, h, 0)),
        out_shape=shape((3, count * size, tokens), BF),
        scratch_shapes=[pltpu.VMEM((PER_STEP, tokens, tokens), BF)],
        compiler_params=params(),
        cost_estimate=cost(2.3 * count),
        name="back",
    )(e, dnum, delta, q, k, v, dq_far, *after)


def weigh_body(*refs, pieces, groups, extra, size, first_row, blocks):
    (info, nt) = refs[:2]
    grads = refs[2 : 2 + groups]
    parts = refs[2 + groups : 2 + groups + pieces]
    others = refs[2 + groups + pieces : 2 + groups + pieces + extra]
    (d_out, keep, send, acc, lines) = refs[-5:]
    rows, tokens = d_out.shape[1:]
    width = nt.shape[0]
    step = pl.program_id(0)

    @pl.when(step == 0)
    def _():
        lines[...] = jnp.zeros_like(lines)
        at = 0
        for part in grads:
            d_out[0, at : at + part.shape[1], :] = part[0]
            at = at + part.shape[1]

    @pl.when((step == 1) | (step == 2))
    def _():
        total = parts[0][...].astype(F32)
        for part in parts[1:]:
            total = total + part[...].astype(F32)
        spread = jnp.where(
            own_head(rows, first_row, tokens, size),
            dot(total.astype(BF).T, group_pick(tokens // R, tokens)),
            0.0,
        )
        at = 0
        for part in grads:
            end = at + part.shape[1]
            d_out[0, at:end, :] = (part[0].astype(F32) + spread[at:end, :]).astype(BF)
            at = end

    @pl.when(step < 3)
    def _():
        value = d_out[0]
        lines[0:8, :] = jnp.where(
            iota((8, rows), 0) == 0, dot_nt(jnp.ones((8, tokens), BF), value), 0.0
        )
        acc[...] = dot_nt(nt[...], value)

    if extra:
        (att, db, vec_mid, bias_up) = others

        @pl.when(step >= 3)
        def _():
            acc[...] = dot(att[...], db[...])

        for half in range(width // rows):

            @pl.when(step == 3 + half)
            def _():
                lines[0:4, :] = vec_mid[0:4, half * rows : (half + 1) * rows]
                for i in range(bias_up.shape[1] // width):
                    start = i * width + half * rows
                    lines[4 + i : 5 + i, :] = bias_up[:, start : start + rows]

    share = width // blocks
    for j in range(blocks // 2):
        for out, leaves in ((keep, 0), (send, 1)):
            start = pl.multiple_of(place_of(info, j, leaves) * share, share)
            out[j, :share, :] = acc[pl.ds(start, share), :].astype(BF)
            out[j, share:, :] = lines[...].astype(BF)


def weigh(info, nt, grads, parts, extra, first_row, after):
    width, tokens = nt.shape
    rows = sum(part.shape[1] for part in grads)
    blocks = 8
    steps = 3 + (width // rows if extra else 0)
    column = first_row // rows
    lanes = width // rows
    kind = lambda i: jnp.minimum(i, 2)
    depth = width // blocks + 16
    sums = shape((blocks // 2, depth, steps * rows), BF)
    sums_spec = pl.BlockSpec((blocks // 2, depth, rows), lambda i: (0, 0, i))
    return pl.pallas_call(
        functools.partial(
            weigh_body,
            pieces=len(parts),
            groups=len(grads),
            extra=len(extra),
            size=width // H,
            first_row=first_row,
            blocks=blocks,
        ),
        grid=(steps,),
        in_specs=[scalars(), whole()]
        + [pl.BlockSpec((1, part.shape[1], tokens), lambda i: (kind(i), 0, 0)) for part in grads]
        + [
            pl.BlockSpec(
                (part.shape[0], rows), lambda i: (0, column + lanes * (kind(i) // 2))
            )
            for part in parts
        ]
        + (
            [whole(), pl.BlockSpec((tokens, rows), lambda i: (0, jnp.maximum(i - 3, 0)))]
            + [whole()] * 2
            if extra
            else []
        )
        + idle(after),
        out_specs=[
            pl.BlockSpec((1, rows, tokens), lambda i: (kind(i), 0, 0)),
            sums_spec,
            sums_spec,
        ],
        out_shape=[shape((3, rows, tokens), BF), sums, sums],
        scratch_shapes=[pltpu.VMEM((width, rows), F32), pltpu.VMEM((16, rows), F32)],
        compiler_params=params(),
        cost_estimate=cost(2.2 * steps),
        name="weigh",
    )(info, nt, *grads, *parts, *extra, *after)


def input_body(*refs, groups):
    (x, gain, dh, wq, wk, wv) = refs[:6]
    grads = refs[6 : 6 + groups]
    dx_out = refs[-1]
    total = None
    for i, weight in enumerate((wq, wk, wv)):
        at = 0
        for grad in grads:
            end = at + grad.shape[1]
            term = dot(weight[:, at:end], grad[i])
            total = term if total is None else total + term
            at = end
    d_normed = total.T
    unit, rstd = normalized(x[...].astype(F32))
    dx_out[...] = (dh[...].astype(F32) + norm_backward(d_normed * row_of(gain), unit, rstd)).astype(BF)


def input_grad(x, gain, dh, wq, wk, wv, grads, begun, after):
    tokens, width = x.shape
    rows = 256
    first = 1 if begun else 0
    steps = tokens // rows - 1 if begun else 1
    block = pl.BlockSpec((rows, width), lambda i: (i + first, 0))
    inputs = [x, gain, dh, wq, wk, wv, *grads, *begun]
    specs = (
        [block, whole(), block]
        + [whole()] * 3
        + [pl.BlockSpec((3, part.shape[1], rows), lambda i: (0, 0, i + first)) for part in grads]
        + idle(begun)
    )
    return pl.pallas_call(
        functools.partial(input_body, groups=len(grads)),
        grid=(steps,),
        in_specs=specs + idle(after),
        out_specs=block,
        out_shape=shape((tokens, width), BF),
        input_output_aliases={len(inputs) - 1: 0} if begun else {},
        compiler_params=params(),
        cost_estimate=cost(3 * steps),
        name="input_grad",
    )(*inputs, *after)


def affine_grads(grads, sums, weights, gain, shift):
    w_grads, d_gain, d_shift = [], 0.0, 0.0
    for grad, line, weight in zip(grads, sums, weights):
        weight = weight.astype(F32)
        w_grads.append(gain * grad + shift * line)
        d_gain = d_gain + jnp.sum(weight * grad, axis=1, keepdims=True)
        d_shift = d_shift + jnp.sum(weight * line, axis=1, keepdims=True)
    return w_grads, d_gain, d_shift


def finish_body(info, f_own, f_got, l_own, l_got, gain, shift, *refs):
    weights, (q_out, k_out, v_out, w_out), vec_outs, lines = refs[:3], refs[3:7], refs[7:-1], refs[-1]
    rows, width = q_out.shape
    half = width // 2
    first = f_own[...].astype(F32) + f_got[...].astype(F32)
    last = l_own[...].astype(F32) + l_got[...].astype(F32)
    grads = [
        jnp.concatenate([part[:, i * half : (i + 1) * half] for part in (first, last)], axis=1)
        for i in range(3)
    ]
    sums = [grad[rows : rows + 1, :] for grad in grads]
    grads = [grad[:rows, :] for grad in grads]
    w_out[...] = first[:rows, 3 * half :]
    here = iota((rows, width), 1) == iota((rows, width), 0) + info[1] * rows
    columns = [
        jnp.sum(jnp.where(here, row_of(line), 0.0), axis=1, keepdims=True) for line in (gain, shift)
    ]
    w_grads, d_gain, d_shift = affine_grads(grads, sums, [w[...] for w in weights], *columns)
    for out, grad in zip((q_out, k_out, v_out), w_grads):
        out[...] = grad
    (b_query, b_value, b_out, d_gain_out, d_shift_out, gain_mlp, shift_mlp, b_down, b_up) = vec_outs
    eye = iota((rows, rows), 0) == iota((rows, rows), 1)
    for out, column in ((d_gain_out, d_gain), (d_shift_out, d_shift)):
        out[...] = jnp.sum(jnp.where(eye, column, 0.0), axis=0, keepdims=True).reshape(rows)
    lines[0:8, :] = first[rows : rows + 8, 3 * half :]
    lines[8:9, :] = sums[0]
    lines[9:10, :] = sums[2]
    turn = (width - info[1] * rows) % width
    turned = pltpu.roll(lines[...], turn, 1)
    for out, i in (
        (b_out, 0), (gain_mlp, 1), (shift_mlp, 2), (b_down, 3), (b_query, 8), (b_value, 9)
    ):
        out[...] = turned[i : i + 1, :rows].reshape(rows)
    wide = b_up.shape[0]
    line = lines[pl.ds(4 + info[1] * wide // width, 1), :]
    line = jnp.where(info[1] * wide % width == 0, line[:, :wide], line[:, width - wide :])
    b_up[...] = line.reshape(wide)


def finish(info, first, last, gain, shift, weights, hidden_units):
    width = weights[0].shape[0]
    rows = first[0].shape[0] - 16
    full = pl.BlockSpec(memory_space=pltpu.VMEM)
    mine = pl.BlockSpec((rows, width), lambda i, info: (info[1], 0))
    return pl.pallas_call(
        finish_body,
        grid_spec=pltpu.PrefetchScalarGridSpec(
            num_scalar_prefetch=1,
            grid=(1,),
            in_specs=[full] * 6 + [mine] * 3,
            out_specs=[full] * 13,
            scratch_shapes=[pltpu.VMEM((16, width), F32)],
        ),
        out_shape=[shape((rows, width), F32)] * 4
        + [shape((rows,), F32)] * 8
        + [shape((hidden_units * rows // width,), F32)],
        compiler_params=params(),
        cost_estimate=cost(3),
        name="finish",
    )(info, *first, *last, gain, shift, *weights)


def finish_feed_body(u_own, u_got, d_own, d_got, up, down):
    up[...] = u_own[...].astype(F32) + u_got[...].astype(F32)
    down[...] = (d_own[...].astype(F32) + d_got[...].astype(F32)).T


def finish_feed(up, down):
    return pl.pallas_call(
        finish_feed_body,
        in_specs=[whole()] * 4,
        out_specs=[whole()] * 2,
        out_shape=[shape(up[0].shape, F32), shape(down[0].shape[::-1], F32)],
        compiler_params=params(),
        cost_estimate=cost(3),
        name="finish_feed",
    )(*up, *down)


def swap(value, axis, mask):
    count = lax.axis_size(axis)
    return lax.ppermute(value, axis, [(i, i ^ mask) for i in range(count)])


def swap_seq(value, turn):
    masks = (2, 4) if turn == 0 else (4, 2)
    return lax.ppermute(value, "seq", [(i, i ^ masks[i & 1]) for i in range(8)])


def swap_rep(value, turn):
    pairs = []
    for i in range(8):
        for z in range(4):
            mask = (1, 2)[(i + turn) & 1]
            pairs.append((i * 4 + z, i * 4 + (z ^ mask)))
    return lax.ppermute(value, ("seq", "rep"), pairs)


def total_of(terms):
    result = terms[0].astype(F32)
    for term in terms[1:]:
        result = result + term.astype(F32)
    return result


class Sum:
    def __init__(self, keep, send, straight=False):
        self.terms, self.send = [keep], send
        self.straight = straight
        self.stage = 0
        self.flying = []

    def start(self, gate):
        stage, self.stage = self.stage, self.stage + 1
        if stage > 5:
            return []
        if stage:
            got, self.flying = [gate(array) for array in self.flying], []
        if stage == 0:
            send = self.send
            self.flying = [swap(send, "seq", 1)]
        elif stage == 1:
            self.terms.append(got[0])
            if self.straight:
                send = total_of([term[1:] for term in self.terms]).astype(BF)
                self.flying = [
                    swap_seq(send[0], 0), swap_seq(send[1], 1), swap(send[2], "seq", 6)
                ]
                self.terms = [term[0] for term in self.terms]
                self.stage = 3
            else:
                send = total_of([term[1::2] for term in self.terms]).astype(BF)
                self.flying = [swap_seq(send, 0)]
        elif stage == 2:
            send = total_of([term[2] for term in self.terms] + [got[0][1]]).astype(BF)
            self.terms = [term[0] for term in self.terms + got]
            self.flying = [swap_seq(send, 1)]
        elif stage < 5:
            send = total_of(self.terms + got).astype(BF)
            self.terms = [send]
            self.flying = [swap_rep(send, stage - 3)]
        else:
            self.terms = self.terms + got
            return []
        return [send]


def plain_sum(value):
    share = lax.psum_scatter(value, "seq", scatter_dimension=0, tiled=True)
    return lax.psum(share, "rep").astype(F32)


def in_order(keep, send):
    both = jnp.stack([keep, send], axis=1)
    return both.reshape(-1, *both.shape[2:])


def far_back(values, keys, numer, delta, queries, weights, mine, score_scale):
    prob = dot(values, numer) - delta
    d_scores = (weights.astype(F32) * prob).astype(BF)
    dq = jnp.where(mine, dot(keys.T, d_scores), 0.0).astype(BF)
    queries = jnp.where(mine, queries, jnp.zeros_like(queries))
    dk = dot_nt(d_scores, queries) * score_scale
    return dq, jnp.concatenate([dk.astype(BF), dot_nt(weights, numer).astype(BF)], axis=1)


def per_device(
    tokens,
    lengths,
    tile_valid,
    w_query,
    w_key,
    w_value,
    w_out,
    b_query,
    b_value,
    b_out,
    gain_attn,
    shift_attn,
    gain_mlp,
    shift_mlp,
    w_up,
    b_up,
    w_down,
    b_down,
    cotangent,
):
    rows, width = tokens.shape[1:]
    size = width // H
    score_scale = size ** (-0.5)
    scale = score_scale * LOG2E
    devices = lax.axis_size("seq")
    direct = devices == 8 and lax.axis_size("rep") == 4
    me = lax.axis_index("seq")
    seat = (me, jnp.ones_like(me)) if direct else (jnp.zeros_like(me),) * 2
    info = jnp.stack([lengths[0] - me * rows, *seat]).astype(jnp.int32)
    x = tokens[0]
    g = cotangent[0]

    def after(kernel, array):
        return lax.optimization_barrier((array, kernel))[0]

    q, k, v, nt, far = project(
        info, x, gain_attn, shift_attn, w_query, w_key, w_value, b_query, b_value, tile_valid, size
    )
    groups = (4, 12)
    if direct:
        twin = swap(far, "seq", 1)
        early = near(info, q, k, v, tile_valid, scale, 0, groups[0], [])
        pair = jnp.concatenate([far, after(early[2], twin)], axis=0)
        parts = [pair] + [swap(pair, "seq", mask) for mask in (2, 4, 6)]
        late = near(info, q, k, v, tile_valid, scale, groups[0], groups[1], [pair])
    else:
        parts = [lax.all_gather(far, "seq", axis=0, tiled=True)]
        early = near(info, q, k, v, tile_valid, scale, 0, groups[0], [])
        late = near(info, q, k, v, tile_valid, scale, groups[0], groups[1], [])
    numers, peaks = [early[1], late[1]], [early[2], late[2]]
    att, near_fade, far_fade, hidden, n_two, nt_two, e_far = merge(
        q, numers, peaks, x, w_out, b_out, gain_mlp, shift_mlp, parts, scale
    )
    act, gt, up_keep, up_send, dn_two, bias_up = feed(
        info, n_two, nt_two, g, w_up, w_down, b_up
    )
    weights = (w_query, w_key, w_value)
    heads = H // 2

    def attend(first, sent):
        late_part = first >= groups[0]
        skip = first - groups[0] if late_part else first
        return back(
            (late if late_part else early)[0], skip, dnum, delta, q, k, v, dq_far, first, heads // 2,
            score_scale, sent,
        )

    def weigh_half(grads, extra, first, sent):
        return weigh(info, nt, grads, owned, extra, first * size, sent)

    if not direct:
        share = width // 8
        down_keep, down_send = down_grad(info, gt, act, [])
        grad_up = plain_sum(in_order(up_keep, up_send).reshape(width, -1))
        grad_down = plain_sum(in_order(down_keep, down_send).swapaxes(1, 2).reshape(-1, width))
        db, dnum, delta, far_num, far_delta, vec_mid = split(
            hidden, dn_two, g, gain_mlp, att, near_fade, far_fade, w_out, []
        )
        dq_far, far_grad = far_back(
            parts[0][:, width : 2 * width], parts[0][:, :width], far_num, far_delta, q, e_far,
            own_head(width, 0, rows, size), score_scale,
        )
        owned = [lax.psum_scatter(far_grad, "seq", scatter_dimension=0, tiled=True)]
        pieces = [attend(first, []) for first in range(0, H, heads // 2)]
        grads, sums, lines = [], [], []
        for i, extra in enumerate(([att, db, vec_mid, bias_up], [])):
            grad, keep, send = weigh_half(pieces[2 * i : 2 * i + 2], extra, i * heads, [])
            grads.append(grad)
            both = in_order(keep, send)
            sums.append(plain_sum(both[:, :share].reshape(width, -1)))
            lines.append(lax.psum(both[0, share:].astype(F32), ("seq", "rep")))
        begun = input_grad(x, gain_attn, db, *weights, grads, [], [])
        dx = input_grad(x, gain_attn, db, *weights, grads, [begun], [])
        mixed = lower(act, w_down, hidden, b_down, [])
        wide = heads * size
        own = width // devices
        mine = lambda v, count=own: lax.dynamic_slice_in_dim(v, me * count, count, 0)
        triple = lambda pair: [
            jnp.concatenate([part[:, i * wide : (i + 1) * wide] for part in pair], axis=1)
            for i in range(3)
        ]
        totals = [line[0] for line in triple(lines)]
        qkv, d_gain, d_shift = affine_grads(
            triple(sums),
            totals,
            [mine(w) for w in weights],
            mine(gain_attn)[:, None],
            mine(shift_attn)[:, None],
        )
        grad_out, lines = sums[0][:, 3 * wide :], lines[0][:, 3 * wide :]
        vectors = [
            mine(totals[0]), mine(totals[2]), mine(lines[0]), d_gain[:, 0], d_shift[:, 0],
            mine(lines[1]), mine(lines[2]), mine(lines[3]),
            mine(lines[4:8].reshape(-1), own * w_up.shape[1] // width),
        ]
    else:

        def round_of(kernel, *sums, landing=()):
            flying = flights(*sums, *landing)
            landed = lax.optimization_barrier((kernel, *flying))[1:] if flying else []
            where = {id(old): new for old, new in zip(flying, landed)}
            for item in landing:
                item.flying = [where[id(array)] for array in item.flying]
            return [array for item in sums for array in item.start(lambda a: where[id(a)])]

        def flights(*sums):
            return [array for item in sums for array in item.flying]

        up = Sum(up_keep, up_send)
        down_keep, down_send = down_grad(info, gt, act, round_of(None, up))
        down = Sum(down_keep, down_send)
        sent = round_of(down_keep, down, up)
        db, dnum, delta, far_num, far_delta, vec_mid = split(
            hidden, dn_two, g, gain_mlp, att, near_fade, far_fade, w_out, sent
        )
        dq_far, far_keep, far_send = far_kernel(
            q, far_num, far_delta, e_far, parts, score_scale, round_of(far_delta, down)
        )
        far_got = swap(far_send, "seq", 1)
        pieces = [attend(0, [far_send] + round_of(dq_far, up))]
        sent = round_of(pieces[-1], up, down)
        far_sum = total_of([far_keep, after(pieces[-1], far_got)]).astype(BF)
        owned = [far_sum[0]] + [swap(far_sum[j], "seq", 2 * j) for j in range(1, 4)]
        pieces.append(attend(4, [far_sum] + sent))
        sent = round_of(pieces[-1], down)
        grad_a, keep, send = weigh_half(pieces, [att, db, vec_mid, bias_up], 0, sent)
        first_grads = Sum(keep, send)
        sent = round_of(grad_a, first_grads, up, landing=[down])
        pieces = [attend(8, sent + flights(down))]
        pieces.append(attend(12, round_of(pieces[-1], first_grads, down)))
        sent = round_of(pieces[-1], first_grads, landing=[up])
        grad_b, keep, send = weigh_half(pieces, [], heads, sent + flights(up))
        last_grads = Sum(keep, send, True)
        sent = round_of(grad_b, last_grads, first_grads, landing=[down])
        begun = input_grad(
            x, gain_attn, db, *weights, [grad_a, grad_b], [], sent + flights(down)
        )
        sent = round_of(begun, last_grads)
        dx = input_grad(x, gain_attn, db, *weights, [grad_a, grad_b], [begun], sent)
        sent = round_of(dx, last_grads, first_grads)
        mixed = lower(after(dx, act), w_down, hidden, b_down, sent)
        round_of(mixed, last_grads, first_grads, up, down)
        round_of(mixed, last_grads)
        grad_up, grad_down = finish_feed(up.terms, down.terms)
        *qkv, grad_out, b_q, b_v, b_o, d_gain, d_shift, g_m, s_m, b_d, b_u = finish(
            info, first_grads.terms, last_grads.terms, gain_attn, shift_attn, weights,
            w_up.shape[1],
        )
        vectors = [b_q, b_v, b_o, d_gain, d_shift, g_m, s_m, b_d, b_u]
    *vectors, bias_up, bias_down = vectors[:7] + [vectors[8], vectors[7]]
    return (mixed[None], dx[None], *qkv, grad_out, *vectors, grad_up, bias_up, grad_down, bias_down)


def solution(mesh):
    split_specs = P("rep", "seq", None)
    in_specs = (split_specs, P("rep"), P("rep", "seq")) + (P(),) * 15 + (split_specs,)
    out_specs = (
        (split_specs,) * 2
        + (P("seq", None),) * 4
        + (P("seq"),) * 7
        + (P("seq", None), P("seq"), P("seq", None), P("seq"))
    )
    return jax.shard_map(
        per_device, mesh=mesh, in_specs=in_specs, out_specs=out_specs, check_vma=False
    )
```
